32 devices in a mesh: rep: 2 (over x), shard: 4 (over y, core), tp: 4 (over z).
Axes of the slice: x: 2, y: 2, z: 4, core: 2. Of those that a mesh axis runs over, the one named last changes fastest.
Arguments:
- tokens: bfloat16 [16, 448, 1024], P(('rep', 'shard'), 'tp'), may hold values from -6 to 6
- encoded: bfloat16 [16, 1500, 1024], P(('rep', 'shard')), may hold values from -6 to 6
- cotangent: bfloat16 [16, 448, 1024], P(('rep', 'shard'), 'tp'), may hold values from -6 to 6
- adapter_of: int32 [16], P(('rep', 'shard')), may hold values from 0 to 7
- w_attn_in: bfloat16 [1, 2, 3, 1024, 1024], P(None, None, None, 'shard', 'tp'), may hold values from -0.1875 to 0.1875
- w_attn_out: bfloat16 [1, 2, 1024, 1024], P(None, None, 'tp', 'shard'), may hold values from -0.75 to 0.75
- w_up: bfloat16 [1, 1024, 4096], P(None, 'shard', 'tp'), may hold values from -0.1875 to 0.1875
- w_down: bfloat16 [1, 4096, 1024], P(None, 'tp', 'shard'), may hold values from -0.09375 to 0.09375
- norm_gain: float32 [1, 3, 1024], replicated, may hold values from 0.1 to 1.9
- norm_shift: float32 [1, 3, 1024], replicated, may hold values from -1.2 to 1.2
- down_attn_in: bfloat16 [1, 2, 3, 128, 1024], P(None, None, None, 'shard'), may hold values from -0.1875 to 0.1875
- up_attn_in: bfloat16 [1, 2, 3, 128, 1024], P(None, None, None, 'shard', 'tp'), may hold values from -0.75 to 0.75
- down_feed_in: bfloat16 [1, 128, 1024], P(None, 'shard'), may hold values from -0.1875 to 0.1875
- up_feed_in: bfloat16 [1, 128, 4096], P(None, 'shard', 'tp'), may hold values from -0.75 to 0.75
- down_attn_out: bfloat16 [1, 2, 128, 1024], P(None, None, 'shard', 'tp'), may hold values from -0.1875 to 0.1875
- up_attn_out: bfloat16 [1, 2, 128, 1024], P(None, None, 'shard'), may hold values from -0.75 to 0.75
- down_feed_out: bfloat16 [1, 128, 4096], P(None, 'shard', 'tp'), may hold values from -0.09375 to 0.09375
- up_feed_out: bfloat16 [1, 128, 1024], P(None, 'shard'), may hold values from -0.75 to 0.75
Outputs:
- activations: bfloat16 [16, 448, 1024], P(('rep', 'shard'), 'tp')
- grad_tokens: float32 [16, 448, 1024], P(('rep', 'shard'), 'tp')
- grad_encoded: float32 [16, 1500, 1024], P(('rep', 'shard'), 'tp')
- grad_down_attn_in: float32 [1, 2, 3, 128, 1024], P(None, None, None, ('shard', 'tp'))
- grad_up_attn_in: float32 [1, 2, 3, 128, 1024], P(None, None, None, 'shard', 'tp')
- grad_down_feed_in: float32 [1, 128, 1024], P(None, ('shard', 'tp'))
- grad_up_feed_in: float32 [1, 128, 4096], P(None, 'shard', 'tp')
- grad_down_attn_out: float32 [1, 2, 128, 1024], P(None, None, 'shard', 'tp')
- grad_up_attn_out: float32 [1, 2, 128, 1024], P(None, None, ('shard', 'tp'))
- grad_down_feed_out: float32 [1, 128, 4096], P(None, 'shard', 'tp')
- grad_up_feed_out: float32 [1, 128, 1024], P(None, ('shard', 'tp'))
The draws below stay inside these ranges and needn't reach their ends.
All inputs are finite; a program needn't handle non-finite values.
Results may differ from the reference program's by a relative error of at most 0.017.
The reference program's roundings to bfloat16 on the way count: a program that leaves them out, or rounds other values in their place, can miss the bound.
Values may be sent and summed in bfloat16 or wider, within the bound.
A program may use at most 192 MiB of HBM per device.

```python
import jax
import jax.numpy as jnp
from jax import lax

D = 1024
HD = 64
FF = 4096
S = 448
F = 1500
ADAPTERS = 8
RANK = 16
LAYERS = 1
CLIPS = 16


def draw_tokens(key, part):
    key = jax.random.fold_in(key, 11)
    values = jax.random.normal(key, (CLIPS, S, D), jnp.float32)
    return jnp.clip(values, -6.0, 6.0).astype(jnp.bfloat16)


def draw_encoded(key, part):
    key = jax.random.fold_in(key, 23)
    values = jax.random.normal(key, (CLIPS, F, D), jnp.float32)
    return jnp.clip(values, -6.0, 6.0).astype(jnp.bfloat16)


def draw_norm_shift(key, part):
    key = jax.random.fold_in(key, 37)
    values = 0.3 * jax.random.normal(key, (LAYERS, 3, D), jnp.float32)
    return jnp.clip(values, -1.2, 1.2)


def plant(values, key, smallest, largest):
    longest = values.shape.index(max(values.shape))
    spots = []
    for shift in (0, 1):
        where = [jax.random.randint(jax.random.fold_in(key, axis), (), 0, length) for axis, length in enumerate(values.shape)]
        where[longest] = (where[longest] + shift) % values.shape[longest]
        spots.append(tuple(where))
    return values.at[spots[0]].set(smallest).at[spots[1]].set(largest)


def steps_of(rng, extent, split, smallest, high):
    level, own = 1.0, jax.random.fold_in(rng, 6)
    for axis_at, shards_of in split:
        draws = jnp.exp(jax.random.uniform(jax.random.fold_in(own, axis_at), (shards_of,), jnp.float32, smallest / len(split), high / len(split)))
        level = level * jnp.repeat(draws, extent[axis_at] // shards_of).reshape([-1 if axis == axis_at else 1 for axis in range(len(extent))])
    return level


def centred(key, shape, width, bound, shards=(), kind=jnp.bfloat16):
    level = steps_of(key, shape, shards, -0.22, 0.18) if shards else 1.0
    values = jax.random.normal(key, shape, jnp.float32) * width * level
    return jnp.minimum(jnp.maximum(values, -bound), bound).astype(kind)


def setup_inputs(seed: int = 0) -> dict:
    key_of = jax.random.split(jax.random.key(seed), 19)
    tokens = draw_tokens(jax.random.fold_in(key_of[18], 71), 0)
    encoded = draw_encoded(jax.random.fold_in(key_of[18], 71), 0)
    cotangent = centred(key_of[2], (CLIPS, S, D), 1.0, 6.0, ((0, 8), (1, 4)))
    adapter_of = plant(jax.random.randint(key_of[3], (CLIPS,), 0, ADAPTERS), jax.random.fold_in(key_of[3], 1), 0, ADAPTERS - 1).astype(jnp.int32)
    w_attn_in = centred(key_of[4], (LAYERS, 2, 3, D, D), D ** -0.5, 0.1875, ((3, 4), (4, 4)))
    w_attn_out = centred(key_of[5], (LAYERS, 2, D, D), (D // 16) ** -0.5, 0.75, ((2, 4), (3, 4)))
    w_up = centred(key_of[6], (LAYERS, D, FF), D ** -0.5, 0.1875, ((1, 4), (2, 4)))
    w_down = centred(key_of[7], (LAYERS, FF, D), FF ** -0.5, 0.09375, ((1, 4), (2, 4)))
    norm_gain = jnp.clip(1.0 + 0.18 * jax.random.normal(key_of[8], (LAYERS, 3, D), jnp.float32), 0.1, 1.9)
    norm_shift = draw_norm_shift(jax.random.fold_in(key_of[18], 71), 0)
    down_attn_in = centred(key_of[10], (LAYERS, 2, 3, ADAPTERS * RANK, D), D ** -0.5, 0.1875, ((3, 4),))
    up_attn_in = centred(key_of[11], (LAYERS, 2, 3, ADAPTERS * RANK, D), (4 * RANK) ** -0.5, 0.75, ((3, 4), (4, 4)))
    down_feed_in = centred(key_of[12], (LAYERS, ADAPTERS * RANK, D), D ** -0.5, 0.1875, ((1, 4),))
    up_feed_in = centred(key_of[13], (LAYERS, ADAPTERS * RANK, FF), (4 * RANK) ** -0.5, 0.75, ((1, 4), (2, 4)))
    down_attn_out = centred(key_of[14], (LAYERS, 2, ADAPTERS * RANK, D), D ** -0.5, 0.1875, ((2, 4), (3, 4)))
    up_attn_out = centred(key_of[15], (LAYERS, 2, ADAPTERS * RANK, D), (4 * RANK) ** -0.5, 0.75, ((2, 4),))
    down_feed_out = centred(key_of[16], (LAYERS, ADAPTERS * RANK, FF), FF ** -0.5, 0.09375, ((1, 4), (2, 4)))
    up_feed_out = centred(key_of[17], (LAYERS, ADAPTERS * RANK, D), (4 * RANK) ** -0.5, 0.75, ((1, 4),))
    return dict(tokens=tokens, encoded=encoded, cotangent=cotangent, adapter_of=adapter_of, w_attn_in=w_attn_in, w_attn_out=w_attn_out, w_up=w_up, w_down=w_down, norm_gain=norm_gain, norm_shift=norm_shift, down_attn_in=down_attn_in, up_attn_in=up_attn_in, down_feed_in=down_feed_in, up_feed_in=up_feed_in, down_attn_out=down_attn_out, up_attn_out=up_attn_out, down_feed_out=down_feed_out, up_feed_out=up_feed_out)


@jax.custom_vjp
def low(v):
    return lax.optimization_barrier(v.astype(jnp.bfloat16)).astype(jnp.float32)

@jax.custom_vjp
def low_back(v):
    return v

def low_keep(v):
    return (low(v), None)

def low_pass(kept, grad):
    return (grad,)

def back_keep(v):
    return (v, None)

def back_low(kept, grad):
    return (low(grad),)
low.defvjp(low_keep, low_pass)
low_back.defvjp(back_keep, back_low)
precise = lax.Precision.HIGHEST
epsilon = 1e-05
masked_score = -1e+30

def layer_norm(inputs, gain_row, shift_row):
    centered = inputs - lax.optimization_barrier(jnp.mean(inputs, axis=-1, keepdims=True))
    variance = lax.optimization_barrier(jnp.mean(centered * centered, axis=-1, keepdims=True))
    return centered * lax.rsqrt(variance + epsilon) * gain_row + shift_row

def project(inputs, weight, down_rows, up_rows, select):
    main_term = jnp.einsum('ctd,dp->ctp', inputs, weight, precision=precise)
    inner_rank = jnp.einsum('ctd,kd->ctk', inputs, down_rows, precision=precise) * select[:, None, :]
    return main_term + jnp.einsum('ctk,kp->ctp', inner_rank, up_rows, precision=precise)

def attend(queries, keys_in, values_in, causal):
    clip_count, length = (queries.shape[0], queries.shape[1])
    frames = keys_in.shape[1]
    head_count = queries.shape[2] // HD
    query_heads = queries.reshape(clip_count, length, head_count, HD)
    key_heads = keys_in.reshape(clip_count, frames, head_count, HD)
    value_heads = values_in.reshape(clip_count, frames, head_count, HD)
    scores = low_back(jnp.einsum('cqhe,ckhe->chqk', query_heads, key_heads, precision=precise) * HD ** (-0.5))
    if causal:
        allowed = jnp.arange(length)[:, None] >= jnp.arange(frames)[None, :]
        scores = jnp.where(allowed, scores, masked_score)
    attention = jax.nn.softmax(scores, axis=-1)
    mixture = jnp.einsum('chqk,ckhe->cqhe', low(attention), value_heads, precision=precise)
    return mixture.reshape(clip_count, length, head_count * HD)

def forward(hidden, encoded, adapters, frozen, select):
    down_attn_in, up_attn_in, down_feed_in, up_feed_in, down_attn_out, up_attn_out, down_feed_out, up_feed_out = adapters
    w_attn_in, w_attn_out, w_up, w_down, norm_gain, norm_shift = frozen
    for layer_index in range(LAYERS):
        for side_index in range(2):
            normed = low(layer_norm(hidden, norm_gain[layer_index, side_index], norm_shift[layer_index, side_index]))
            source = normed if side_index == 0 else encoded
            queries = low(low_back(project(normed, w_attn_in[layer_index, side_index, 0], down_attn_in[layer_index, side_index, 0], up_attn_in[layer_index, side_index, 0], select)))
            keys_out = low(low_back(project(source, w_attn_in[layer_index, side_index, 1], down_attn_in[layer_index, side_index, 1], up_attn_in[layer_index, side_index, 1], select)))
            values_out = low(low_back(project(source, w_attn_in[layer_index, side_index, 2], down_attn_in[layer_index, side_index, 2], up_attn_in[layer_index, side_index, 2], select)))
            mixture = low(low_back(attend(queries, keys_out, values_out, side_index == 0)))
            hidden = hidden + low_back(project(mixture, w_attn_out[layer_index, side_index], down_attn_out[layer_index, side_index], up_attn_out[layer_index, side_index], select))
        normed = low(layer_norm(hidden, norm_gain[layer_index, 2], norm_shift[layer_index, 2]))
        pre_active = low_back(project(normed, w_up[layer_index], down_feed_in[layer_index], up_feed_in[layer_index], select))
        active = low(jax.nn.gelu(pre_active, approximate=False))
        hidden = hidden + low_back(project(active, w_down[layer_index], down_feed_out[layer_index], up_feed_out[layer_index], select))
    return hidden

def reference(tokens, encoded, cotangent, adapter_of, w_attn_in, w_attn_out, w_up, w_down, norm_gain, norm_shift, down_attn_in, up_attn_in, down_feed_in, up_feed_in, down_attn_out, up_attn_out, down_feed_out, up_feed_out):
    adapters = tuple((stored.astype(jnp.float32) for stored in (down_attn_in, up_attn_in, down_feed_in, up_feed_in, down_attn_out, up_attn_out, down_feed_out, up_feed_out)))
    frozen = tuple((stored.astype(jnp.float32) for stored in (w_attn_in, w_attn_out, w_up, w_down, norm_gain, norm_shift)))
    group_size = 4
    rank_ids = jnp.arange(ADAPTERS * RANK, dtype=jnp.int32) // RANK

    def one_group(running, group_index):
        first_clip = (group_index * group_size).astype(jnp.int32)
        hidden = lax.dynamic_slice_in_dim(tokens, first_clip, group_size, 0).astype(jnp.float32)
        states = lax.dynamic_slice_in_dim(encoded, first_clip, group_size, 0).astype(jnp.float32)
        upstream = lax.dynamic_slice_in_dim(cotangent, first_clip, group_size, 0).astype(jnp.float32)
        chosen = lax.dynamic_slice_in_dim(adapter_of, first_clip, group_size, 0)
        select = (rank_ids[None, :] == chosen[:, None]).astype(jnp.float32)
        result, pullback = jax.vjp(lambda inputs, memory, params: forward(inputs, memory, params, frozen, select), hidden, states, adapters)
        grad_hidden, grad_states, grad_params = pullback(upstream)
        running = tuple((before + update for before, update in zip(running, grad_params)))
        return (running, (result.astype(jnp.bfloat16), grad_hidden, grad_states))
    initial = tuple((jnp.zeros_like(stored) for stored in adapters))
    totals, (outputs, grad_tokens, grad_encoded) = lax.scan(one_group, initial, jnp.arange(CLIPS // group_size, dtype=jnp.int32))
    return (outputs.reshape(CLIPS, S, D), grad_tokens.reshape(CLIPS, S, D), grad_encoded.reshape(CLIPS, F, D), totals[0], totals[1], totals[2], totals[3], totals[4], totals[5], totals[6], totals[7])
```

```python
from functools import partial

import jax
import jax.numpy as jnp
from jax import lax
from jax.sharding import Mesh, PartitionSpec as P

HD = 64
RANK = 16
epsilon = 1e-05
masked_score = -1e30
f32, bf16 = jnp.float32, jnp.bfloat16
SWAP = ((0, 1), (1, 0))


def dot(a, b, dims):
    return lax.dot_general(a, b, (dims, ((), ())), preferred_element_type=f32)


def mm(a, b):
    return dot(a, b, ((1,), (0,)))


def mm_t(a, b):
    return dot(a, b, ((1,), (1,)))


def t_mm(a, b):
    return dot(a, b, ((0,), (0,)))


def layer_norm(inputs, gain_row, shift_row):
    centered = inputs - jnp.mean(inputs, axis=-1, keepdims=True)
    variance = jnp.mean(centered * centered, axis=-1, keepdims=True)
    return centered * lax.rsqrt(variance + epsilon) * gain_row + shift_row


def norm_back(hidden, gain_row, shift_row, grad):
    return jax.vjp(lambda rows: layer_norm(rows, gain_row, shift_row), hidden)[1](grad)[0]


def heads_of(rows):
    return rows.reshape(rows.shape[0], rows.shape[1] // HD, HD)


def make_scores(queries, keys, causal):
    scores = jnp.einsum("qhe,khe->hqk", queries, keys, preferred_element_type=f32) * HD**-0.5
    if causal:
        allowed = jnp.arange(queries.shape[0])[:, None] >= jnp.arange(keys.shape[0])[None, :]
        scores = jnp.where(allowed, scores, masked_score)
    return scores


def attend_forward(queries, keys, values, causal):
    scores = make_scores(heads_of(queries), heads_of(keys), causal)
    highest = jnp.max(scores, axis=-1, keepdims=True)
    expanded = jnp.exp(scores - highest)
    totals = jnp.sum(expanded, axis=-1, keepdims=True)
    probs = (expanded / totals).astype(bf16)
    mixture = jnp.einsum("hqk,khe->qhe", probs, heads_of(values), preferred_element_type=f32)
    return mixture.reshape(queries.shape).astype(bf16), highest + jnp.log(totals)


def attend_backward(queries, keys, values, log_total, grad, causal):
    qh, kh, vh, gh = (heads_of(rows) for rows in (queries, keys, values, grad))
    probs = jnp.exp(make_scores(qh, kh, causal) - log_total)
    grad_values = jnp.einsum("hqk,qhe->khe", probs.astype(bf16), gh, preferred_element_type=f32)
    grad_probs = jnp.einsum("qhe,khe->hqk", gh, vh, preferred_element_type=f32)
    grad_scores = probs * (grad_probs - jnp.sum(probs * grad_probs, axis=-1, keepdims=True))
    grad_scores = grad_scores.astype(bf16)
    grad_queries = jnp.einsum("hqk,khe->qhe", grad_scores, kh, preferred_element_type=f32) * HD**-0.5
    grad_keys = jnp.einsum("hqk,qhe->khe", grad_scores, qh, preferred_element_type=f32) * HD**-0.5
    return (
        grad_queries.reshape(queries.shape).astype(bf16),
        grad_keys.reshape(keys.shape).astype(bf16),
        grad_values.reshape(values.shape).astype(bf16),
    )


def swap_core(rows):
    return lax.ppermute(rows, "core", SWAP)


def core_sum(part):
    return part + swap_core(part)


def own_and_other(stacked):
    core = lax.axis_index("core")
    keep = lax.dynamic_index_in_dim(stacked, core, 0, keepdims=False)
    send = lax.dynamic_index_in_dim(stacked, 1 - core, 0, keepdims=False)
    return keep, swap_core(send)


def in_core_order(own, other):
    first = lax.axis_index("core") == 0
    return jnp.stack([jnp.where(first, own, other), jnp.where(first, other, own)])


def scatter_sh(stacked):
    n = lax.axis_size("sh")
    if n == 2:
        me = lax.axis_index("sh")
        keep = lax.dynamic_index_in_dim(stacked, me, 0, keepdims=False)
        send = lax.dynamic_index_in_dim(stacked, 1 - me, 0, keepdims=False)
        return keep + lax.ppermute(send, "sh", SWAP)
    return lax.psum_scatter(stacked, "sh", scatter_dimension=0, tiled=False)


def over_z(stacked):
    return lax.all_to_all(stacked, "tp", 0, 0, tiled=True)


def half_columns(rows):
    width = rows.shape[-1] // 2
    return lax.dynamic_slice_in_dim(rows, lax.axis_index("core") * width, width, rows.ndim - 1)


def rows_home(half):
    tp = lax.axis_size("tp")
    moved = over_z(half.reshape(tp, half.shape[0] // tp, half.shape[1]))
    own, other = own_and_other(moved.reshape(2, tp // 2, *moved.shape[1:]))
    both = in_core_order(own, other)
    return jnp.moveaxis(both, 0, 2).reshape(both.shape[1], both.shape[2], 2 * half.shape[1])


def rows_here(rows):
    tp = lax.axis_size("tp")
    both = in_core_order(rows, swap_core(rows)).reshape(4, *rows.shape[1:])
    moved = over_z(half_columns(both))
    moved = moved.reshape(tp * rows.shape[1], rows.shape[2] // 2)
    pair = in_core_order(moved, swap_core(moved))
    return jnp.concatenate([pair[0], pair[1]], axis=-1)


def gather_weights(w_attn_in, w_attn_out, w_up, w_down):
    def over_shard(block, axis):
        return lax.all_gather(block, ("sh", "core"), axis=axis, tiled=True)

    def over_tp(block, axis):
        return lax.all_gather(block, "tp", axis=axis, tiled=True)

    core = lax.axis_index("core")

    def half(block, axis):
        width = block.shape[axis] // 2
        return lax.dynamic_slice_in_dim(block, core * width, width, axis)

    w_in = over_tp(half(over_shard(w_attn_in.reshape(6, *w_attn_in.shape[3:]), 1), 2), 2)
    w_out = over_tp(half(over_shard(w_attn_out[0], 2), 1), 1)
    w_first = over_tp(half(over_shard(w_up[0], 0), 1), 1)
    w_second = over_tp(half(over_shard(w_down[0], 1), 0), 0)
    return w_in, w_out, w_first, w_second


def on_device(
    tokens,
    encoded,
    cotangent,
    adapter_of,
    w_attn_in,
    w_attn_out,
    w_up,
    w_down,
    norm_gain,
    norm_shift,
    down_attn_in,
    up_attn_in,
    down_feed_in,
    up_feed_in,
    down_attn_out,
    up_attn_out,
    down_feed_out,
    up_feed_out,
):
    n, tp = lax.axis_size("sh"), lax.axis_size("tp")
    sh, core, z = lax.axis_index("sh"), lax.axis_index("core"), lax.axis_index("tp")
    width = w_attn_in.shape[3] * 2 * n
    held_rows = down_feed_in.shape[1]
    quarter = width // tp
    piece = quarter // 2

    ids = lax.all_gather(adapter_of, ("sh", "core"), tiled=True)

    row_ids = (sh * 2 + core) * held_rows + jnp.arange(held_rows)
    wanted = ids.reshape(n, tp)[:, :, None] * RANK + jnp.arange(RANK)
    picks = (wanted[..., None] == row_ids).astype(bf16)
    whole = jnp.concatenate(
        [
            down_attn_in.reshape(6, held_rows, width),
            down_feed_in,
            up_attn_out[0],
            up_feed_out,
        ]
    )
    def in_quarters(rows):
        return jnp.moveaxis(rows.reshape(held_rows, tp, quarter), 1, 0)

    split = jnp.concatenate(
        [
            up_attn_in.reshape(6, held_rows, quarter),
            in_quarters(up_feed_in[0]),
            down_attn_out[0],
            in_quarters(down_feed_out[0]),
        ]
    )
    picks_z = lax.dynamic_index_in_dim(picks, z, 1, keepdims=False)
    chosen_whole = jnp.einsum("srk,mkd->smrd", picks_z, whole, preferred_element_type=f32).astype(bf16)
    chosen_split = jnp.einsum("szrk,mkd->szmrd", picks, split, preferred_element_type=f32).astype(bf16)
    chosen_whole = core_sum(scatter_sh(chosen_whole))
    chosen_split = over_z(core_sum(scatter_sh(chosen_split)))

    def columns(first, count):
        mine = half_columns(chosen_split[:, first : first + count])
        return jnp.moveaxis(mine, 0, 2).reshape(count, RANK, tp * piece)

    def wide_columns(first):
        mine = lax.dynamic_slice_in_dim(chosen_split[:, first : first + tp], core * 2, 2, 1)
        return jnp.moveaxis(mine, 2, 0).reshape(RANK, tp * 2 * quarter)

    a_in, a_up, b_out, b_down = chosen_whole[:6], chosen_whole[6], chosen_whole[7:9], chosen_whole[9]
    b_in, b_up, a_out, a_down = columns(0, 6), wide_columns(6), columns(6 + tp, 2), wide_columns(8 + tp)

    w_in, w_out, w_first, w_second = gather_weights(w_attn_in, w_attn_out, w_up, w_down)

    def merge(weight, down_rows, up_rows):
        return (weight.astype(f32) + t_mm(down_rows, up_rows)).astype(bf16)

    w_in = [merge(w_in[i], a_in[i], b_in[i]) for i in range(6)]
    w_out = [merge(w_out[i], a_out[i], b_out[i]) for i in range(2)]
    w_first = merge(w_first, a_up, b_up)
    w_second = merge(w_second, a_down, b_down)

    hidden = rows_here(tokens).astype(f32)
    upstream = rows_here(cotangent)
    mine = lax.dynamic_index_in_dim(encoded, z % 2, 0, keepdims=False)
    memory = jnp.where(core == z // 2, mine, swap_core(mine))

    kept = []
    for side in range(2):
        normed = layer_norm(hidden, norm_gain[0, side], norm_shift[0, side]).astype(bf16)
        source = normed if side == 0 else memory
        queries = mm(normed, w_in[3 * side]).astype(bf16)
        keys = mm(source, w_in[3 * side + 1]).astype(bf16)
        values = mm(source, w_in[3 * side + 2]).astype(bf16)
        mixture, log_total = attend_forward(queries, keys, values, side == 0)
        kept.append((hidden, normed, source, queries, keys, values, mixture, log_total))
        hidden = hidden + core_sum(mm(mixture, w_out[side]))
    normed = layer_norm(hidden, norm_gain[0, 2], norm_shift[0, 2]).astype(bf16)
    pre_active = mm(normed, w_first)
    active = jax.nn.gelu(pre_active, approximate=False).astype(bf16)
    result = (hidden + core_sum(mm(active, w_second))).astype(bf16)
    activations = rows_home(half_columns(result))

    grad_hidden = upstream.astype(f32)
    grad_active = mm_t(upstream, w_second)
    _, gelu_back = jax.vjp(partial(jax.nn.gelu, approximate=False), pre_active)
    grad_pre = gelu_back(grad_active)[0].astype(bf16)
    grad_hidden = grad_hidden + norm_back(
        hidden, norm_gain[0, 2], norm_shift[0, 2], core_sum(mm_t(grad_pre, w_first))
    )

    def rank_grads(inputs, grad, down_rows, up_rows):
        inner = mm_t(inputs, down_rows).astype(bf16)
        back = mm_t(grad, up_rows).astype(bf16)
        return t_mm(back, inputs), t_mm(inner, grad)

    split_grads, whole_grads = [None] * 4, [None] * 4
    whole_grads[1], split_grads[1] = rank_grads(normed, grad_pre, a_up, b_up)
    split_grads[3], whole_grads[3] = rank_grads(active, upstream, a_down, b_down)
    in_whole, in_split, out_whole, out_split = [None] * 6, [None] * 6, [None] * 2, [None] * 2
    for side in (1, 0):
        hidden, normed, source, queries, keys, values, mixture, log_total = kept[side]
        upstream = grad_hidden.astype(bf16)
        grad_mixture = mm_t(upstream, w_out[side]).astype(bf16)
        out_split[side], out_whole[side] = rank_grads(mixture, upstream, a_out[side], b_out[side])
        grads = attend_backward(queries, keys, values, log_total, grad_mixture, side == 0)
        terms = [mm_t(grads[i], w_in[3 * side + i]) for i in range(3)]
        for i in range(3):
            inputs = normed if i == 0 else source
            in_whole[3 * side + i], in_split[3 * side + i] = rank_grads(
                inputs, grads[i], a_in[3 * side + i], b_in[3 * side + i]
            )
        if side == 1:
            part = (terms[1] + terms[2]).astype(bf16)
            own, other = own_and_other(jnp.moveaxis(part.reshape(part.shape[0], 2, -1), 1, 0))
            grad_encoded = rows_home((own.astype(f32) + other.astype(f32)).astype(bf16)).astype(f32)
            term = terms[0]
        else:
            term = terms[0] + terms[1] + terms[2]
        grad_hidden = grad_hidden + norm_back(
            hidden, norm_gain[0, side], norm_shift[0, side], core_sum(term)
        )
    grad_tokens = rows_home(half_columns(grad_hidden).astype(bf16)).astype(f32)

    def in_pieces(rows):
        return jnp.moveaxis(rows.reshape(RANK, tp, piece), 1, 0)[:, None]

    def in_wide_pieces(rows):
        return jnp.moveaxis(rows.reshape(RANK, tp, tp, piece), 0, 2)

    partial_whole = jnp.stack(in_whole + [whole_grads[1]] + out_whole + [whole_grads[3]]).astype(bf16)
    partial_whole = jnp.moveaxis(partial_whole.reshape(-1, RANK, tp, 2, piece), (3, 2), (0, 1))
    own, other = own_and_other(jnp.moveaxis(partial_whole, 2, 2))
    compact = jnp.concatenate(
        [in_pieces(rows) for rows in in_split]
        + [in_wide_pieces(split_grads[1])]
        + [in_pieces(rows) for rows in out_split]
        + [in_wide_pieces(split_grads[3])],
        axis=1,
    ).astype(bf16)
    compact = jnp.concatenate([compact, own + other], axis=1)
    compact = over_z(compact)
    here = ids.reshape(n, tp)[sh]
    rows = jnp.arange(2 * n * held_rows)
    place = (here[:, None] * RANK + jnp.arange(RANK))[None] == rows[:, None, None]
    dense = jnp.einsum("gkr,kmrp->gmp", place.astype(bf16), compact, preferred_element_type=f32)
    dense = dense.astype(bf16).reshape(n, 2, held_rows, *dense.shape[1:])
    dense = scatter_sh(dense)
    dense = dense + lax.ppermute(dense, "rep", SWAP)
    both = in_core_order(*own_and_other(dense))
    done = jnp.moveaxis(both, 0, 2)
    count = 8 + 2 * tp
    sums = done[:, :count].astype(f32)

    def narrow(first, number):
        block = sums[:, first : first + number].reshape(held_rows, number, quarter)
        return jnp.moveaxis(block, 1, 0)

    def wide(first):
        block = sums[:, first : first + tp].reshape(held_rows, 2, tp // 2, 2, piece)
        return block

    def wide_of(first):
        block = jnp.moveaxis(sums[:, first : first + tp], 2, 1)
        return block.reshape(held_rows, 2 * tp * piece)

    grad_up_attn_in = narrow(0, 6).reshape(1, 2, 3, held_rows, quarter)
    grad_up_feed_in = wide_of(6)[None]
    grad_down_attn_out = narrow(6 + tp, 2)[None]
    grad_down_feed_out = wide_of(8 + tp)[None]
    rest = done[:, count:].reshape(tp, held_rows // tp, 10, quarter)
    rest = jnp.moveaxis(over_z(rest), 0, 2)
    rest = jnp.moveaxis(rest.reshape(held_rows // tp, 10, width), 1, 0).astype(f32)
    return (
        activations,
        grad_tokens,
        grad_encoded,
        rest[:6].reshape(1, 2, 3, held_rows // tp, width),
        grad_up_attn_in,
        rest[6:7],
        grad_up_feed_in,
        grad_down_attn_out,
        rest[7:9][None],
        grad_down_feed_out,
        rest[9:10],
    )


def solution(mesh):
    rep, shard, tp = (mesh.shape[name] for name in ("rep", "shard", "tp"))
    fine = Mesh(mesh.devices.reshape(rep, shard // 2, 2, tp), ("rep", "sh", "core", "tp"))
    shard = ("sh", "core")
    clips = ("rep", "sh", "core")
    both = ("sh", "core", "tp")
    placed = (
        P(clips, "tp", None),
        P(clips, None, None),
        P(clips, "tp", None),
        P(clips),
        P(None, None, None, shard, "tp"),
        P(None, None, "tp", shard),
        P(None, shard, "tp"),
        P(None, "tp", shard),
        P(),
        P(),
        P(None, None, None, shard, None),
        P(None, None, None, shard, "tp"),
        P(None, shard, None),
        P(None, shard, "tp"),
        P(None, None, shard, "tp"),
        P(None, None, shard, None),
        P(None, shard, "tp"),
        P(None, shard, None),
    )
    return jax.shard_map(
        on_device,
        mesh=fine,
        in_specs=placed,
        out_specs=(
            P(clips, "tp", None),
            P(clips, "tp", None),
            P(clips, "tp", None),
            P(None, None, None, both, None),
            P(None, None, None, shard, "tp"),
            P(None, both, None),
            P(None, shard, "tp"),
            P(None, None, shard, "tp"),
            P(None, None, both, None),
            P(None, shard, "tp"),
            P(None, both, None),
        ),
        check_vma=False,
    )
```

```python
import functools
from functools import partial

import jax
import jax.numpy as jnp
from jax import lax
from jax.experimental import pallas as pl
from jax.experimental.pallas import tpu as pltpu
from jax.sharding import Mesh, PartitionSpec as P

HD = 64
RANK = 16
epsilon = 1e-05
masked_score = -1e30
f32, bf16 = jnp.float32, jnp.bfloat16
SWAP = ((0, 1), (1, 0))
MESH = pl.DeviceIdType.MESH


class Unit:
    def __init__(self, kind, index):
        self.kind, self.index = kind, index
        self.rows = 512 if kind in ("in", "up") else 128
        self.most = self.rows * 3 // 4
        self.via_y = 304 if self.rows == 512 else 80


UNITS = (
    [Unit("in", i) for i in (0, 1, 2)]
    + [Unit("out", 0)]
    + [Unit("in", i) for i in (3, 4, 5)]
    + [Unit("out", 1)]
    + [Unit(kind, j) for j in range(4) for kind in ("up", "down")]
)


def gather_kernel(tok, enc, cot, w_in, w_out, w_up, w_down, g_tok, g_enc, g_cot, g_in, g_out, g_up, g_down, sems, semr, loc):
    x, y, c, z = (lax.axis_index(a) for a in ("rep", "sh", "core", "tp"))
    count = [0]
    waits = []

    def when(cond, fn):
        if cond is None:
            fn()
        else:
            pl.when(cond)(fn)

    def block(u, yy, zz, first, size):
        def al(v, m):
            return pl.multiple_of(v, m)
        if u.kind == "in":
            return g_in.at[u.index, pl.ds(al(yy * 512 + first, 16), size), pl.ds(al(zz * 128, 128), 128)]
        if u.kind == "up":
            return g_up.at[pl.ds(al(yy * 512 + first, 16), size), pl.ds(al(zz * 512 + u.index * 128, 128), 128)]
        if u.kind == "out":
            return g_out.at[u.index, pl.ds(al(zz * 128 + first, 16), size), pl.ds(al(yy * 512, 512), 512)]
        return g_down.at[pl.ds(al(zz * 512 + u.index * 128 + first, 16), size), pl.ds(al(yy * 512, 512), 512)]

    def half_src(u, cc):
        if u.kind == "in":
            return w_in.at[u.index, :, pl.ds(pl.multiple_of(cc * 128, 128), 128)]
        if u.kind == "up":
            return w_up.at[:, pl.ds(pl.multiple_of(cc * 512 + u.index * 128, 128), 128)]
        if u.kind == "out":
            return w_out.at[u.index, pl.ds(pl.multiple_of(cc * 128, 128), 128), :]
        return w_down.at[pl.ds(pl.multiple_of(cc * 512 + u.index * 128, 128), 128), :]

    def half_dst(u, cc):
        if u.kind == "in":
            return block(u, y, z, cc * 256, 256)
        if u.kind == "up":
            return block(u, y, z, cc * 256, 256)
        al = pl.multiple_of
        if u.kind == "out":
            return g_out.at[u.index, pl.ds(al(z * 128, 128), 128), pl.ds(al(y * 512 + cc * 256, 256), 256)]
        return g_down.at[pl.ds(al(z * 512 + u.index * 128, 128), 128), pl.ds(al(y * 512 + cc * 256, 256), 256)]

    def remote(src, dst, s, r, dev):
        return pltpu.make_async_remote_copy(src_ref=src, dst_ref=dst, send_sem=s, recv_sem=r, device_id=dev, device_id_type=MESH)

    def send(cond, src, dst, s, r, dev):
        when(cond, lambda: remote(src, dst, s, r, dev).start())
        waits.append((cond, lambda: remote(src, dst, s, r, dev).wait_send()))

    def got(dst, s, r, dev):
        remote(dst, dst, s, r, dev).wait_recv()

    bar = pltpu.get_barrier_semaphore()
    peers = [{"rep": 1 - x}, {"sh": 1 - y}, {"core": 1 - c}] + [{"tp": lax.rem(z + k, 4)} for k in (1, 2, 3)]
    for dev in peers:
        pl.semaphore_signal(bar, inc=1, device_id=dev, device_id_type=MESH)
    pl.semaphore_wait(bar, 6)
    X, Y, C = peers[:3]
    UP, DOWN = {"tp": z + 1}, {"tp": z - 1}
    NU = len(UNITS)
    def S(kind, u, j):
        return sems.at[kind, u, j]
    def R(kind, u, j):
        return semr.at[kind, u, j]
    def core_exchange(i):
        u = UNITS[i]
        send(None, half_src(u, 1 - c), half_dst(u, c), S(0, i, 0), R(0, i, 0), C)
        pltpu.make_async_copy(half_src(u, c), half_dst(u, c), loc.at[i]).start()

    def own(i):
        u = UNITS[i]
        got(half_dst(u, 1 - c), S(0, i, 0), R(0, i, 0), C)
        pltpu.make_async_copy(half_src(u, c), half_dst(u, c), loc.at[i]).wait()
        zb = block(u, y, z, x * (u.rows - u.most), u.most)
        send(z < 3, zb, zb, S(1, i, z), R(1, i, z), UP)
        send(z > 0, zb, zb, S(2, i, z), R(1, i, z), DOWN)
        yb = block(u, y, z, x * (u.rows - u.via_y), u.via_y)
        send(None, yb, yb, S(3, i, z), R(3, i, z), Y)

    def hop(i, k):
        u = UNITS[i]
        for ok, j, more, dev, kind in (((z >= k), z - k, (z >= k) & (z < 3), UP, 1), ((z + k <= 3), z + k, (z + k <= 3) & (z > 0), DOWN, 2)):
            zb = block(u, y, j, x * (u.rows - u.most), u.most)
            when(ok, functools.partial(got, zb, S(1, i, j), R(1, i, j), X))
            send(more, zb, zb, S(kind, i, j), R(1, i, j), dev)
            yb = block(u, y, j, x * (u.rows - u.via_y), u.via_y)
            send(ok, yb, yb, S(3, i, j), R(3, i, j), Y)
            xb = block(u, y, j, x * u.most, u.rows - u.most)
            send(ok, xb, xb, S(4, i, j), R(4, i, j), X)

    def cross(i, k):
        u = UNITS[i]
        for ok, j in ((z >= k, z - k), (z + k <= 3, z + k)) if k else ((None, z),):
            yb = block(u, 1 - y, j, x * (u.rows - u.via_y), u.via_y)
            when(ok, functools.partial(got, yb, S(3, i, j), R(3, i, j), X))
            xb = block(u, 1 - y, j, x * u.via_y, u.rows - u.via_y)
            send(ok, xb, xb, S(5, i, j), R(5, i, j), X)

    def last(i, k):
        u = UNITS[i]
        for ok, j in ((z >= k, z - k), (z + k <= 3, z + k)) if k else ((None, z),):
            if k:
                xb = block(u, y, j, (1 - x) * u.most, u.rows - u.most)
                when(ok, functools.partial(got, xb, S(4, i, j), R(4, i, j), X))
            xb = block(u, 1 - y, j, (1 - x) * u.via_y, u.rows - u.via_y)
            when(ok, functools.partial(got, xb, S(5, i, j), R(5, i, j), X))

    NM = 0
    def rows_out(src, dst, slot):
        for i in (0, 1):
            zd = 2 * c + i
            d = dst.at[pl.ds(pl.multiple_of(z * 112, 16), 112)]
            send(zd != z, src.at[i], d, S(0, slot * 2 + i, 1), R(0, slot * 4 + z, 2), {"tp": zd})
            def local(i=i, d=d):
                cp = pltpu.make_async_copy(src.at[i], d, loc.at[NU + slot])
                cp.start()
                cp.wait()
            when(zd == z, local)

    def rows_in(dst, slot):
        mine = c == z // 2
        def wait3():
            for k in (1, 2, 3):
                j = lax.rem(z + k, 4)
                d = dst.at[pl.ds(pl.multiple_of(j * 112, 16), 112)]
                got(d, S(0, 0, 1), R(0, slot * 4 + j, 2), X)
        when(mine, wait3)
        send(mine, dst, dst, S(0, 8 + slot, 3), R(0, 8 + slot, 3), C)

    def rows_have(dst, slot):
        when(c != z // 2, lambda: got(dst, S(0, 8 + slot, 3), R(0, 8 + slot, 3), C))

    for i in range(NU):
        core_exchange(i)
    rows_out(tok, g_tok, 0)
    mine = c == z // 2
    enc_parts = []

    def enc_src(part):
        return enc.at[lax.rem(z, 2), part]

    def enc_local(part, slot):
        return pltpu.make_async_copy(enc_src(part), g_enc.at[part], loc.at[NU + 2 + slot])

    def enc_start(part, slot):
        enc_local(part, slot).start()

    for t in range(NU + 6):
        if t < NU:
            own(t)
        for k in (1, 2, 3):
            if 0 <= t - k < NU:
                hop(t - k, k)
        for k in (0, 1, 2, 3):
            if 0 <= t - k - 1 < NU:
                cross(t - k - 1, k)
        if t == 5:
            rows_in(g_tok, 0)
        if t == 10:
            rows_out(cot, g_cot, 1)
        if t == 17:
            rows_in(g_cot, 1)
        if t in (6, 8, 10):
            part = slice((t - 6) * 256, (t - 4) * 256 if t < 10 else 1500)
            enc_parts.append((part, (t - 6) // 2))
            send(mine, enc_src(part), g_enc.at[part], S(0, (t - 6) // 2, 3), R(0, 4 + (t - 6) // 2, 3), C)
            when(mine, functools.partial(enc_start, part, (t - 6) // 2))
        for k in (0, 1, 2, 3):
            if 0 <= t - k - 2 < NU:
                last(t - k - 2, k)
    rows_have(g_tok, 0)
    rows_have(g_cot, 1)
    for part, slot in enc_parts:
        when(mine, lambda: enc_local(part, slot).wait())
        when(c != z // 2, lambda: got(g_enc.at[part], S(0, 0, 3), R(0, 4 + slot, 3), C))
    for cond, fn in waits:
        when(cond, fn)


def gather(tok, enc, cot, w_in, w_out, w_up, w_down):
    any_ = pl.BlockSpec(memory_space=pl.ANY)
    NU = len(UNITS)
    shapes = [(448, 1024), (1500, 1024), (448, 1024), (6, 1024, 512), (2, 512, 1024), (1024, 2048), (2048, 1024)]
    return pl.pallas_call(
        gather_kernel,
        out_shape=[jax.ShapeDtypeStruct(s, bf16) for s in shapes],
        in_specs=[any_] * 7,
        out_specs=[any_] * 7,
        scratch_shapes=[
            pltpu.SemaphoreType.DMA((6, NU, 4)),
            pltpu.SemaphoreType.DMA((6, NU, 4)),
            pltpu.SemaphoreType.DMA((NU + 5,)),
        ],
        compiler_params=pltpu.CompilerParams(collective_id=1, has_side_effects=True),
    )(tok, enc, cot, w_in, w_out, w_up, w_down)


def dot(a, b, dims):
    return lax.dot_general(a, b, (dims, ((), ())), preferred_element_type=f32)


def mm(a, b):
    return dot(a, b, ((1,), (0,)))


def mm_t(a, b):
    return dot(a, b, ((1,), (1,)))


def t_mm(a, b):
    return dot(a, b, ((0,), (0,)))


def layer_norm(inputs, gain_row, shift_row):
    centered = inputs - jnp.mean(inputs, axis=-1, keepdims=True)
    variance = jnp.mean(centered * centered, axis=-1, keepdims=True)
    return centered * lax.rsqrt(variance + epsilon) * gain_row + shift_row


def norm_back(hidden, gain_row, shift_row, grad):
    return jax.vjp(lambda rows: layer_norm(rows, gain_row, shift_row), hidden)[1](grad)[0]


def heads_of(rows):
    return rows.reshape(rows.shape[0], rows.shape[1] // HD, HD)


def make_scores(queries, keys, causal):
    scores = jnp.einsum("qhe,khe->hqk", queries, keys, preferred_element_type=f32) * HD**-0.5
    if causal:
        allowed = jnp.arange(queries.shape[0])[:, None] >= jnp.arange(keys.shape[0])[None, :]
        scores = jnp.where(allowed, scores, masked_score)
    return scores


def attend_forward(queries, keys, values, causal):
    scores = make_scores(heads_of(queries), heads_of(keys), causal)
    highest = jnp.max(scores, axis=-1, keepdims=True)
    expanded = jnp.exp(scores - highest)
    totals = jnp.sum(expanded, axis=-1, keepdims=True)
    probs = (expanded / totals).astype(bf16)
    mixture = jnp.einsum("hqk,khe->qhe", probs, heads_of(values), preferred_element_type=f32)
    return mixture.reshape(queries.shape).astype(bf16), highest + jnp.log(totals)


def attend_backward(queries, keys, values, log_total, grad, causal):
    qh, kh, vh, gh = (heads_of(rows) for rows in (queries, keys, values, grad))
    probs = jnp.exp(make_scores(qh, kh, causal) - log_total)
    grad_values = jnp.einsum("hqk,qhe->khe", probs.astype(bf16), gh, preferred_element_type=f32)
    grad_probs = jnp.einsum("qhe,khe->hqk", gh, vh, preferred_element_type=f32)
    grad_scores = probs * (grad_probs - jnp.sum(probs * grad_probs, axis=-1, keepdims=True))
    grad_scores = grad_scores.astype(bf16)
    grad_queries = jnp.einsum("hqk,khe->qhe", grad_scores, kh, preferred_element_type=f32) * HD**-0.5
    grad_keys = jnp.einsum("hqk,qhe->khe", grad_scores, qh, preferred_element_type=f32) * HD**-0.5
    return (
        grad_queries.reshape(queries.shape).astype(bf16),
        grad_keys.reshape(keys.shape).astype(bf16),
        grad_values.reshape(values.shape).astype(bf16),
    )


def swap_core(rows):
    return lax.ppermute(rows, "core", SWAP)


def core_sum(part):
    return part + swap_core(part)


def own_and_other(stacked):
    core = lax.axis_index("core")
    keep = lax.dynamic_index_in_dim(stacked, core, 0, keepdims=False)
    send = lax.dynamic_index_in_dim(stacked, 1 - core, 0, keepdims=False)
    return keep, swap_core(send)


def in_core_order(own, other):
    first = lax.axis_index("core") == 0
    return jnp.stack([jnp.where(first, own, other), jnp.where(first, other, own)])


def scatter_sh(stacked):
    n = lax.axis_size("sh")
    if n == 2:
        me = lax.axis_index("sh")
        keep = lax.dynamic_index_in_dim(stacked, me, 0, keepdims=False)
        send = lax.dynamic_index_in_dim(stacked, 1 - me, 0, keepdims=False)
        return keep + lax.ppermute(send, "sh", SWAP)
    return lax.psum_scatter(stacked, "sh", scatter_dimension=0, tiled=False)


def over_z(stacked):
    return lax.all_to_all(stacked, "tp", 0, 0, tiled=True)


def half_columns(rows):
    width = rows.shape[-1] // 2
    return lax.dynamic_slice_in_dim(rows, lax.axis_index("core") * width, width, rows.ndim - 1)


def rows_home(half):
    tp = lax.axis_size("tp")
    moved = over_z(half.reshape(tp, half.shape[0] // tp, half.shape[1]))
    own, other = own_and_other(moved.reshape(2, tp // 2, *moved.shape[1:]))
    both = in_core_order(own, other)
    return jnp.moveaxis(both, 0, 2).reshape(both.shape[1], both.shape[2], 2 * half.shape[1])


def rows_here(rows):
    tp = lax.axis_size("tp")
    both = in_core_order(rows, swap_core(rows)).reshape(4, *rows.shape[1:])
    moved = over_z(half_columns(both))
    moved = moved.reshape(tp * rows.shape[1], rows.shape[2] // 2)
    pair = in_core_order(moved, swap_core(moved))
    return jnp.concatenate([pair[0], pair[1]], axis=-1)


def gather_weights(w_attn_in, w_attn_out, w_up, w_down):
    def over_shard(block, axis):
        return lax.all_gather(block, ("sh", "core"), axis=axis, tiled=True)

    def over_tp(block, axis):
        return lax.all_gather(block, "tp", axis=axis, tiled=True)

    core = lax.axis_index("core")

    def half(block, axis):
        width = block.shape[axis] // 2
        return lax.dynamic_slice_in_dim(block, core * width, width, axis)

    w_in = over_tp(half(over_shard(w_attn_in.reshape(6, *w_attn_in.shape[3:]), 1), 2), 2)
    w_out = over_tp(half(over_shard(w_attn_out[0], 2), 1), 1)
    w_first = over_tp(half(over_shard(w_up[0], 0), 1), 1)
    w_second = over_tp(half(over_shard(w_down[0], 1), 0), 0)
    return w_in, w_out, w_first, w_second


def on_device(
    tokens,
    encoded,
    cotangent,
    adapter_of,
    w_attn_in,
    w_attn_out,
    w_up,
    w_down,
    norm_gain,
    norm_shift,
    down_attn_in,
    up_attn_in,
    down_feed_in,
    up_feed_in,
    down_attn_out,
    up_attn_out,
    down_feed_out,
    up_feed_out,
):
    n, tp = lax.axis_size("sh"), lax.axis_size("tp")
    sh, core, z = lax.axis_index("sh"), lax.axis_index("core"), lax.axis_index("tp")
    width = w_attn_in.shape[3] * 2 * n
    held_rows = down_feed_in.shape[1]
    quarter = width // tp
    piece = quarter // 2

    ids = lax.all_gather(adapter_of, ("sh", "core"), tiled=True)

    row_ids = (sh * 2 + core) * held_rows + jnp.arange(held_rows)
    wanted = ids.reshape(n, tp)[:, :, None] * RANK + jnp.arange(RANK)
    picks = (wanted[..., None] == row_ids).astype(bf16)
    whole = jnp.concatenate(
        [
            down_attn_in.reshape(6, held_rows, width),
            down_feed_in,
            up_attn_out[0],
            up_feed_out,
        ]
    )
    def in_quarters(rows):
        return jnp.moveaxis(rows.reshape(held_rows, tp, quarter), 1, 0)

    split = jnp.concatenate(
        [
            up_attn_in.reshape(6, held_rows, quarter),
            in_quarters(up_feed_in[0]),
            down_attn_out[0],
            in_quarters(down_feed_out[0]),
        ]
    )
    picks_z = lax.dynamic_index_in_dim(picks, z, 1, keepdims=False)
    chosen_whole = jnp.einsum("srk,mkd->smrd", picks_z, whole, preferred_element_type=f32).astype(bf16)
    chosen_split = jnp.einsum("szrk,mkd->szmrd", picks, split, preferred_element_type=f32).astype(bf16)
    chosen_whole = core_sum(scatter_sh(chosen_whole))
    chosen_split = over_z(core_sum(scatter_sh(chosen_split)))

    def columns(first, count):
        mine = half_columns(chosen_split[:, first : first + count])
        return jnp.moveaxis(mine, 0, 2).reshape(count, RANK, tp * piece)

    def wide_columns(first):
        mine = lax.dynamic_slice_in_dim(chosen_split[:, first : first + tp], core * 2, 2, 1)
        return jnp.moveaxis(mine, 2, 0).reshape(RANK, tp * 2 * quarter)

    a_in, a_up, b_out, b_down = chosen_whole[:6], chosen_whole[6], chosen_whole[7:9], chosen_whole[9]
    b_in, b_up, a_out, a_down = columns(0, 6), wide_columns(6), columns(6 + tp, 2), wide_columns(8 + tp)

    if n == 2:
        taken, memory, upstream, w_in, w_out, w_first, w_second = gather(
            tokens,
            encoded,
            cotangent,
            w_attn_in.reshape(6, *w_attn_in.shape[3:]),
            w_attn_out[0],
            w_up[0],
            w_down[0],
        )
    else:
        w_in, w_out, w_first, w_second = gather_weights(w_attn_in, w_attn_out, w_up, w_down)
        taken = rows_here(tokens)
        upstream = rows_here(cotangent)
        mine = lax.dynamic_index_in_dim(encoded, z % 2, 0, keepdims=False)
        memory = jnp.where(core == z // 2, mine, swap_core(mine))

    def merge(weight, down_rows, up_rows):
        return (weight.astype(f32) + t_mm(down_rows, up_rows)).astype(bf16)

    w_in = [merge(w_in[i], a_in[i], b_in[i]) for i in range(6)]
    w_out = [merge(w_out[i], a_out[i], b_out[i]) for i in range(2)]
    w_first = merge(w_first, a_up, b_up)
    w_second = merge(w_second, a_down, b_down)

    hidden = taken.astype(f32)

    kept = []
    for side in range(2):
        normed = layer_norm(hidden, norm_gain[0, side], norm_shift[0, side]).astype(bf16)
        source = normed if side == 0 else memory
        queries = mm(normed, w_in[3 * side]).astype(bf16)
        keys = mm(source, w_in[3 * side + 1]).astype(bf16)
        values = mm(source, w_in[3 * side + 2]).astype(bf16)
        mixture, log_total = attend_forward(queries, keys, values, side == 0)
        kept.append((hidden, normed, source, queries, keys, values, mixture, log_total))
        hidden = hidden + core_sum(mm(mixture, w_out[side]))
    normed = layer_norm(hidden, norm_gain[0, 2], norm_shift[0, 2]).astype(bf16)
    pre_active = mm(normed, w_first)
    active = jax.nn.gelu(pre_active, approximate=False).astype(bf16)
    result = (hidden + core_sum(mm(active, w_second))).astype(bf16)
    activations = rows_home(half_columns(result))

    grad_hidden = upstream.astype(f32)
    grad_active = mm_t(upstream, w_second)
    _, gelu_back = jax.vjp(partial(jax.nn.gelu, approximate=False), pre_active)
    grad_pre = gelu_back(grad_active)[0].astype(bf16)
    grad_hidden = grad_hidden + norm_back(
        hidden, norm_gain[0, 2], norm_shift[0, 2], core_sum(mm_t(grad_pre, w_first))
    )

    def rank_grads(inputs, grad, down_rows, up_rows):
        inner = mm_t(inputs, down_rows).astype(bf16)
        back = mm_t(grad, up_rows).astype(bf16)
        return t_mm(back, inputs), t_mm(inner, grad)

    split_grads, whole_grads = [None] * 4, [None] * 4
    whole_grads[1], split_grads[1] = rank_grads(normed, grad_pre, a_up, b_up)
    split_grads[3], whole_grads[3] = rank_grads(active, upstream, a_down, b_down)
    in_whole, in_split, out_whole, out_split = [None] * 6, [None] * 6, [None] * 2, [None] * 2
    for side in (1, 0):
        hidden, normed, source, queries, keys, values, mixture, log_total = kept[side]
        upstream = grad_hidden.astype(bf16)
        grad_mixture = mm_t(upstream, w_out[side]).astype(bf16)
        out_split[side], out_whole[side] = rank_grads(mixture, upstream, a_out[side], b_out[side])
        grads = attend_backward(queries, keys, values, log_total, grad_mixture, side == 0)
        terms = [mm_t(grads[i], w_in[3 * side + i]) for i in range(3)]
        for i in range(3):
            inputs = normed if i == 0 else source
            in_whole[3 * side + i], in_split[3 * side + i] = rank_grads(
                inputs, grads[i], a_in[3 * side + i], b_in[3 * side + i]
            )
        if side == 1:
            part = (terms[1] + terms[2]).astype(bf16)
            own, other = own_and_other(jnp.moveaxis(part.reshape(part.shape[0], 2, -1), 1, 0))
            grad_encoded = rows_home((own.astype(f32) + other.astype(f32)).astype(bf16)).astype(f32)
            term = terms[0]
        else:
            term = terms[0] + terms[1] + terms[2]
        grad_hidden = grad_hidden + norm_back(
            hidden, norm_gain[0, side], norm_shift[0, side], core_sum(term)
        )
    grad_tokens = rows_home(half_columns(grad_hidden).astype(bf16)).astype(f32)

    def in_pieces(rows):
        return jnp.moveaxis(rows.reshape(RANK, tp, piece), 1, 0)[:, None]

    def in_wide_pieces(rows):
        return jnp.moveaxis(rows.reshape(RANK, tp, tp, piece), 0, 2)

    partial_whole = jnp.stack(in_whole + [whole_grads[1]] + out_whole + [whole_grads[3]]).astype(bf16)
    partial_whole = jnp.moveaxis(partial_whole.reshape(-1, RANK, tp, 2, piece), (3, 2), (0, 1))
    own, other = own_and_other(jnp.moveaxis(partial_whole, 2, 2))
    compact = jnp.concatenate(
        [in_pieces(rows) for rows in in_split]
        + [in_wide_pieces(split_grads[1])]
        + [in_pieces(rows) for rows in out_split]
        + [in_wide_pieces(split_grads[3])],
        axis=1,
    ).astype(bf16)
    compact = jnp.concatenate([compact, own + other], axis=1)
    compact = over_z(compact)
    here = ids.reshape(n, tp)[sh]
    rows = jnp.arange(2 * n * held_rows)
    place = (here[:, None] * RANK + jnp.arange(RANK))[None] == rows[:, None, None]
    dense = jnp.einsum("gkr,kmrp->gmp", place.astype(bf16), compact, preferred_element_type=f32)
    dense = dense.astype(bf16).reshape(n, 2, held_rows, *dense.shape[1:])
    dense = scatter_sh(dense)
    dense = dense + lax.ppermute(dense, "rep", SWAP)
    both = in_core_order(*own_and_other(dense))
    done = jnp.moveaxis(both, 0, 2)
    count = 8 + 2 * tp
    sums = done[:, :count].astype(f32)

    def narrow(first, number):
        block = sums[:, first : first + number].reshape(held_rows, number, quarter)
        return jnp.moveaxis(block, 1, 0)

    def wide(first):
        block = sums[:, first : first + tp].reshape(held_rows, 2, tp // 2, 2, piece)
        return block

    def wide_of(first):
        block = jnp.moveaxis(sums[:, first : first + tp], 2, 1)
        return block.reshape(held_rows, 2 * tp * piece)

    grad_up_attn_in = narrow(0, 6).reshape(1, 2, 3, held_rows, quarter)
    grad_up_feed_in = wide_of(6)[None]
    grad_down_attn_out = narrow(6 + tp, 2)[None]
    grad_down_feed_out = wide_of(8 + tp)[None]
    rest = done[:, count:].reshape(tp, held_rows // tp, 10, quarter)
    rest = jnp.moveaxis(over_z(rest), 0, 2)
    rest = jnp.moveaxis(rest.reshape(held_rows // tp, 10, width), 1, 0).astype(f32)
    return (
        activations,
        grad_tokens,
        grad_encoded,
        rest[:6].reshape(1, 2, 3, held_rows // tp, width),
        grad_up_attn_in,
        rest[6:7],
        grad_up_feed_in,
        grad_down_attn_out,
        rest[7:9][None],
        grad_down_feed_out,
        rest[9:10],
    )


def solution(mesh):
    rep, shard, tp = (mesh.shape[name] for name in ("rep", "shard", "tp"))
    fine = Mesh(mesh.devices.reshape(rep, shard // 2, 2, tp), ("rep", "sh", "core", "tp"))
    shard = ("sh", "core")
    clips = ("rep", "sh", "core")
    both = ("sh", "core", "tp")
    placed = (
        P(clips, "tp", None),
        P(clips, None, None),
        P(clips, "tp", None),
        P(clips),
        P(None, None, None, shard, "tp"),
        P(None, None, "tp", shard),
        P(None, shard, "tp"),
        P(None, "tp", shard),
        P(),
        P(),
        P(None, None, None, shard, None),
        P(None, None, None, shard, "tp"),
        P(None, shard, None),
        P(None, shard, "tp"),
        P(None, None, shard, "tp"),
        P(None, None, shard, None),
        P(None, shard, "tp"),
        P(None, shard, None),
    )
    return jax.shard_map(
        on_device,
        mesh=fine,
        in_specs=placed,
        out_specs=(
            P(clips, "tp", None),
            P(clips, "tp", None),
            P(clips, "tp", None),
            P(None, None, None, both, None),
            P(None, None, None, shard, "tp"),
            P(None, both, None),
            P(None, shard, "tp"),
            P(None, None, shard, "tp"),
            P(None, None, both, None),
            P(None, shard, "tp"),
            P(None, both, None),
        ),
        check_vma=False,
    )
```

```python
import functools

import jax
import jax.numpy as jnp
from jax import lax
from jax.experimental import pallas as pl
from jax.experimental.pallas import tpu as pltpu
from jax.sharding import Mesh, PartitionSpec as P

HD = 64
RANK = 16
epsilon = 1e-05
masked_score = -1e30
f32, bf16 = jnp.float32, jnp.bfloat16
SWAP = ((0, 1), (1, 0))
MESH = pl.DeviceIdType.MESH


def dot(a, b, dims):
    return lax.dot_general(a, b, (dims, ((), ())), preferred_element_type=f32)


def mm(a, b):
    return dot(a, b, ((1,), (0,)))


def mm_t(a, b):
    return dot(a, b, ((1,), (1,)))


def t_mm(a, b):
    return dot(a, b, ((0,), (0,)))


HIDE = -1e30
SCALE = HD**-0.5
EPS = 1e-05
VM = pl.BlockSpec(memory_space=pltpu.VMEM)


def nn(a, b):
    return lax.dot_general(a, b, (((1,), (0,)), ((), ())), preferred_element_type=f32)


def nt(a, b):
    return lax.dot_general(a, b, (((1,), (1,)), ((), ())), preferred_element_type=f32)


def normalize(rows):
    centered = rows - jnp.mean(rows, axis=-1, keepdims=True)
    variance = jnp.mean(centered * centered, axis=-1, keepdims=True)
    inverse = lax.rsqrt(variance + EPS)
    return centered * inverse, inverse


def norm_back(rows, gain, grad):
    unit, inverse = normalize(rows)
    scaled = grad * gain
    first = jnp.mean(scaled, axis=-1, keepdims=True)
    second = jnp.mean(scaled * unit, axis=-1, keepdims=True)
    return (scaled - first - unit * second) * inverse


def pair_lanes(p):
    return pl.ds(pl.multiple_of(p * 128, 128), 128)


def scores_t(keys, queries, frames, causal):
    s = nt(keys, queries) * SCALE
    if causal:
        key = lax.broadcasted_iota(jnp.int32, s.shape, 0)
        query = lax.broadcasted_iota(jnp.int32, s.shape, 1)
        s = jnp.where(query >= key, s, HIDE)
    elif frames < s.shape[0]:
        full = frames // 128 * 128
        key = full + lax.broadcasted_iota(jnp.int32, (s.shape[0] - full, s.shape[1]), 0)
        s = jnp.concatenate([s[:full], jnp.where(key < frames, s[full:], HIDE)])
    return s


def attend_forward(q, k, v, mix, lse, frames, causal, start=0, number=None):
    def pair(p, carry):
        lanes = pair_lanes(p)
        qp, kp = q[:, lanes], k[:, lanes]
        vt = v[:, lanes].T
        first = lax.broadcasted_iota(jnp.int32, qp.shape, 1) < HD
        outs, logs = [], []
        for h in (0, 1):
            s = scores_t(kp, jnp.where(first == (h == 0), qp, 0), frames, causal)
            top = jnp.max(s, axis=0, keepdims=True)
            e = jnp.exp(s - top)
            total = jnp.sum(e, axis=0, keepdims=True)
            probs = (e * (1.0 / total)).astype(bf16)
            outs.append(nn(vt, probs)[h * HD : (h + 1) * HD])
            logs.append(top + jnp.log(total))
        mix[:, lanes] = jnp.concatenate(outs).T.astype(bf16)
        lse[p] = jnp.concatenate(logs)
        return carry

    lax.fori_loop(start, start + (number or q.shape[1] // 128), pair, 0)


def attend_backward(q, k, v, do, lse, dq, dk, dv, frames, causal):
    def pair(p, carry):
        lanes = pair_lanes(p)
        qp, kp, vp, dop = q[:, lanes], k[:, lanes], v[:, lanes], do[:, lanes]
        kt = kp.T
        logs = lse[p]
        first = lax.broadcasted_iota(jnp.int32, qp.shape, 1) < HD
        dqs, dks, dvs = [], [], []
        for h in (0, 1):
            mine = first == (h == 0)
            s = scores_t(kp, jnp.where(mine, qp, 0), frames, causal)
            probs = jnp.exp(s - logs[h : h + 1])
            dvs.append(nn(probs.astype(bf16), dop))
            dp = nt(vp, jnp.where(mine, dop, 0))
            t = probs * dp
            ds = (t - probs * jnp.sum(t, axis=0, keepdims=True)).astype(bf16)
            dks.append(nn(ds, qp))
            dqs.append(nn(kt, ds)[h * HD : (h + 1) * HD])
        first_k = lax.broadcasted_iota(jnp.int32, kp.shape, 1) < HD
        dv[:, lanes] = jnp.where(first_k, dvs[0], dvs[1]).astype(bf16)
        dk[:, lanes] = (jnp.where(first_k, dks[0], dks[1]) * SCALE).astype(bf16)
        dq[:, lanes] = (jnp.concatenate(dqs).T * SCALE).astype(bf16)
        return carry

    lax.fori_loop(0, q.shape[1] // 128, pair, 0)


def params():
    return pltpu.CompilerParams(vmem_limit_bytes=60 * 1024 * 1024)


def sds(shape, dtype):
    return jax.ShapeDtypeStruct(shape, dtype)


def self_forward(tok, gain, shift, wi, wo):
    def kernel(tok, gain, shift, wi, wo, normed, q, k, v, lse, mix, part):
        unit, _ = normalize(tok[...].astype(f32))
        normed[...] = (unit * gain[...] + shift[...]).astype(bf16)
        for i, out in enumerate((q, k, v)):
            out[...] = nn(normed[...], wi[i]).astype(bf16)
        attend_forward(q, k, v, mix, lse, tok.shape[0], True)
        part[...] = nn(mix[...], wo[...])

    r, d = tok.shape
    w = wi.shape[2]
    return pl.pallas_call(kernel, out_shape=[sds((r, d), bf16)] + [sds((r, w), bf16)] * 3 + [sds((w // 128, 2, r), f32), sds((r, w), bf16), sds((r, d), f32)],
        in_specs=[VM] * 5, out_specs=[VM] * 7, compiler_params=params(), name="self_forward")(tok, gain, shift, wi, wo)


def memory_project(enc, wi):
    def kernel(enc, wi, k, v):
        frames = enc.shape[0]
        for i, out in enumerate((k, v)):
            out[:frames] = nn(enc[...], wi[i]).astype(bf16)
            out[frames:] = jnp.zeros((out.shape[0] - frames, out.shape[1]), bf16)
    frames = -(-enc.shape[0] // 128) * 128
    return pl.pallas_call(kernel, out_shape=[sds((frames, wi.shape[2]), bf16)] * 2, in_specs=[VM] * 2, out_specs=[VM] * 2, compiler_params=params(), name="memory_project")(enc, wi)


def cross_forward(hid, part, other, gain, shift, wq, k, v, wo, frames):
    def kernel(hid, part, other, gain, shift, wq, k, v, wo, hidden, normed, q, lse, mix, out):
        hidden[...] = hid[...].astype(f32) + part[...] + other[...]
        unit, _ = normalize(hidden[...])
        normed[...] = (unit * gain[...] + shift[...]).astype(bf16)
        q[...] = nn(normed[...], wq[...]).astype(bf16)
        attend_forward(q, k, v, mix, lse, frames, False)
        out[...] = nn(mix[...], wo[...])

    r, d = hid.shape
    w = wq.shape[1]
    return pl.pallas_call(kernel, out_shape=[sds((r, d), f32), sds((r, d), bf16), sds((r, w), bf16), sds((w // 128, 2, r), f32), sds((r, w), bf16), sds((r, d), f32)],
        in_specs=[VM] * 9, out_specs=[VM] * 6, compiler_params=params(), name="cross_forward")(hid, part, other, gain, shift, wq, k, v, wo)


def rank_t(rows16, inputs):
    return nt(rows16, inputs).astype(bf16)


def feed(hid, part, other, gain, shift, up, down, e, a_up, b_up, a_down, b_down):
    CH = 512

    def kernel(hid, part, other, gain, shift, up, down, e, a_up, b_up, a_down, b_down, hidden, out, back, g_aup, g_bup, g_adown, g_bdown, normed):
        hidden[...] = hid[...] + part[...] + other[...]
        unit, _ = normalize(hidden[...])
        normed[...] = (unit * gain[...] + shift[...]).astype(bf16)
        t_in = rank_t(a_up[...], normed[...])
        r_out = rank_t(b_down[...], e[...])
        r_in = jnp.zeros((16, hid.shape[0]), f32)
        t_out = jnp.zeros((16, hid.shape[0]), f32)
        for j in range(up.shape[1] // CH):
            cols = slice(j * CH, (j + 1) * CH)
            pre = nn(normed[...], up[:, cols])
            cdf = 0.5 * (1.0 + lax.erf(pre * (2**-0.5)))
            active = (pre * cdf).astype(bf16)
            slope = cdf + pre * jnp.exp(-0.5 * pre * pre) * 0.3989422804014327
            grad = (nt(e[...], down[cols]) * slope).astype(bf16)
            term, term_b = nn(active, down[cols]), nt(grad, up[:, cols])
            if j == 0:
                out[...], back[...] = term, term_b
            else:
                out[...] += term
                back[...] += term_b
            g_bup[:, cols] = nn(t_in, grad)
            g_adown[:, cols] = nn(r_out, active)
            r_in += nt(b_up[:, cols], grad)
            t_out += nt(a_down[:, cols], active)
        g_aup[...] = nn(r_in.astype(bf16), normed[...])
        g_bdown[...] = nn(t_out.astype(bf16), e[...])

    r, d = hid.shape
    w = up.shape[1]
    return pl.pallas_call(kernel, out_shape=[sds((r, d), f32)] * 3 + [sds((16, d), f32), sds((16, w), f32), sds((16, w), f32), sds((16, d), f32)],
        in_specs=[VM] * 12, out_specs=[VM] * 7, scratch_shapes=[pltpu.VMEM((r, d), bf16)], compiler_params=params(), name="feed")(
            hid, part, other, gain, shift, up, down, e, a_up, b_up, a_down, b_down)


def cross_backward(hid3, gain3, g, part, other, wo, wq, q, k, v, lse, frames):
    def kernel(hid3, gain3, g, part, other, wo, wq, q, k, v, lse, g_out, e, dq, dk, dv, back, do):
        g_out[...] = g[...].astype(f32) + norm_back(hid3[...], gain3[...], part[...] + other[...])
        e[...] = g_out[...].astype(bf16)
        do[...] = nt(e[...], wo[...]).astype(bf16)
        attend_backward(q, k, v, do, lse, dq, dk, dv, frames, False)
        back[...] = nt(dq[...], wq[...])

    r, d = hid3.shape
    w, f = q.shape[1], k.shape[0]
    return pl.pallas_call(kernel, out_shape=[sds((r, d), f32), sds((r, d), bf16), sds((r, w), bf16), sds((f, w), bf16), sds((f, w), bf16), sds((r, d), f32)],
        in_specs=[VM] * 11, out_specs=[VM] * 6, scratch_shapes=[pltpu.VMEM((r, w), bf16)], compiler_params=params(), name="cross_backward")(
            hid3, gain3, g, part, other, wo, wq, q, k, v, lse)


def self_backward(hid2, gain2, g, part, other, wo, wi, q, k, v, lse):
    def kernel(hid2, gain2, g, part, other, wo, wi, q, k, v, lse, g_out, e, dq, dk, dv, back, do):
        g_out[...] = g[...] + norm_back(hid2[...], gain2[...], part[...] + other[...])
        e[...] = g_out[...].astype(bf16)
        do[...] = nt(e[...], wo[...]).astype(bf16)
        attend_backward(q, k, v, do, lse, dq, dk, dv, q.shape[0], True)
        back[...] = nt(dq[...], wi[0])
        back[...] += nt(dk[...], wi[1])
        back[...] += nt(dv[...], wi[2])

    r, d = hid2.shape
    w = q.shape[1]
    return pl.pallas_call(kernel, out_shape=[sds((r, d), f32), sds((r, d), bf16)] + [sds((r, w), bf16)] * 3 + [sds((r, d), f32)],
        in_specs=[VM] * 11, out_specs=[VM] * 6, scratch_shapes=[pltpu.VMEM((r, w), bf16)], compiler_params=params(), name="self_backward")(
            hid2, gain2, g, part, other, wo, wi, q, k, v, lse)


def final_norm(hid, gain, g, part, other):
    def kernel(hid, gain, g, part, other, out):
        out[...] = (g[...] + norm_back(hid[...].astype(f32), gain[...], part[...] + other[...])).astype(bf16)

    return pl.pallas_call(kernel, out_shape=sds(hid.shape, bf16), in_specs=[VM] * 5, out_specs=VM, compiler_params=params(), name="final_norm")(hid, gain, g, part, other)


def memory_backward(dk, dv, wi, frames):
    def kernel(dk, dv, wi, out):
        out[...] = (nt(dk[:frames], wi[0]) + nt(dv[:frames], wi[1])).astype(bf16)
    d = wi.shape[1]
    return pl.pallas_call(kernel, out_shape=sds((frames, d), bf16), in_specs=[VM] * 3, out_specs=VM, compiler_params=params(), name="memory_backward")(dk, dv, wi)


def attention_ranks(normed, source, mix, dq, dk, dv, e, a_in, b_in, a_out, b_out):
    def kernel(*refs):
        operands, results = refs[:-4], refs[-4:]
        given = operands[:7] if source is not None else operands[:1] + operands[:1] + operands[1:6]
        normed, source_, mix, dq, dk, dv, e = given
        a_in, b_in, a_out, b_out = operands[-4:]
        ga_in, gb_in, ga_out, gb_out = results
        for i, (u, g) in enumerate(((normed, dq), (source_, dk), (source_, dv))):
            rows = u.shape[0]
            inner = rank_t(a_in[i], u[...])
            back = rank_t(b_in[i], g[:rows])
            gb_in[i] = nn(inner, g[:rows]).astype(bf16)
            ga_in[i] = nn(back, u[...]).astype(bf16)
        ga_out[...] = nn(rank_t(b_out[...], e[...]), mix[...]).astype(bf16)
        gb_out[...] = nn(rank_t(a_out[...], mix[...]), e[...]).astype(bf16)

    args = [normed] + ([source] if source is not None else []) + [mix, dq, dk, dv, e, a_in, b_in, a_out, b_out]
    return pl.pallas_call(kernel, out_shape=[sds(t.shape, bf16) for t in (a_in, b_in, a_out, b_out)],
        in_specs=[VM] * len(args), out_specs=[VM] * 4, compiler_params=params(), name="attention_ranks")(*args)


OFFS = (2, 3, 4, 6, 8)


class Unit:
    def __init__(self, place, kind, index):
        self.place, self.tall, self.index = place, kind == "a", index
        self.rows = 512 if self.tall else 128
        late = place >= 10
        if self.tall:
            self.most, self.via_y = (496, 400) if late else (400, 304)
        else:
            self.most, self.via_y = (112, 96) if late else (96, 80)


def make_units():
    order = [("a", 0), ("a", 1), ("a", 2), ("b", 0), ("a", 3), ("a", 4), ("a", 5), ("b", 1)]
    for j in range(4):
        order += [("a", 6 + j), ("b", 2 + j)]
    return [Unit(i, kind, index) for i, (kind, index) in enumerate(order)]


def layer_kernel(
    tok, enc, cot, w_in, w_out, w_up, w_down, ids, gain, shift,
    d_ai, u_ai, d_fi, u_fi, d_ao, u_ao, d_fo, u_fo,
    result, g_rows, g_memory, gsplit, gwhole,
    ga, gb, rows, grads, memory, normed, q0, k0, v0, mix, q1, k1, v1, lse, hidden, g_now, do, dq, dkv,
    outbox, inbox, idbuf, cs, cw, rs, rw, ys, yw, fz, fw, r_in, t_out, r_up,
    core_s, core_r, up_s, dn_s, z_r, y_s, y_r, x_s, x_r, row_s, row_r, loc, ad_s, ad_r, ex_s, ex_r,
):
    units = make_units()
    count = len(units)
    frames = enc.shape[1]
    x, y, c, z = (lax.axis_index(a) for a in ("rep", "sh", "core", "tp"))
    al = pl.multiple_of
    sent = {}

    def when(cond, fn):
        fn() if cond is None else pl.when(cond)(fn)

    def remote(src, dst, s, r, dev):
        return pltpu.make_async_remote_copy(
            src_ref=src, dst_ref=dst, send_sem=s, recv_sem=r, device_id=dev, device_id_type=MESH
        )

    def send(key, cond, src, dst, s, r, dev):
        when(cond, lambda: remote(src, dst, s, r, dev).start())
        sent.setdefault(key, []).append((cond, lambda: remote(src, dst, s, r, dev).wait_send()))

    def settle(key):
        for cond, fn in sent.pop(key, []):
            when(cond, fn)

    X, Y, C = {"rep": 1 - x}, {"sh": 1 - y}, {"core": 1 - c}
    YC = {"sh": 1 - y, "core": 1 - c}
    UP, DOWN = {"tp": z + 1}, {"tp": z - 1}
    others = [lax.rem(z + k, 4) for k in (1, 2, 3)]

    def got(dst, r):
        remote(dst, dst, r, r, X).wait_recv()

    bar = pltpu.get_barrier_semaphore()
    for dev in [X, Y, C, YC] + [{"tp": j} for j in others]:
        pl.semaphore_signal(bar, inc=1, device_id=dev, device_id_type=MESH)
    pl.semaphore_wait(bar, 7)

    def block(u, yy, zz, first, size):
        if u.tall:
            return ga.at[pl.ds(al(u.index * 1024 + yy * 512 + first, 16), size), pl.ds(al(zz * 128, 128), 128)]
        return gb.at[u.index, zz, pl.ds(al(first, 16), size), pl.ds(al(yy * 512, 512), 512)]

    def across(u, yy, first, size):
        if u.tall:
            return ga.at[pl.ds(al(u.index * 1024 + yy * 512 + first, 16), size)]
        return gb.at[u.index, :, pl.ds(al(first, 16), size), pl.ds(al(yy * 512, 512), 512)]

    def three(u, first, size):
        if u.tall:
            return ga.at[pl.ds(al(u.index * 1024 + y * 512 + first, 16), size), 0:384]
        return gb.at[u.index, 0:3, pl.ds(al(first, 16), size), pl.ds(al(y * 512, 512), 512)]

    def half_src(u, cc):
        m = u.index
        if u.tall:
            if m < 6:
                return w_in.at[m, :, pl.ds(al(cc * 128, 128), 128)]
            return w_up.at[:, pl.ds(al(cc * 512 + (m - 6) * 128, 128), 128)]
        if m < 2:
            return w_out.at[m, pl.ds(al(cc * 128, 128), 128)]
        return w_down.at[pl.ds(al(cc * 512 + (m - 2) * 128, 128), 128)]

    def half_dst(u, cc):
        if u.tall:
            return block(u, y, z, cc * 256, 256)
        return gb.at[u.index, z, :, pl.ds(al(y * 512 + cc * 256, 256), 256)]

    def core_exchange(u):
        i = u.place
        send("core", None, half_src(u, 1 - c), half_dst(u, c), core_s.at[i], core_r.at[i], C)
        pltpu.make_async_copy(half_src(u, c), half_dst(u, c), loc.at[i]).start()

    def to_y(u, j):
        b = block(u, y, j, x * (u.rows - u.via_y), u.via_y)
        remote(b, b, y_s.at[u.place], y_r.at[u.place], Y).start()

    def own(u):
        i = u.place
        got(half_dst(u, 1 - c), core_r.at[i])
        pltpu.make_async_copy(half_src(u, c), half_dst(u, c), loc.at[i]).wait()
        zb = block(u, y, z, x * (u.rows - u.most), u.most)
        send(i, z < 3, zb, zb, up_s.at[i, z], z_r.at[i, z], UP)
        send(i, z > 0, zb, zb, dn_s.at[i, z], z_r.at[i, z], DOWN)
        to_y(u, z)

    def hop(u, k):
        i = u.place
        ways = (
            (z >= k, z - k, (z >= k) & (z < 3), UP, up_s),
            (z + k <= 3, z + k, (z + k <= 3) & (z > 0), DOWN, dn_s),
        )
        for ok, j, more, dev, sems in ways:
            zb = block(u, y, j, x * (u.rows - u.most), u.most)

            def arrive(zb=zb, j=j):
                got(zb, z_r.at[i, j])
                to_y(u, j)
                b = block(u, y, j, x * u.most, u.rows - u.most)
                remote(b, b, x_s.at[i, 0], x_r.at[i, 0], X).start()

            when(ok, arrive)
            send(i, more, zb, zb, sems.at[i, j], z_r.at[i, j], dev)

    def cross(u):
        i = u.place
        got(across(u, 1 - y, x * (u.rows - u.via_y), u.via_y), y_r.at[i])
        b = across(u, 1 - y, x * u.via_y, u.rows - u.via_y)
        send(i, None, b, b, x_s.at[i, 1], x_r.at[i, 1], X)

    def last(u):
        i = u.place
        got(three(u, (1 - x) * u.most, u.rows - u.most), x_r.at[i, 0])
        got(across(u, 1 - y, (1 - x) * u.via_y, u.rows - u.via_y), x_r.at[i, 1])
        b = across(u, y, x * (u.rows - u.via_y), u.via_y)
        remote(b, b, y_s.at[i], y_r.at[i], Y).wait_send()
        b = three(u, x * u.most, u.rows - u.most)
        remote(b, b, x_s.at[i, 0], x_r.at[i, 0], X).wait_send()
        settle(i)

    mine = c == z // 2

    def rows_out(src, dst, slot):
        for i in (0, 1):
            zd = 2 * c + i
            d = dst.at[pl.ds(al(z * 112, 16), 112)]
            send("rows", zd != z, src.at[i], d, row_s.at[slot, i], row_r.at[slot, z], {"tp": zd})
            when(
                zd == z,
                lambda i=i, d=d: pltpu.make_async_copy(src.at[i], d, loc.at[count + slot]).start(),
            )

    def rows_in(dst, slot):
        def wait():
            for j in others:
                got(dst.at[pl.ds(al(j * 112, 16), 112)], row_r.at[slot, j])
            d = dst.at[pl.ds(al(z * 112, 16), 112)]
            pltpu.make_async_copy(d, d, loc.at[count + slot]).wait()

        when(mine, wait)
        send("rows", mine, dst, dst, row_s.at[slot, 2], row_r.at[slot, 4], C)

    def rows_have(dst, slot):
        when(c != z // 2, lambda: got(dst, row_r.at[slot, 4]))

    parts = [slice(t * 96, (t + 1) * 96 if t < 15 else frames) for t in range(16)]

    def enc_local(t):
        return pltpu.make_async_copy(
            enc.at[lax.rem(z, 2), parts[t]], memory.at[parts[t]], loc.at[count + 2 + t]
        )

    def enc_send(t):
        send(
            "rows", mine, enc.at[lax.rem(z, 2), parts[t]], memory.at[parts[t]], row_s.at[2, t], row_r.at[2, t], C
        )
        when(mine, lambda: enc_local(t).start())

    def enc_have():
        for t in range(16):
            when(mine, lambda: enc_local(t).wait())
            when(c != z // 2, lambda: got(memory.at[parts[t]], row_r.at[2, t]))

    me = 2 * y + c

    def ids_out():
        for k, dev in enumerate((C, Y, YC)):
            send("ids", None, ids, idbuf.at[me], ad_s.at[k], ad_r.at[k], dev)
        idbuf[pl.ds(me, 1)] = ids[...][None]

    def adapters_pick():
        for k, s in enumerate((2 * y + 1 - c, 2 * (1 - y) + c, 2 * (1 - y) + 1 - c)):
            got(idbuf.at[s], ad_r.at[k])
        held = lax.broadcasted_iota(jnp.int32, (128, 32), 1) + me * 32
        rank = lax.rem(lax.broadcasted_iota(jnp.int32, (128, 32), 0), 16)
        lines = [
            [jnp.broadcast_to(idbuf[2 * s + k // 2, k % 2 : k % 2 + 1, :32], (16, 32)) for k in range(4)]
            for s in range(2)
        ]
        wanted = jnp.concatenate([line for pair in lines for line in pair])
        target = held.astype(f32) - rank.astype(f32)
        picks = jnp.where(wanted * 16.0 == target, 1.0, 0.0).astype(bf16)
        here = []
        for s in range(2):
            line = lines[s][0]
            for k in (1, 2, 3):
                line = jnp.where(z == k, lines[s][k], line)
            here.append(line)
        picks_z = jnp.where(jnp.concatenate(here) * 16.0 == target[:32], 1.0, 0.0).astype(bf16)
        for h in range(2):
            cols = slice(h * 128, h * 128 + 128)
            wide = slice(h * 512, h * 512 + 512)
            given = [u_ai[m][:, cols] for m in range(6)] + [u_fi[:, wide]]
            given += [d_ao[m][:, cols] for m in range(2)] + [d_fo[:, wide]]
            cs[h] = nn(picks, jnp.concatenate(given, axis=1)).astype(bf16)
            if h == 0:
                given = [d_ai[m] for m in range(5)]
            else:
                given = [d_ai[5], d_fi[...], u_ao[0], u_ao[1], u_fo[...]]
            cw[h] = nn(picks_z, jnp.concatenate(given, axis=1)).astype(bf16)
        send("pick", None, cs.at[1 - c], rs, ad_s.at[3], ad_r.at[3], C)
        send("pick", None, cw.at[1 - c], rw, ad_s.at[4], ad_r.at[4], C)

    def adapters_y():
        got(rs, ad_r.at[3])
        got(rw, ad_r.at[4])
        rs[...] += cs[pl.ds(c, 1)][0]
        rw[...] += cw[pl.ds(c, 1)][0]
        send("pick", None, rs.at[pl.ds(al((1 - y) * 64, 64), 64)], ys, ad_s.at[5], ad_r.at[5], Y)
        send("pick", None, rw.at[pl.ds(al((1 - y) * 16, 16), 16)], yw, ad_s.at[6], ad_r.at[6], Y)

    def adapters_z():
        got(ys, ad_r.at[5])
        got(yw, ad_r.at[6])
        ys[...] += rs[pl.ds(al(y * 64, 64), 64)]
        fw[pl.ds(c, 1)] = (yw[...] + rw[pl.ds(al(y * 16, 16), 16)])[None]
        for k, j in enumerate(others):
            send("pick", None, ys.at[pl.ds(al(j * 16, 16), 16)], fz.at[z], ad_s.at[7 + k], ad_r.at[7 + z], {"tp": j})
        fz[pl.ds(z, 1)] = ys[pl.ds(al(z * 16, 16), 16)][None]
        send("pick", None, fw.at[c], fw.at[c], ad_s.at[11], ad_r.at[11], C)

    def adapters_have():
        for j in others:
            got(fz.at[j], ad_r.at[7 + j])
        got(fw.at[1 - c], ad_r.at[11])
        settle("pick")
        settle("ids")

    def whole(m):
        return fw[m // 5, :, (m % 5) * 1024 : (m % 5) * 1024 + 1024]

    def split(s):
        return jnp.concatenate([fz[k, :, s * 128 : s * 128 + 128] for k in range(4)], axis=1)

    def merge(u):
        m = u.index
        if u.tall:
            down_t = whole(min(m, 6)).T
            up_rows = split(m)
            for b in range(4):
                place = slice(m * 1024 + b * 256, m * 1024 + b * 256 + 256)
                ga[place] = (ga[place].astype(f32) + nn(down_t[b * 256 : b * 256 + 256], up_rows)).astype(bf16)
        else:
            down_t = split(10 + m).T
            up_rows = whole(7 + m if m < 2 else 9)
            for k in range(4):
                gb[m, k] = (gb[m, k].astype(f32) + nn(down_t[k * 128 : k * 128 + 128], up_rows)).astype(bf16)

    def wa(m):
        return ga[m * 1024 : (m + 1) * 1024]

    def wb(m):
        return gb[m].reshape(512, 1024)

    def part_out(e, slot):
        send(("part", e), None, outbox.at[slot], inbox.at[slot], ex_s.at[e], ex_r.at[e], C)

    def part_sum(e, slot):
        got(inbox.at[slot], ex_r.at[e])
        return outbox[slot] + inbox[slot]

    def norm_rows(side, source):
        unit, _ = normalize(source)
        normed[side] = (unit * gain[side] + shift[side]).astype(bf16)

    def start_rows():
        rows_have(rows, 0)
        norm_rows(0, rows[...].astype(f32))

    def project(m, source, out, length):
        def run():
            out[:length] = nn(source(), wa(m)).astype(bf16)
        return run

    def attention(side, first, number):
        q, k, v = ((q0, k0, v0), (q1, k1, v1))[side]
        length = (rows.shape[0], frames)[side]
        return lambda: attend_forward(q, k, v, mix.at[side], lse.at[side], length, side == 0, first, number)

    def part0():
        outbox[0] = nn(mix[0], wb(0))
        part_out(0, 0)

    def second_rows():
        hidden[0] = rows[...].astype(f32) + part_sum(0, 0)
        norm_rows(1, hidden[0])

    def fill():
        for out in (k1, v1):
            out[frames:] = jnp.zeros((out.shape[0] - frames, out.shape[1]), bf16)

    def part1():
        outbox[1] = nn(mix[1], wb(1))
        part_out(1, 1)

    def third_rows():
        hidden[1] = hidden[0] + part_sum(1, 1)
        norm_rows(2, hidden[1])
        rows_have(grads, 1)

    def feed_first():
        settle(("part", 0))
        settle(("part", 1))
        r_up[0] = rank_t(whole(6), normed[2])
        r_up[1] = rank_t(whole(9), grads[...])

    def chunk(j):
        def run():
            up, down = wa(6 + j), wb(2 + j)
            pre = nn(normed[2], up)
            cdf = 0.5 * (1.0 + lax.erf(pre * (2**-0.5)))
            active = (pre * cdf).astype(bf16)
            slope = cdf + pre * jnp.exp(-0.5 * pre * pre) * 0.3989422804014327
            grad = (nt(grads[...], down) * slope).astype(bf16)
            if j == 0:
                outbox[1] = nn(active, down)
                outbox[0] = nt(grad, up)
                r_in[...] = nt(split(6 + j), grad)
                t_out[...] = nt(split(12 + j), active)
            else:
                outbox[1] += nn(active, down)
                outbox[0] += nt(grad, up)
                r_in[...] += nt(split(6 + j), grad)
                t_out[...] += nt(split(12 + j), active)
            gsplit[6 + j] = nn(r_up[0], grad).astype(bf16)
            gsplit[12 + j] = nn(r_up[1], active).astype(bf16)
        return run

    tasks = {}

    def task(tick, fn):
        tasks.setdefault(tick, []).append(fn)

    task(1, adapters_pick)
    task(3, adapters_y)
    task(5, adapters_z)
    task(7, adapters_have)
    task(7, lambda: rows_in(rows, 0))
    task(8, start_rows)
    for u in units:
        task(2 * u.place + OFFS[4], functools.partial(merge, u))
    base = OFFS[4]
    task(base + 1, project(0, lambda: normed[0], q0, 448))
    task(base + 3, project(1, lambda: normed[0], k0, 448))
    task(base + 5, project(2, lambda: normed[0], v0, 448))
    task(base + 5, attention(0, 0, 2))
    task(base + 6, attention(0, 2, 2))
    task(base + 7, part0)
    task(base + 9, second_rows)
    task(base + 9, project(3, lambda: normed[1], q1, 448))
    task(base + 10, enc_have)
    task(base + 10, fill)
    task(base + 11, project(4, lambda: memory[...], k1, 1500))
    task(base + 12, project(5, lambda: memory[...], v1, 1500))
    task(base + 13, attention(1, 0, 2))
    task(base + 14, attention(1, 2, 2))
    task(base + 15, part1)
    task(base + 17, third_rows)
    task(base + 18, feed_first)
    task(12, lambda: rows_out(cot, grads, 1))
    task(22, lambda: rows_in(grads, 1))
    for j in range(4):
        task(base + 19 + 4 * j, chunk(j))

    ids_out()
    rows_out(tok, rows, 0)
    for u in units:
        core_exchange(u)
    for t in range(max(2 * count + base, max(tasks)) + 1):
        def at(offset):
            i, odd = divmod(t - offset, 2)
            return units[i] if not odd and 0 <= i < count else None

        if at(0):
            own(at(0))
        for k in (1, 2, 3):
            if at(OFFS[k - 1]):
                hop(at(OFFS[k - 1]), k)
        if at(OFFS[3]):
            cross(at(OFFS[3]))
        if at(OFFS[4]):
            last(at(OFFS[4]))
        if t < 16:
            enc_send(t)
        for fn in tasks.get(t, []):
            fn()

    def to_hbm(src, dst, slot):
        return pltpu.make_async_copy(src, dst, loc.at[count + 18 + slot])

    part_out(3, 0)
    gwhole[6] = nn(r_in[...].astype(bf16), normed[2]).astype(bf16)
    gwhole[9] = nn(t_out[...].astype(bf16), grads[...]).astype(bf16)
    g_now[...] = grads[...].astype(f32) + norm_back(hidden[1], gain[2], part_sum(3, 0))
    part_out(2, 1)
    settle("rows")
    grads[...] = g_now[...].astype(bf16)
    do[...] = nt(grads[...], wb(1)).astype(bf16)
    dk1, dv1 = ga.at[pl.ds(6144, 1536)], ga.at[pl.ds(7680, 1536)]
    attend_backward(q1, k1, v1, do, lse.at[1], dq, dk1, dv1, frames, False)
    settle(("part", 3))
    outbox[0] = nt(dq[...], wa(3))
    normed[2] = (hidden[1] + part_sum(2, 1)).astype(bf16)
    to_hbm(normed.at[2], result, 0).start()
    part_out(4, 0)

    def ranks(side, source, dk, dv):
        for i, (u, g) in enumerate(((normed.at[side], dq), (source, dk), (source, dv))):
            m = 3 * side + i
            held = g[: u.shape[0]]
            inner = rank_t(whole(m), u[...])
            back = rank_t(split(m), held)
            gsplit[m] = nn(inner, held).astype(bf16)
            gwhole[m] = nn(back, u[...]).astype(bf16)
        gsplit[10 + side] = nn(rank_t(whole(7 + side), grads[...]), mix[side]).astype(bf16)
        gwhole[7 + side] = nn(rank_t(split(10 + side), mix[side]), grads[...]).astype(bf16)

    def memory_half(h, place):
        rows_of = [pl.ds(al(m * 1024 + h * 512, 512), 512) for m in (4, 5)]
        return nt(dk1[place], ga[rows_of[0]]) + nt(dv1[place], ga[rows_of[1]])

    thirds = [slice(b * 512, b * 512 + 512) for b in range(3)]
    for place in thirds:
        k1[place] = memory_half(1 - c, place).astype(bf16)
    ranks(1, memory, dk1, dv1)
    g_now[...] += norm_back(hidden[0], gain[1], part_sum(4, 0))
    send("memory", None, k1, v1, ex_s.at[6], ex_r.at[6], C)
    grads[...] = g_now[...].astype(bf16)
    do[...] = nt(grads[...], wb(0)).astype(bf16)
    attend_backward(q0, k0, v0, do, lse.at[0], dq, dkv.at[0], dkv.at[1], rows.shape[0], True)
    settle(("part", 2))
    outbox[1] = nt(dq[...], wa(0))
    outbox[1] += nt(dkv[0], wa(1))
    outbox[1] += nt(dkv[1], wa(2))
    part_out(5, 1)
    got(v1, ex_r.at[6])
    settle("memory")
    for place in thirds:
        k1[place] = (memory_half(c, place) + v1[place].astype(f32)).astype(bf16)
    to_hbm(k1, g_memory, 1).start()
    ranks(0, normed.at[0], dkv.at[0], dkv.at[1])
    normed[1] = (g_now[...] + norm_back(rows[...].astype(f32), gain[0], part_sum(5, 1))).astype(bf16)
    to_hbm(normed.at[1], g_rows, 2).start()
    for src, dst, slot in ((normed.at[2], result, 0), (k1, g_memory, 1), (normed.at[1], g_rows, 2)):
        to_hbm(src, dst, slot).wait()
    for key in list(sent):
        settle(key)


def layer(tok, enc, cot, w_in, w_out, w_up, w_down, ids, gain, shift, *adapters):
    any_ = pl.BlockSpec(memory_space=pl.ANY)
    r, d = 448, tok.shape[2]
    frames = enc.shape[1]
    padded = -(-frames // 512) * 512
    dma = pltpu.SemaphoreType.DMA

    def vm(*shape, dtype=bf16):
        return pltpu.VMEM(shape, dtype)

    n = 16
    return pl.pallas_call(
        layer_kernel,
        out_shape=[sds((r, d), bf16), sds((r, d), bf16), sds((padded, d // 2), bf16), sds((16, 16, 512), bf16), sds((10, 16, d), bf16)],
        in_specs=[any_] * 7 + [VM] * 11,
        out_specs=[any_] * 3 + [VM] * 2,
        scratch_shapes=[
            vm(10 * d, 512), vm(6, 4, 128, d), vm(r, d), vm(r, d), vm(frames, d), vm(3, r, d),
            vm(r, 512), vm(r, 512), vm(r, 512), vm(2, r, 512), vm(r, 512), vm(padded, 512), vm(padded, 512),
            vm(2, 4, 2, r, dtype=f32), vm(2, r, d, dtype=f32), vm(r, d, dtype=f32), vm(r, 512), vm(r, 512), vm(2, r, 512),
            vm(2, r, d, dtype=f32), vm(2, r, d, dtype=f32),
            vm(4, 8, 128, dtype=f32), vm(2, 128, 2048), vm(2, 32, 5120), vm(128, 2048), vm(32, 5120), vm(64, 2048), vm(16, 5120),
            vm(4, 16, 2048), vm(2, 16, 5120), vm(16, r, dtype=f32), vm(16, r, dtype=f32), vm(2, 16, r),
            dma((n,)), dma((n,)), dma((n, 4)), dma((n, 4)), dma((n, 4)), dma((n,)), dma((n,)), dma((n, 2)), dma((n, 2)),
            dma((3, 16)), dma((3, 16)), dma((n + 21,)), dma((12,)), dma((12,)), dma((7,)), dma((7,)),
        ],
        compiler_params=pltpu.CompilerParams(
            collective_id=1, has_side_effects=True, vmem_limit_bytes=61 * 1024 * 1024
        ),
        name="layer",
    )(tok, enc, cot, w_in, w_out, w_up, w_down, ids, gain, shift, *adapters)


def swap_core(rows):
    return lax.ppermute(rows, "core", SWAP)


def core_sum(part):
    return part + swap_core(part)


def own_and_other(stacked):
    core = lax.axis_index("core")
    keep = lax.dynamic_index_in_dim(stacked, core, 0, keepdims=False)
    send = lax.dynamic_index_in_dim(stacked, 1 - core, 0, keepdims=False)
    return keep, swap_core(send)


def in_core_order(own, other):
    first = lax.axis_index("core") == 0
    return jnp.stack([jnp.where(first, own, other), jnp.where(first, other, own)])


def scatter_sh(stacked):
    n = lax.axis_size("sh")
    if n == 2:
        me = lax.axis_index("sh")
        keep = lax.dynamic_index_in_dim(stacked, me, 0, keepdims=False)
        send = lax.dynamic_index_in_dim(stacked, 1 - me, 0, keepdims=False)
        return keep + lax.ppermute(send, "sh", SWAP)
    return lax.psum_scatter(stacked, "sh", scatter_dimension=0, tiled=False)


def over_z(stacked):
    return lax.all_to_all(stacked, "tp", 0, 0, tiled=True)


def half_columns(rows):
    width = rows.shape[-1] // 2
    return lax.dynamic_slice_in_dim(rows, lax.axis_index("core") * width, width, rows.ndim - 1)


def rows_home(half):
    tp = lax.axis_size("tp")
    moved = over_z(half.reshape(tp, half.shape[0] // tp, half.shape[1]))
    own, other = own_and_other(moved.reshape(2, tp // 2, *moved.shape[1:]))
    both = in_core_order(own, other)
    return jnp.moveaxis(both, 0, 2).reshape(both.shape[1], both.shape[2], 2 * half.shape[1])


def rows_here(rows):
    tp = lax.axis_size("tp")
    both = in_core_order(rows, swap_core(rows)).reshape(4, *rows.shape[1:])
    moved = over_z(half_columns(both))
    moved = moved.reshape(tp * rows.shape[1], rows.shape[2] // 2)
    pair = in_core_order(moved, swap_core(moved))
    return jnp.concatenate([pair[0], pair[1]], axis=-1)


def gather_weights(w_attn_in, w_attn_out, w_up, w_down):
    def over_shard(block, axis):
        return lax.all_gather(block, ("sh", "core"), axis=axis, tiled=True)

    def over_tp(block, axis):
        return lax.all_gather(block, "tp", axis=axis, tiled=True)

    core = lax.axis_index("core")

    def half(block, axis):
        width = block.shape[axis] // 2
        return lax.dynamic_slice_in_dim(block, core * width, width, axis)

    w_in = over_tp(half(over_shard(w_attn_in.reshape(6, *w_attn_in.shape[3:]), 1), 2), 2)
    w_out = over_tp(half(over_shard(w_attn_out[0], 2), 1), 1)
    w_first = over_tp(half(over_shard(w_up[0], 0), 1), 1)
    w_second = over_tp(half(over_shard(w_down[0], 1), 0), 0)
    return w_in, w_out, w_first, w_second


def wide_parts(args):
    (
        tokens, encoded, cotangent, adapter_of, w_attn_in, w_attn_out, w_up, w_down, norm_gain, norm_shift,
        down_attn_in, up_attn_in, down_feed_in, up_feed_in, down_attn_out, up_attn_out, down_feed_out, up_feed_out,
    ) = args
    n, tp = lax.axis_size("sh"), lax.axis_size("tp")
    sh, core, z = lax.axis_index("sh"), lax.axis_index("core"), lax.axis_index("tp")
    width = w_attn_in.shape[3] * 2 * n
    held_rows = down_feed_in.shape[1]
    quarter = width // tp
    piece = quarter // 2

    ids = lax.all_gather(adapter_of, ("sh", "core"), tiled=True)

    row_ids = (sh * 2 + core) * held_rows + jnp.arange(held_rows)
    wanted = ids.reshape(n, tp)[:, :, None] * RANK + jnp.arange(RANK)
    picks = (wanted[..., None] == row_ids).astype(bf16)
    whole = jnp.concatenate(
        [
            down_attn_in.reshape(6, held_rows, width),
            down_feed_in,
            up_attn_out[0],
            up_feed_out,
        ]
    )
    def in_quarters(rows):
        return jnp.moveaxis(rows.reshape(held_rows, tp, quarter), 1, 0)

    split = jnp.concatenate(
        [
            up_attn_in.reshape(6, held_rows, quarter),
            in_quarters(up_feed_in[0]),
            down_attn_out[0],
            in_quarters(down_feed_out[0]),
        ]
    )
    picks_z = lax.dynamic_index_in_dim(picks, z, 1, keepdims=False)
    chosen_whole = jnp.einsum("srk,mkd->smrd", picks_z, whole, preferred_element_type=f32).astype(bf16)
    chosen_split = jnp.einsum("szrk,mkd->szmrd", picks, split, preferred_element_type=f32).astype(bf16)
    chosen_whole = core_sum(scatter_sh(chosen_whole))
    chosen_split = over_z(core_sum(scatter_sh(chosen_split)))

    def columns(first, count):
        mine = half_columns(chosen_split[:, first : first + count])
        return jnp.moveaxis(mine, 0, 2).reshape(count, RANK, tp * piece)

    def wide_columns(first):
        mine = lax.dynamic_slice_in_dim(chosen_split[:, first : first + tp], core * 2, 2, 1)
        return jnp.moveaxis(mine, 2, 0).reshape(RANK, tp * 2 * quarter)

    a_in, a_up, b_out, b_down = chosen_whole[:6], chosen_whole[6], chosen_whole[7:9], chosen_whole[9]
    b_in, b_up, a_out, a_down = columns(0, 6), wide_columns(6), columns(6 + tp, 2), wide_columns(8 + tp)

    w_in, w_out, w_first, w_second = gather_weights(w_attn_in, w_attn_out, w_up, w_down)
    taken = rows_here(tokens)
    upstream = rows_here(cotangent)
    mine = lax.dynamic_index_in_dim(encoded, z % 2, 0, keepdims=False)
    memory = jnp.where(core == z // 2, mine, swap_core(mine))

    def merge(weight, down_rows, up_rows):
        return (weight.astype(f32) + t_mm(down_rows, up_rows)).astype(bf16)

    w_in = [merge(w_in[i], a_in[i], b_in[i]) for i in range(6)]
    w_out = [merge(w_out[i], a_out[i], b_out[i]) for i in range(2)]
    w_first = merge(w_first, a_up, b_up)
    w_second = merge(w_second, a_down, b_down)

    gain, shift = norm_gain[0][:, None], norm_shift[0][:, None]
    frames = memory.shape[0]
    w_in = jnp.stack(w_in)
    normed0, q0, k0, v0, lse0, mix0, part = self_forward(taken, gain[0], shift[0], w_in[:3], w_out[0])
    k1, v1 = memory_project(memory, w_in[4:])
    hidden1, normed1, q1, lse1, mix1, part1 = cross_forward(
        taken, part, swap_core(part), gain[1], shift[1], w_in[3], k1, v1, w_out[1], frames
    )
    hidden2, part2, back, g_aup, g_bup, g_adown, g_bdown = feed(
        hidden1, part1, swap_core(part1), gain[2], shift[2], w_first, w_second, upstream, a_up, b_up, a_down, b_down
    )
    result = (hidden2 + core_sum(part2)).astype(bf16)
    grad, e1, dq1, dk1, dv1, back1 = cross_backward(
        hidden2, gain[2], upstream, back, swap_core(back), w_out[1], w_in[3], q1, k1, v1, lse1, frames
    )
    part = memory_backward(dk1, dv1, w_in[4:], frames)
    own, other = own_and_other(jnp.moveaxis(part.reshape(part.shape[0], 2, -1), 1, 0))
    memory_rows = (own.astype(f32) + other.astype(f32)).astype(bf16)
    grad, e0, dq0, dk0, dv0, back0 = self_backward(
        hidden1, gain[1], grad, back1, swap_core(back1), w_out[0], w_in[:3], q0, k0, v0, lse0
    )
    grad = final_norm(taken, gain[0], grad, back0, swap_core(back0))
    ranks1 = attention_ranks(normed1, memory, mix1, dq1, dk1, dv1, e1, a_in[3:], b_in[3:], a_out[1], b_out[1])
    ranks0 = attention_ranks(normed0, None, mix0, dq0, dk0, dv0, e0, a_in[:3], b_in[:3], a_out[0], b_out[0])
    feed_up = jnp.moveaxis(g_bup.reshape(RANK, tp, tp, piece), 2, 0).reshape(tp, RANK, tp * piece)
    feed_down = jnp.moveaxis(g_adown.reshape(RANK, tp, tp, piece), 2, 0).reshape(tp, RANK, tp * piece)
    out_split = jnp.stack([ranks0[2], ranks1[2]])
    out_whole = jnp.stack([ranks0[3], ranks1[3]])
    split_grads = jnp.concatenate([ranks0[1], ranks1[1], feed_up.astype(bf16), out_split, feed_down.astype(bf16)])
    whole_grads = jnp.concatenate(
        [ranks0[0], ranks1[0], g_aup.astype(bf16)[None], out_whole, g_bdown.astype(bf16)[None]]
    )
    here = ids.reshape(n, tp)[sh]
    return result, grad, memory_rows, split_grads, whole_grads, here


def narrow_parts(args):
    (
        tokens, encoded, cotangent, adapter_of, w_attn_in, w_attn_out, w_up, w_down, norm_gain, norm_shift,
        down_attn_in, up_attn_in, down_feed_in, up_feed_in, down_attn_out, up_attn_out, down_feed_out, up_feed_out,
    ) = args

    def six(rows):
        return rows.reshape(6, *rows.shape[3:])

    lines = jnp.pad(adapter_of.astype(f32), (0, 6))[:, None] * jnp.ones((1, 128), f32)
    outs = layer(
        tokens, encoded, cotangent, six(w_attn_in), w_attn_out[0], w_up[0], w_down[0], lines,
        norm_gain[0][:, None], norm_shift[0][:, None], six(down_attn_in), six(up_attn_in), down_feed_in[0],
        up_feed_in[0], down_attn_out[0], up_attn_out[0], down_feed_out[0], up_feed_out[0],
    )
    here = in_core_order(adapter_of, swap_core(adapter_of)).reshape(4)
    return (*outs[:2], outs[2][: encoded.shape[1]], *outs[3:], here)


def on_device(*args):
    n, tp = lax.axis_size("sh"), lax.axis_size("tp")
    held_rows, quarter = args[12].shape[1], args[11].shape[4]
    width, piece = quarter * tp, quarter // 2
    result, grad, memory_rows, split_grads, whole_grads, here = (narrow_parts if n == 2 else wide_parts)(args)
    activations = rows_home(half_columns(result))
    grad_encoded = rows_home(memory_rows).astype(f32)
    grad_tokens = rows_home(half_columns(grad)).astype(f32)
    compact = jnp.moveaxis(split_grads.reshape(-1, RANK, tp, piece), 2, 0)
    own, other = own_and_other(jnp.moveaxis(whole_grads.reshape(-1, RANK, tp, 2, piece), (3, 2), (0, 1)))
    compact = jnp.concatenate([compact, own + other], axis=1)
    compact = over_z(compact)
    rows = jnp.arange(2 * n * held_rows)
    place = (here[:, None] * RANK + jnp.arange(RANK))[None] == rows[:, None, None]
    dense = jnp.einsum("gkr,kmrp->gmp", place.astype(bf16), compact, preferred_element_type=f32)
    dense = dense.astype(bf16).reshape(n, 2, held_rows, *dense.shape[1:])
    dense = scatter_sh(dense)
    dense = dense + lax.ppermute(dense, "rep", SWAP)
    both = in_core_order(*own_and_other(dense))
    done = jnp.moveaxis(both, 0, 2)
    count = 8 + 2 * tp
    sums = done[:, :count].astype(f32)

    def narrow(first, number):
        block = sums[:, first : first + number].reshape(held_rows, number, quarter)
        return jnp.moveaxis(block, 1, 0)

    def wide_of(first):
        block = jnp.moveaxis(sums[:, first : first + tp], 2, 1)
        return block.reshape(held_rows, 2 * tp * piece)

    grad_up_attn_in = narrow(0, 6).reshape(1, 2, 3, held_rows, quarter)
    grad_up_feed_in = wide_of(6)[None]
    grad_down_attn_out = narrow(6 + tp, 2)[None]
    grad_down_feed_out = wide_of(8 + tp)[None]
    rest = done[:, count:].reshape(tp, held_rows // tp, 10, quarter)
    rest = jnp.moveaxis(over_z(rest), 0, 2)
    rest = jnp.moveaxis(rest.reshape(held_rows // tp, 10, width), 1, 0).astype(f32)
    return (
        activations,
        grad_tokens,
        grad_encoded,
        rest[:6].reshape(1, 2, 3, held_rows // tp, width),
        grad_up_attn_in,
        rest[6:7],
        grad_up_feed_in,
        grad_down_attn_out,
        rest[7:9][None],
        grad_down_feed_out,
        rest[9:10],
    )


def solution(mesh):
    rep, shard, tp = (mesh.shape[name] for name in ("rep", "shard", "tp"))
    fine = Mesh(mesh.devices.reshape(rep, shard // 2, 2, tp), ("rep", "sh", "core", "tp"))
    shard = ("sh", "core")
    clips = ("rep", "sh", "core")
    both = ("sh", "core", "tp")
    placed = (
        P(clips, "tp", None),
        P(clips, None, None),
        P(clips, "tp", None),
        P(clips),
        P(None, None, None, shard, "tp"),
        P(None, None, "tp", shard),
        P(None, shard, "tp"),
        P(None, "tp", shard),
        P(),
        P(),
        P(None, None, None, shard, None),
        P(None, None, None, shard, "tp"),
        P(None, shard, None),
        P(None, shard, "tp"),
        P(None, None, shard, "tp"),
        P(None, None, shard, None),
        P(None, shard, "tp"),
        P(None, shard, None),
    )
    return jax.shard_map(
        on_device,
        mesh=fine,
        in_specs=placed,
        out_specs=(
            P(clips, "tp", None),
            P(clips, "tp", None),
            P(clips, "tp", None),
            P(None, None, None, both, None),
            P(None, None, None, shard, "tp"),
            P(None, both, None),
            P(None, shard, "tp"),
            P(None, None, shard, "tp"),
            P(None, None, both, None),
            P(None, shard, "tp"),
            P(None, both, None),
        ),
        check_vma=False,
    )
```

```python
import functools

import jax
import jax.numpy as jnp
from jax import lax
from jax.experimental import pallas as pl
from jax.experimental.pallas import tpu as pltpu
from jax.sharding import Mesh, PartitionSpec as P

HD = 64
RANK = 16
epsilon = 1e-05
masked_score = -1e30
f32, bf16 = jnp.float32, jnp.bfloat16
SWAP = ((0, 1), (1, 0))
MESH = pl.DeviceIdType.MESH


def dot(a, b, dims):
    return lax.dot_general(a, b, (dims, ((), ())), preferred_element_type=f32)


def mm(a, b):
    return dot(a, b, ((1,), (0,)))


def mm_t(a, b):
    return dot(a, b, ((1,), (1,)))


def t_mm(a, b):
    return dot(a, b, ((0,), (0,)))


HIDE = -1e30
SCALE = HD**-0.5
EPS = 1e-05
VM = pl.BlockSpec(memory_space=pltpu.VMEM)


def nn(a, b):
    return lax.dot_general(a, b, (((1,), (0,)), ((), ())), preferred_element_type=f32)


def nt(a, b):
    return lax.dot_general(a, b, (((1,), (1,)), ((), ())), preferred_element_type=f32)


def normalize(rows):
    centered = rows - jnp.mean(rows, axis=-1, keepdims=True)
    variance = jnp.mean(centered * centered, axis=-1, keepdims=True)
    inverse = lax.rsqrt(variance + EPS)
    return centered * inverse, inverse


def norm_back(rows, gain, grad):
    unit, inverse = normalize(rows)
    scaled = grad * gain
    first = jnp.mean(scaled, axis=-1, keepdims=True)
    second = jnp.mean(scaled * unit, axis=-1, keepdims=True)
    return (scaled - first - unit * second) * inverse


def pair_lanes(p):
    return pl.ds(pl.multiple_of(p * 128, 128), 128)


def scores_t(keys, queries, frames, causal, groups=1):
    s = nt(keys, queries) * SCALE
    if causal:
        key = lax.broadcasted_iota(jnp.int32, s.shape, 0)
        query = lax.broadcasted_iota(jnp.int32, s.shape, 1)
        s = jnp.where(query >= key, s, HIDE)
    elif frames < s.shape[0]:
        step, used = s.shape[0] // groups, frames // groups
        kept = used // 16 * 16
        key = kept + lax.broadcasted_iota(jnp.int32, (step - kept, s.shape[1]), 0)
        blocks = [s[g * step : (g + 1) * step] for g in range(groups)]
        s = jnp.concatenate([part for b in blocks for part in (b[:kept], jnp.where(key < used, b[kept:], HIDE))])
    return s


def attend_forward(q, k, v, mix, lse, frames, causal, start=0, number=None, groups=1):
    def pair(p, carry):
        lanes = pair_lanes(p)
        qp, kp = q[:, lanes], k[:, lanes]
        vt = v[:, lanes].T
        first = lax.broadcasted_iota(jnp.int32, qp.shape, 1) < HD
        outs, logs = [], []
        for h in (0, 1):
            s = scores_t(kp, jnp.where(first == (h == 0), qp, 0), frames, causal, groups)
            top = jnp.max(s, axis=0, keepdims=True)
            e = jnp.exp(s - top)
            total = jnp.sum(e, axis=0, keepdims=True)
            probs = (e * (1.0 / total)).astype(bf16)
            outs.append(nn(vt, probs)[h * HD : (h + 1) * HD])
            logs.append(top + jnp.log(total))
        mix[:, lanes] = jnp.concatenate(outs).T.astype(bf16)
        lse[p] = jnp.concatenate(logs)
        return carry

    lax.fori_loop(start, start + (number or q.shape[1] // 128), pair, 0)


def attend_backward(q, k, v, do, lse, dq, dk, dv, frames, causal, start=0, number=None, groups=1):
    def pair(p, carry):
        lanes = pair_lanes(p)
        qp, kp, vp, dop = q[:, lanes], k[:, lanes], v[:, lanes], do[:, lanes]
        kt = kp.T
        logs = lse[p]
        first = lax.broadcasted_iota(jnp.int32, qp.shape, 1) < HD
        dqs, dks, dvs = [], [], []
        for h in (0, 1):
            mine = first == (h == 0)
            s = scores_t(kp, jnp.where(mine, qp, 0), frames, causal, groups)
            probs = jnp.exp(s - logs[h : h + 1])
            dvs.append(nn(probs.astype(bf16), dop))
            dp = nt(vp, jnp.where(mine, dop, 0))
            t = probs * dp
            ds = (t - probs * jnp.sum(t, axis=0, keepdims=True)).astype(bf16)
            dks.append(nn(ds, qp))
            dqs.append(nn(kt, ds)[h * HD : (h + 1) * HD])
        first_k = lax.broadcasted_iota(jnp.int32, kp.shape, 1) < HD
        dv[:, lanes] = jnp.where(first_k, dvs[0], dvs[1]).astype(bf16)
        dk[:, lanes] = (jnp.where(first_k, dks[0], dks[1]) * SCALE).astype(bf16)
        dq[:, lanes] = (jnp.concatenate(dqs).T * SCALE).astype(bf16)
        return carry

    lax.fori_loop(start, start + (number or q.shape[1] // 128), pair, 0)


def params():
    return pltpu.CompilerParams(vmem_limit_bytes=60 * 1024 * 1024)


def sds(shape, dtype):
    return jax.ShapeDtypeStruct(shape, dtype)


def self_forward(tok, gain, shift, wi, wo):
    def kernel(tok, gain, shift, wi, wo, normed, q, k, v, lse, mix, part):
        unit, _ = normalize(tok[...].astype(f32))
        normed[...] = (unit * gain[...] + shift[...]).astype(bf16)
        for i, out in enumerate((q, k, v)):
            out[...] = nn(normed[...], wi[i]).astype(bf16)
        attend_forward(q, k, v, mix, lse, tok.shape[0], True)
        part[...] = nn(mix[...], wo[...])

    r, d = tok.shape
    w = wi.shape[2]
    return pl.pallas_call(kernel, out_shape=[sds((r, d), bf16)] + [sds((r, w), bf16)] * 3 + [sds((w // 128, 2, r), f32), sds((r, w), bf16), sds((r, d), f32)],
        in_specs=[VM] * 5, out_specs=[VM] * 7, compiler_params=params(), name="self_forward")(tok, gain, shift, wi, wo)


def memory_project(enc, wi):
    def kernel(enc, wi, k, v):
        frames = enc.shape[0]
        for i, out in enumerate((k, v)):
            out[:frames] = nn(enc[...], wi[i]).astype(bf16)
            out[frames:] = jnp.zeros((out.shape[0] - frames, out.shape[1]), bf16)
    frames = -(-enc.shape[0] // 128) * 128
    return pl.pallas_call(kernel, out_shape=[sds((frames, wi.shape[2]), bf16)] * 2, in_specs=[VM] * 2, out_specs=[VM] * 2, compiler_params=params(), name="memory_project")(enc, wi)


def cross_forward(hid, part, other, gain, shift, wq, k, v, wo, frames):
    def kernel(hid, part, other, gain, shift, wq, k, v, wo, hidden, normed, q, lse, mix, out):
        hidden[...] = hid[...].astype(f32) + part[...] + other[...]
        unit, _ = normalize(hidden[...])
        normed[...] = (unit * gain[...] + shift[...]).astype(bf16)
        q[...] = nn(normed[...], wq[...]).astype(bf16)
        attend_forward(q, k, v, mix, lse, frames, False)
        out[...] = nn(mix[...], wo[...])

    r, d = hid.shape
    w = wq.shape[1]
    return pl.pallas_call(kernel, out_shape=[sds((r, d), f32), sds((r, d), bf16), sds((r, w), bf16), sds((w // 128, 2, r), f32), sds((r, w), bf16), sds((r, d), f32)],
        in_specs=[VM] * 9, out_specs=[VM] * 6, compiler_params=params(), name="cross_forward")(hid, part, other, gain, shift, wq, k, v, wo)


def rank_t(rows16, inputs):
    return nt(rows16, inputs).astype(bf16)


def feed(hid, part, other, gain, shift, up, down, e, a_up, b_up, a_down, b_down):
    CH = 512

    def kernel(hid, part, other, gain, shift, up, down, e, a_up, b_up, a_down, b_down, hidden, out, back, g_aup, g_bup, g_adown, g_bdown, normed):
        hidden[...] = hid[...] + part[...] + other[...]
        unit, _ = normalize(hidden[...])
        normed[...] = (unit * gain[...] + shift[...]).astype(bf16)
        t_in = rank_t(a_up[...], normed[...])
        r_out = rank_t(b_down[...], e[...])
        r_in = jnp.zeros((16, hid.shape[0]), f32)
        t_out = jnp.zeros((16, hid.shape[0]), f32)
        for j in range(up.shape[1] // CH):
            cols = slice(j * CH, (j + 1) * CH)
            pre = nn(normed[...], up[:, cols])
            cdf = 0.5 * (1.0 + lax.erf(pre * (2**-0.5)))
            active = (pre * cdf).astype(bf16)
            slope = cdf + pre * jnp.exp(-0.5 * pre * pre) * 0.3989422804014327
            grad = (nt(e[...], down[cols]) * slope).astype(bf16)
            term, term_b = nn(active, down[cols]), nt(grad, up[:, cols])
            if j == 0:
                out[...], back[...] = term, term_b
            else:
                out[...] += term
                back[...] += term_b
            g_bup[:, cols] = nn(t_in, grad)
            g_adown[:, cols] = nn(r_out, active)
            r_in += nt(b_up[:, cols], grad)
            t_out += nt(a_down[:, cols], active)
        g_aup[...] = nn(r_in.astype(bf16), normed[...])
        g_bdown[...] = nn(t_out.astype(bf16), e[...])

    r, d = hid.shape
    w = up.shape[1]
    return pl.pallas_call(kernel, out_shape=[sds((r, d), f32)] * 3 + [sds((16, d), f32), sds((16, w), f32), sds((16, w), f32), sds((16, d), f32)],
        in_specs=[VM] * 12, out_specs=[VM] * 7, scratch_shapes=[pltpu.VMEM((r, d), bf16)], compiler_params=params(), name="feed")(
            hid, part, other, gain, shift, up, down, e, a_up, b_up, a_down, b_down)


def cross_backward(hid3, gain3, g, part, other, wo, wq, q, k, v, lse, frames):
    def kernel(hid3, gain3, g, part, other, wo, wq, q, k, v, lse, g_out, e, dq, dk, dv, back, do):
        g_out[...] = g[...].astype(f32) + norm_back(hid3[...], gain3[...], part[...] + other[...])
        e[...] = g_out[...].astype(bf16)
        do[...] = nt(e[...], wo[...]).astype(bf16)
        attend_backward(q, k, v, do, lse, dq, dk, dv, frames, False)
        back[...] = nt(dq[...], wq[...])

    r, d = hid3.shape
    w, f = q.shape[1], k.shape[0]
    return pl.pallas_call(kernel, out_shape=[sds((r, d), f32), sds((r, d), bf16), sds((r, w), bf16), sds((f, w), bf16), sds((f, w), bf16), sds((r, d), f32)],
        in_specs=[VM] * 11, out_specs=[VM] * 6, scratch_shapes=[pltpu.VMEM((r, w), bf16)], compiler_params=params(), name="cross_backward")(
            hid3, gain3, g, part, other, wo, wq, q, k, v, lse)


def self_backward(hid2, gain2, g, part, other, wo, wi, q, k, v, lse):
    def kernel(hid2, gain2, g, part, other, wo, wi, q, k, v, lse, g_out, e, dq, dk, dv, back, do):
        g_out[...] = g[...] + norm_back(hid2[...], gain2[...], part[...] + other[...])
        e[...] = g_out[...].astype(bf16)
        do[...] = nt(e[...], wo[...]).astype(bf16)
        attend_backward(q, k, v, do, lse, dq, dk, dv, q.shape[0], True)
        back[...] = nt(dq[...], wi[0])
        back[...] += nt(dk[...], wi[1])
        back[...] += nt(dv[...], wi[2])

    r, d = hid2.shape
    w = q.shape[1]
    return pl.pallas_call(kernel, out_shape=[sds((r, d), f32), sds((r, d), bf16)] + [sds((r, w), bf16)] * 3 + [sds((r, d), f32)],
        in_specs=[VM] * 11, out_specs=[VM] * 6, scratch_shapes=[pltpu.VMEM((r, w), bf16)], compiler_params=params(), name="self_backward")(
            hid2, gain2, g, part, other, wo, wi, q, k, v, lse)


def final_norm(hid, gain, g, part, other):
    def kernel(hid, gain, g, part, other, out):
        out[...] = (g[...] + norm_back(hid[...].astype(f32), gain[...], part[...] + other[...])).astype(bf16)

    return pl.pallas_call(kernel, out_shape=sds(hid.shape, bf16), in_specs=[VM] * 5, out_specs=VM, compiler_params=params(), name="final_norm")(hid, gain, g, part, other)


def memory_backward(dk, dv, wi, frames):
    def kernel(dk, dv, wi, out):
        out[...] = (nt(dk[:frames], wi[0]) + nt(dv[:frames], wi[1])).astype(bf16)
    d = wi.shape[1]
    return pl.pallas_call(kernel, out_shape=sds((frames, d), bf16), in_specs=[VM] * 3, out_specs=VM, compiler_params=params(), name="memory_backward")(dk, dv, wi)


def attention_ranks(normed, source, mix, dq, dk, dv, e, a_in, b_in, a_out, b_out):
    def kernel(*refs):
        operands, results = refs[:-4], refs[-4:]
        given = operands[:7] if source is not None else operands[:1] + operands[:1] + operands[1:6]
        normed, source_, mix, dq, dk, dv, e = given
        a_in, b_in, a_out, b_out = operands[-4:]
        ga_in, gb_in, ga_out, gb_out = results
        for i, (u, g) in enumerate(((normed, dq), (source_, dk), (source_, dv))):
            rows = u.shape[0]
            inner = rank_t(a_in[i], u[...])
            back = rank_t(b_in[i], g[:rows])
            gb_in[i] = nn(inner, g[:rows]).astype(bf16)
            ga_in[i] = nn(back, u[...]).astype(bf16)
        ga_out[...] = nn(rank_t(b_out[...], e[...]), mix[...]).astype(bf16)
        gb_out[...] = nn(rank_t(a_out[...], mix[...]), e[...]).astype(bf16)

    args = [normed] + ([source] if source is not None else []) + [mix, dq, dk, dv, e, a_in, b_in, a_out, b_out]
    return pl.pallas_call(kernel, out_shape=[sds(t.shape, bf16) for t in (a_in, b_in, a_out, b_out)],
        in_specs=[VM] * len(args), out_specs=[VM] * 4, compiler_params=params(), name="attention_ranks")(*args)


OFFS = (2, 3, 4, 6, 8)


class Unit:
    def __init__(self, place, kind, index):
        self.place, self.tall, self.index = place, kind == "a", index
        self.rows = 512 if self.tall else 128
        late = place >= 10
        if self.tall:
            self.most, self.via_y = (496, 400) if late else (400, 304)
        else:
            self.most, self.via_y = (112, 96) if late else (96, 80)


def make_units():
    order = [("a", 0), ("a", 1), ("a", 2), ("b", 0), ("a", 3), ("a", 4), ("a", 5), ("b", 1)]
    for j in range(4):
        order += [("a", 6 + j), ("b", 2 + j)]
    return [Unit(i, kind, index) for i, (kind, index) in enumerate(order)]


def layer_kernel(
    tok, enc, cot, w_in, w_out, w_up, w_down, ids, gain, shift,
    d_ai, u_ai, d_fi, u_fi, d_ao, u_ao, d_fo, u_fo,
    acts, g_tok, g_enc, split_sum, whole_sum,
    ga, gb, rows, grads, memory, normed, q0, k0, v0, mix, q1, k1, v1, lse, hidden, g_now, dd, dkv,
    outbox, inbox, idbuf, rs, rw, ys, yw, ys_own, yw_own, fz, fw, r_in, t_out, r_up, gsplit, gwhole, wz,
    rwb0, rwb1, rwb2, czs0, czs1, czs2, czw0, czw1, czw2, sb0, sb1, sb2, yb0, yb1, yb2, xb0, xb1, xb2, cb0, cb1, cb2,
    core_s, core_r, up_s, dn_s, z_r, y_s, y_r, x_s, x_r, row_s, row_r, loc, ad_s, ad_r, ex_s, ex_r, b_s, b_r, home_s, home_r,
):
    units = make_units()
    count = len(units)
    frames, groups = 1500 * enc.shape[1] // 1536, 4
    do, dq = dd.at[0], dd.at[1]
    x, y, c, z = (lax.axis_index(a) for a in ("rep", "sh", "core", "tp"))
    al = pl.multiple_of
    sent = {}

    def when(cond, fn):
        fn() if cond is None else pl.when(cond)(fn)

    def remote(src, dst, s, r, dev):
        return pltpu.make_async_remote_copy(
            src_ref=src, dst_ref=dst, send_sem=s, recv_sem=r, device_id=dev, device_id_type=MESH
        )

    def send(key, cond, src, dst, s, r, dev):
        when(cond, lambda: remote(src, dst, s, r, dev).start())
        sent.setdefault(key, []).append((cond, lambda: remote(src, dst, s, r, dev).wait_send()))

    def settle(key):
        for cond, fn in sent.pop(key, []):
            when(cond, fn)

    X, Y, C = {"rep": 1 - x}, {"sh": 1 - y}, {"core": 1 - c}
    YC = {"sh": 1 - y, "core": 1 - c}
    UP, DOWN = {"tp": z + 1}, {"tp": z - 1}
    others = [lax.rem(z + k, 4) for k in (1, 2, 3)]

    def got(dst, r):
        remote(dst, dst, r, r, X).wait_recv()

    bar = pltpu.get_barrier_semaphore()
    for dev in [X, Y, C, YC] + [{"tp": j} for j in others] + [{"tp": j, "core": 1 - c} for j in others]:
        pl.semaphore_signal(bar, inc=1, device_id=dev, device_id_type=MESH)
    pl.semaphore_wait(bar, 10)

    def block(u, yy, zz, first, size):
        if u.tall:
            return ga.at[pl.ds(al(u.index * 1024 + yy * 512 + first, 16), size), pl.ds(al(zz * 128, 128), 128)]
        return gb.at[u.index, zz, pl.ds(al(first, 16), size), pl.ds(al(yy * 512, 512), 512)]

    def across(u, yy, first, size):
        if u.tall:
            return ga.at[pl.ds(al(u.index * 1024 + yy * 512 + first, 16), size)]
        return gb.at[u.index, :, pl.ds(al(first, 16), size), pl.ds(al(yy * 512, 512), 512)]

    def three(u, first, size):
        if u.tall:
            return ga.at[pl.ds(al(u.index * 1024 + y * 512 + first, 16), size), 0:384]
        return gb.at[u.index, 0:3, pl.ds(al(first, 16), size), pl.ds(al(y * 512, 512), 512)]

    def half_src(u, cc):
        m = u.index
        if u.tall:
            if m < 6:
                return w_in.at[m, :, pl.ds(al(cc * 128, 128), 128)]
            return w_up.at[:, pl.ds(al(cc * 512 + (m - 6) * 128, 128), 128)]
        if m < 2:
            return w_out.at[m, pl.ds(al(cc * 128, 128), 128)]
        return w_down.at[pl.ds(al(cc * 512 + (m - 2) * 128, 128), 128)]

    def half_dst(u, cc):
        if u.tall:
            return block(u, y, z, cc * 256, 256)
        return gb.at[u.index, z, :, pl.ds(al(y * 512 + cc * 256, 256), 256)]

    def core_exchange(u):
        i = u.place
        send("core", None, half_src(u, 1 - c), half_dst(u, c), core_s.at[i], core_r.at[i], C)
        pltpu.make_async_copy(half_src(u, c), half_dst(u, c), loc.at[i]).start()

    def to_y(u, j):
        b = block(u, y, j, x * (u.rows - u.via_y), u.via_y)
        remote(b, b, y_s.at[u.place], y_r.at[u.place], Y).start()

    def own(u):
        i = u.place
        got(half_dst(u, 1 - c), core_r.at[i])
        pltpu.make_async_copy(half_src(u, c), half_dst(u, c), loc.at[i]).wait()
        zb = block(u, y, z, x * (u.rows - u.most), u.most)
        send(i, z < 3, zb, zb, up_s.at[i, z], z_r.at[i, z], UP)
        send(i, z > 0, zb, zb, dn_s.at[i, z], z_r.at[i, z], DOWN)
        to_y(u, z)

    def hop(u, k):
        i = u.place
        ways = (
            (z >= k, z - k, (z >= k) & (z < 3), UP, up_s),
            (z + k <= 3, z + k, (z + k <= 3) & (z > 0), DOWN, dn_s),
        )
        for ok, j, more, dev, sems in ways:
            zb = block(u, y, j, x * (u.rows - u.most), u.most)

            def arrive(zb=zb, j=j):
                got(zb, z_r.at[i, j])
                to_y(u, j)
                b = block(u, y, j, x * u.most, u.rows - u.most)
                remote(b, b, x_s.at[i, 0], x_r.at[i, 0], X).start()

            when(ok, arrive)
            send(i, more, zb, zb, sems.at[i, j], z_r.at[i, j], dev)

    def cross(u):
        i = u.place
        got(across(u, 1 - y, x * (u.rows - u.via_y), u.via_y), y_r.at[i])
        b = across(u, 1 - y, x * u.via_y, u.rows - u.via_y)
        send(i, None, b, b, x_s.at[i, 1], x_r.at[i, 1], X)

    def last(u):
        i = u.place
        got(three(u, (1 - x) * u.most, u.rows - u.most), x_r.at[i, 0])
        got(across(u, 1 - y, (1 - x) * u.via_y, u.rows - u.via_y), x_r.at[i, 1])
        b = across(u, y, x * (u.rows - u.via_y), u.via_y)
        remote(b, b, y_s.at[i], y_r.at[i], Y).wait_send()
        b = three(u, x * u.most, u.rows - u.most)
        remote(b, b, x_s.at[i, 0], x_r.at[i, 0], X).wait_send()
        settle(i)

    mine = c == z // 2

    def rows_out(src, dst, slot):
        for i in (0, 1):
            zd = 2 * c + i
            d = dst.at[pl.ds(al(z * 112, 16), 112)]
            send("rows", zd != z, src.at[i], d, row_s.at[slot, i], row_r.at[slot, z], {"tp": zd})
            when(
                zd == z,
                lambda i=i, d=d: pltpu.make_async_copy(src.at[i], d, loc.at[count + slot]).start(),
            )

    def rows_in(dst, slot):
        def wait():
            for j in others:
                got(dst.at[pl.ds(al(j * 112, 16), 112)], row_r.at[slot, j])
            d = dst.at[pl.ds(al(z * 112, 16), 112)]
            pltpu.make_async_copy(d, d, loc.at[count + slot]).wait()

        when(mine, wait)
        send("rows", mine, dst, dst, row_s.at[slot, 2], row_r.at[slot, 4], C)

    def rows_have(dst, slot):
        when(c != z // 2, lambda: got(dst, row_r.at[slot, 4]))

    parts = [slice(t * 96, (t + 1) * 96) for t in range(16)]

    def enc_local(t):
        return pltpu.make_async_copy(
            enc.at[lax.rem(z, 2), parts[t]], memory.at[parts[t]], loc.at[count + 2 + t]
        )

    def enc_send(t):
        send(
            "enc", mine, enc.at[lax.rem(z, 2), parts[t]], memory.at[parts[t]], row_s.at[2, t], row_r.at[2, t], C
        )
        when(mine, lambda: enc_local(t).start())

    def enc_have():
        for t in range(16):
            when(mine, lambda: enc_local(t).wait())
            when(c != z // 2, lambda: got(memory.at[parts[t]], row_r.at[2, t]))

    me = 2 * y + c

    def ids_out():
        for k, dev in enumerate((C, Y, YC)):
            send("ids", None, ids, idbuf.at[me], ad_s.at[k], ad_r.at[k], dev)
        idbuf[pl.ds(me, 1)] = ids[...][None]

    def adapters_pick():
        for k, s in enumerate((2 * y + 1 - c, 2 * (1 - y) + c, 2 * (1 - y) + 1 - c)):
            got(idbuf.at[s], ad_r.at[k])
        held = lax.broadcasted_iota(jnp.int32, (128, 32), 1) + me * 32
        rank = lax.rem(lax.broadcasted_iota(jnp.int32, (128, 32), 0), 16)
        lines = [
            [jnp.broadcast_to(idbuf[2 * s + k // 2, k % 2 : k % 2 + 1, :32], (16, 32)) for k in range(4)]
            for s in range(2)
        ]
        wanted = jnp.concatenate([line for pair in lines for line in pair])
        target = held.astype(f32) - rank.astype(f32)
        picks = jnp.where(wanted * 16.0 == target, 1.0, 0.0).astype(bf16)
        here = []
        for s in range(2):
            line = lines[s][0]
            for k in (1, 2, 3):
                line = jnp.where(z == k, lines[s][k], line)
            here.append(line)
        picks_z = jnp.where(jnp.concatenate(here) * 16.0 == target[:32], 1.0, 0.0).astype(bf16)
        for h in range(2):
            cols = slice(h * 128, h * 128 + 128)
            wide = slice(h * 512, h * 512 + 512)
            given = [u_ai[m][:, cols] for m in range(6)] + [u_fi[:, wide]]
            given += [d_ao[m][:, cols] for m in range(2)] + [d_fo[:, wide]]
            for b in range(4):
                block_of = jnp.concatenate(given, axis=1)[:, b * 512 : b * 512 + 512]
                dkv[h, b * 128 : b * 128 + 128] = nn(picks, block_of).astype(bf16)
            if h == 0:
                given = [d_ai[m] for m in range(5)]
            else:
                given = [d_ai[5], d_fi, u_ao[0], u_ao[1], u_fo]
            for b in range(10):
                block_of = given[b // 2][:, b % 2 * 512 : b % 2 * 512 + 512]
                dd[h, b * 32 : b * 32 + 32] = nn(picks_z, block_of).astype(bf16)
        send("pick", None, dkv.at[1 - c], rs, ad_s.at[3], ad_r.at[3], C)
        send("pick", None, dd.at[1 - c, 0:320], rw, ad_s.at[4], ad_r.at[4], C)

    def adapters_y():
        got(rs, ad_r.at[3])
        got(rw, ad_r.at[4])
        rs[...] += dkv[pl.ds(c, 1)][0]
        rw[...] += dd[pl.ds(c, 1), 0:320][0]
        for b in range(4):
            for k in range(2):
                ys_own[k, :, b * 512 : b * 512 + 512] = rs[b * 128 + k * 64 : b * 128 + k * 64 + 64]
        for b in range(10):
            for k in range(2):
                yw_own[k, :, b * 512 : b * 512 + 512] = rw[b * 32 + k * 16 : b * 32 + k * 16 + 16]
        send("pick", None, ys_own.at[1 - y], ys, ad_s.at[5], ad_r.at[5], Y)
        send("pick", None, yw_own.at[1 - y], yw, ad_s.at[6], ad_r.at[6], Y)

    def adapters_z():
        got(ys, ad_r.at[5])
        got(yw, ad_r.at[6])
        ys[...] += ys_own[pl.ds(y, 1)][0]
        fw[pl.ds(c, 1)] = (yw[...] + yw_own[pl.ds(y, 1)][0])[None]
        for k, j in enumerate(others):
            send("pick", None, ys.at[pl.ds(al(j * 16, 16), 16)], fz.at[z], ad_s.at[7 + k], ad_r.at[7 + z], {"tp": j})
        fz[pl.ds(z, 1)] = ys[pl.ds(al(z * 16, 16), 16)][None]
        send("pick", None, fw.at[c], fw.at[c], ad_s.at[11], ad_r.at[11], C)

    def adapters_have():
        for j in others:
            got(fz.at[j], ad_r.at[7 + j])
        got(fw.at[1 - c], ad_r.at[11])
        settle("pick")
        settle("ids")

    def whole(m):
        return fw[m // 5, :, (m % 5) * 1024 : (m % 5) * 1024 + 1024]

    def split(s):
        return jnp.concatenate([fz[k, :, s * 128 : s * 128 + 128] for k in range(4)], axis=1)

    def merge(u):
        m = u.index
        if u.tall:
            down_t = whole(min(m, 6)).T
            up_rows = split(m)
            for b in range(4):
                place = slice(m * 1024 + b * 256, m * 1024 + b * 256 + 256)
                ga[place] = (ga[place].astype(f32) + nn(down_t[b * 256 : b * 256 + 256], up_rows)).astype(bf16)
        else:
            down_t = split(10 + m).T
            up_rows = whole(7 + m if m < 2 else 9)
            for k in range(4):
                gb[m, k] = (gb[m, k].astype(f32) + nn(down_t[k * 128 : k * 128 + 128], up_rows)).astype(bf16)

    def wa(m):
        return ga[m * 1024 : (m + 1) * 1024]

    def wb(m):
        return gb[m].reshape(512, 1024)

    def part_out(e, slot):
        send(("part", e), None, outbox.at[slot], inbox.at[slot], ex_s.at[e], ex_r.at[e], C)

    def part_sum(e, slot):
        got(inbox.at[slot], ex_r.at[e])
        return outbox[slot] + inbox[slot]

    def norm_rows(side, source):
        unit, _ = normalize(source)
        normed[side] = (unit * gain[side] + shift[side]).astype(bf16)

    def start_rows():
        rows_have(rows, 0)
        norm_rows(0, rows[...].astype(f32))

    def project(m, source, out, length):
        def run():
            out[:length] = nn(source(), wa(m)).astype(bf16)
        return run

    def attention(side, first, number):
        q, k, v = ((q0, k0, v0), (q1, k1, v1))[side]
        length = (rows.shape[0], frames)[side]
        return lambda: attend_forward(q, k, v, mix.at[side], lse.at[side], length, side == 0, first, number, groups)

    def part0():
        outbox[0] = nn(mix[0], wb(0))
        part_out(0, 0)

    def second_rows():
        hidden[0] = rows[...].astype(f32) + part_sum(0, 0)
        norm_rows(1, hidden[0])

    def part1():
        outbox[1] = nn(mix[1], wb(1))
        part_out(1, 1)

    def third_rows():
        hidden[1] = hidden[0] + part_sum(1, 1)
        norm_rows(2, hidden[1])
        rows_have(grads, 1)

    def feed_first():
        settle(("part", 0))
        settle(("part", 1))
        r_up[0] = rank_t(whole(6), normed[2])
        r_up[1] = rank_t(whole(9), grads[...])

    def chunk(j):
        def run():
            up, down = wa(6 + j), wb(2 + j)
            pre = nn(normed[2], up)
            cdf = 0.5 * (1.0 + lax.erf(pre * (2**-0.5)))
            active = (pre * cdf).astype(bf16)
            slope = cdf + pre * jnp.exp(-0.5 * pre * pre) * 0.3989422804014327
            grad = (nt(grads[...], down) * slope).astype(bf16)
            if j == 0:
                outbox[1] = nn(active, down)
                outbox[0] = nt(grad, up)
                r_in[...] = nt(split(6 + j), grad)
                t_out[...] = nt(split(12 + j), active)
            else:
                outbox[1] += nn(active, down)
                outbox[0] += nt(grad, up)
                r_in[...] += nt(split(6 + j), grad)
                t_out[...] += nt(split(12 + j), active)
            gsplit[j] = nn(r_up[0], grad).astype(bf16)
            gsplit[4 + j] = nn(r_up[1], active).astype(bf16)
        return run

    tasks = {}

    def task(tick, fn):
        tasks.setdefault(tick, []).append(fn)

    task(1, adapters_pick)
    task(3, adapters_y)
    task(5, adapters_z)
    task(7, adapters_have)
    task(7, lambda: rows_in(rows, 0))
    task(8, start_rows)
    for u in units:
        task(2 * u.place + OFFS[4], functools.partial(merge, u))
    base = OFFS[4]
    task(base + 1, project(0, lambda: normed[0], q0, 448))
    task(base + 3, project(1, lambda: normed[0], k0, 448))
    task(base + 5, project(2, lambda: normed[0], v0, 448))
    task(base + 5, attention(0, 0, 2))
    task(base + 6, attention(0, 2, 2))
    task(base + 7, part0)
    task(base + 9, second_rows)
    task(base + 9, project(3, lambda: normed[1], q1, 448))
    task(base + 10, enc_have)
    task(base + 11, project(4, lambda: memory[...], k1, 1536))
    task(base + 12, project(5, lambda: memory[...], v1, 1536))
    task(base + 13, attention(1, 0, 2))
    task(base + 14, attention(1, 2, 2))
    task(base + 15, part1)
    task(base + 17, third_rows)
    task(base + 18, feed_first)
    task(12, lambda: rows_out(cot, grads, 1))
    task(22, lambda: rows_in(grads, 1))
    for j in range(4):
        task(base + 19 + 4 * j, chunk(j))

    ids_out()
    rows_out(tok, rows, 0)
    for u in units:
        core_exchange(u)
    for t in range(max(2 * count + base, max(tasks)) + 1):
        def at(offset):
            i, odd = divmod(t - offset, 2)
            return units[i] if not odd and 0 <= i < count else None

        if at(0):
            own(at(0))
        for k in (1, 2, 3):
            if at(OFFS[k - 1]):
                hop(at(OFFS[k - 1]), k)
        if at(OFFS[3]):
            cross(at(OFFS[3]))
        if at(OFFS[4]):
            last(at(OFFS[4]))
        if t < 16:
            enc_send(t)
        for fn in tasks.get(t, []):
            fn()

    boxes = list(
        zip(
            (rwb0, rwb1, rwb2), (czs0, czs1, czs2), (czw0, czw1, czw2), (sb0, sb1, sb2), (yb0, yb1, yb2),
            (xb0, xb1, xb2), (cb0, cb1, cb2), ((0, 8, 0, 1), (8, 4, 2, 2), (12, 4, 6, 2)), strict=True,
        )
    )

    def home_core(b):
        rwb, first, half = boxes[b][0], boxes[b][7][2], boxes[b][7][3]
        send(("home", b), None, gwhole.at[pl.ds(first + (1 - c) * half, half)], rwb, b_s.at[b, 0], b_r.at[b, 0], C)

    def home_z(b):
        rwb, czs, czw = boxes[b][:3]
        s0, ns, first, half = boxes[b][7]
        got(rwb, b_r.at[b, 0])
        rwb[...] += gwhole[pl.ds(first + c * half, half)]

        def cuts(j):
            return gsplit.at[s0 : s0 + ns, :, pl.ds(al(j * 128, 128), 128)], rwb.at[:, :, pl.ds(al(j * 256, 256), 256)]

        for k, j in enumerate(others):
            one, two = cuts(j)
            send(("home", b), None, one, czs.at[z], b_s.at[b, 1 + k], b_r.at[b, 1 + z], {"tp": j})
            send(("home", b), None, two, czw.at[z], b_s.at[b, 5 + k], b_r.at[b, 5 + z], {"tp": j})
        one, two = cuts(z)
        czs[pl.ds(z, 1)] = one[...][None]
        czw[pl.ds(z, 1)] = two[...][None]

    def dense_rows(b, to):
        czs, czw, (_, ns, _, half) = boxes[b][1], boxes[b][2], boxes[b][7]
        stack = jnp.concatenate(
            [jnp.concatenate([czs[k, s] for s in range(ns)] + [czw[k, w] for w in range(half)], axis=1) for k in range(4)]
        )
        row = lax.broadcasted_iota(jnp.int32, (64, 64), 0)
        col = lax.broadcasted_iota(jnp.int32, (64, 64), 1)
        clip = col // 16
        chosen = jnp.zeros((64, 64), f32)
        for k in range(4):
            line = idbuf[pl.ds(2 * y + k // 2, 1), k % 2 : k % 2 + 1, :64][0]
            chosen = jnp.where(clip == k, jnp.broadcast_to(line, (64, 64)), chosen)
        target = (row + 64 * to - lax.rem(col, 16)).astype(f32)
        return nn(jnp.where(chosen * 16.0 == target, 1.0, 0.0).astype(bf16), stack)

    def home_y(b):
        _, czs, czw, sb, yb = boxes[b][:5]
        for j in others:
            got(czs.at[j], b_r.at[b, 1 + j])
            got(czw.at[j], b_r.at[b, 5 + j])
        sb[...] = dense_rows(b, 1 - y).astype(bf16)
        send(("home", b), None, sb, yb, b_s.at[b, 9], b_r.at[b, 9], Y)

    def home_x(b):
        yb, xb = boxes[b][4:6]
        got(yb, b_r.at[b, 9])
        yb[...] = (dense_rows(b, y) + yb[...].astype(f32)).astype(bf16)
        send(("home", b), None, yb, xb, b_s.at[b, 10], b_r.at[b, 10], X)

    def home_rows(b):
        yb, xb, cb = boxes[b][4:7]
        got(xb, b_r.at[b, 10])
        xb[...] += yb[...]
        send(("home", b), None, xb.at[pl.ds(al((1 - c) * 32, 32), 32)], cb, b_s.at[b, 11], b_r.at[b, 11], C)

    def home_last(b):
        xb, cb = boxes[b][5:7]
        s0, ns, first, half = boxes[b][7]
        got(cb, b_r.at[b, 11])
        here, there = xb[pl.ds(al(c * 32, 32), 32)].astype(f32), cb[...].astype(f32)
        low, high = jnp.where(c == 0, here, there), jnp.where(c == 0, there, here)
        for s in range(ns):
            lanes = slice(s * 128, s * 128 + 128)
            split_sum[s0 + s] = jnp.concatenate([low[:, lanes], high[:, lanes]], axis=1)
        for w in range(half):
            lanes = slice(ns * 128 + w * 256, ns * 128 + w * 256 + 256)
            for q in range(4):
                wz[q, first + w] = low[q * 8 : q * 8 + 8, lanes]
                wz[q, first + half + w] = high[q * 8 : q * 8 + 8, lanes]
        slots = pl.ds(first, 2 * half)
        for k, j in enumerate(others):
            send(("home", b), None, wz.at[j, slots], whole_sum.at[z, slots], b_s.at[b, 12 + k], b_r.at[b, 12 + z], {"tp": j})
        pltpu.make_async_copy(wz.at[z, slots], whole_sum.at[z, slots], loc.at[count + 18 + b]).start()

    def home_done(b):
        first, half = boxes[b][7][2:]
        slots = pl.ds(first, 2 * half)
        for j in others:
            got(whole_sum.at[j, slots], b_r.at[b, 12 + j])
        pltpu.make_async_copy(wz.at[z, slots], whole_sum.at[z, slots], loc.at[count + 18 + b]).wait()

    def rows_back(src, dst, slot):
        def go():
            for k, j in enumerate(others):
                part = src.at[pl.ds(al(j * 112, 16), 112)]
                remote(part, dst.at[lax.rem(z, 2)], home_s.at[slot, k], home_r.at[slot, z], {"tp": j}).start()
            own_part(src, dst, slot).start()

        when(mine, go)

    def own_part(src, dst, slot):
        part = src.at[pl.ds(al(z * 112, 16), 112)]
        return pltpu.make_async_copy(part, dst.at[lax.rem(z, 2)], loc.at[count + 21 + slot])

    def rows_back_done(src, dst, slot):
        def go():
            for k, j in enumerate(others):
                part = src.at[pl.ds(al(j * 112, 16), 112)]
                remote(part, part, home_s.at[slot, k], home_r.at[slot, z], {"tp": j}).wait_send()
            own_part(src, dst, slot).wait()

        when(mine, go)
        for i in (0, 1):
            source = 2 * c + i
            when(source != z, lambda: got(dst.at[i], home_r.at[slot, source]))

    def enc_dst(quarter_of):
        return g_enc.at[lax.rem(z, 2), :, pl.ds(al(c * 512, 512), 512)]

    def enc_copy(j):
        part = k1.at[pl.ds(al(j * 384, 128), 384)]
        owner = z // 2
        sems = home_s.at[2, j], home_r.at[2 + c, z]
        return part, owner, sems

    def enc_back(j):
        part, owner, (s, r) = enc_copy(j)
        when((j != z) | (c != owner), lambda: remote(part, enc_dst(j), s, r, {"tp": j, "core": owner}).start())
        when((j == z) & (c == owner), lambda: pltpu.make_async_copy(part, enc_dst(j), loc.at[count + 23]).start())

    def enc_back_done():
        for j in range(4):
            part, owner, (s, r) = enc_copy(j)
            when((j != z) | (c != owner), lambda: remote(part, enc_dst(j), s, r, {"tp": j, "core": owner}).wait_send())
            when((j == z) & (c == owner), lambda: pltpu.make_async_copy(part, enc_dst(j), loc.at[count + 23]).wait())
        for i in (0, 1):
            for other in (0, 1):
                source = 2 * c + i
                when(
                    (source != z) | (c != other),
                    lambda: got(g_enc.at[i, :, other * 512 : other * 512 + 512], home_r.at[2 + other, source]),
                )

    def rank_pair(side, i, u, g):
        s0, w0 = (12, 6) if side == 0 else (8, 2)
        m = 3 * side + i
        inner = rank_t(whole(m), u[...])
        back = rank_t(split(m), g[...])
        gsplit[s0 + i] = nn(inner, g[...]).astype(bf16)
        gwhole[w0 + i] = nn(back, u[...]).astype(bf16)

    def rank_out(side):
        s0, w0 = (12, 6) if side == 0 else (8, 2)
        gsplit[s0 + 3] = nn(rank_t(whole(7 + side), grads[...]), mix[side]).astype(bf16)
        gwhole[w0 + 3] = nn(rank_t(split(10 + side), mix[side]), grads[...]).astype(bf16)

    def memory_half(h, place):
        rows_of = [pl.ds(al(m * 1024 + h * 512, 512), 512) for m in (4, 5)]
        return nt(dk1[place], ga[rows_of[0]]) + nt(dv1[place], ga[rows_of[1]])

    quarters = [slice(q * 384, q * 384 + 384) for q in range(4)]
    dk1, dv1 = ga.at[pl.ds(6144, 1536)], ga.at[pl.ds(7680, 1536)]
    dk0, dv0 = dkv.at[0, 0:448], dkv.at[1, 0:448]
    part_out(3, 0)
    gwhole[0] = nn(r_in[...].astype(bf16), normed[2]).astype(bf16)
    gwhole[1] = nn(t_out[...].astype(bf16), grads[...]).astype(bf16)
    home_core(0)
    g_now[...] = grads[...].astype(f32) + norm_back(hidden[1], gain[2], part_sum(3, 0))
    part_out(2, 1)
    settle("rows")
    grads[...] = g_now[...].astype(bf16)
    do[...] = nt(grads[...], wb(1)).astype(bf16)
    home_z(0)
    attend_backward(q1, k1, v1, do, lse.at[1], dq, dk1, dv1, frames, False, 0, 2, groups)
    normed[2] = (hidden[1] + part_sum(2, 1)).astype(bf16)
    rows_back(normed.at[2], acts, 0)
    rank_out(1)
    home_y(0)
    attend_backward(q1, k1, v1, do, lse.at[1], dq, dk1, dv1, frames, False, 2, 2, groups)
    settle(("part", 3))
    outbox[0] = nt(dq[...], wa(3))
    part_out(4, 0)
    for place in quarters:
        k1[place] = memory_half(1 - c, place).astype(bf16)
    home_x(0)
    grad_part = part_sum(4, 0)
    send("memory", None, k1, v1, ex_s.at[6], ex_r.at[6], C)
    g_now[...] += norm_back(hidden[0], gain[1], grad_part)
    grads[...] = g_now[...].astype(bf16)
    do[...] = nt(grads[...], wb(0)).astype(bf16)
    got(v1, ex_r.at[6])
    settle("memory")
    for q, place in enumerate(quarters):
        k1[place] = (memory_half(c, place) + v1[place].astype(f32)).astype(bf16)
        enc_back(q)
    rank_pair(1, 0, normed.at[1], dq)
    home_rows(0)
    attend_backward(q0, k0, v0, do, lse.at[0], dq, dk0, dv0, rows.shape[0], True)
    settle(("part", 2))
    outbox[1] = nt(dq[...], wa(0))
    outbox[1] += nt(dk0[...], wa(1))
    outbox[1] += nt(dv0[...], wa(2))
    part_out(5, 1)
    home_last(0)
    rank_pair(0, 0, normed.at[0], dq)
    rank_pair(0, 1, normed.at[0], dk0)
    rank_pair(0, 2, normed.at[0], dv0)
    rank_out(0)
    home_core(2)
    normed[0] = (g_now[...] + norm_back(rows[...].astype(f32), gain[0], part_sum(5, 1))).astype(bf16)
    rows_back(normed.at[0], g_tok, 1)
    home_z(2)
    rank_pair(1, 1, memory, dk1)
    rank_pair(1, 2, memory, dv1)
    home_core(1)
    home_y(2)
    home_z(1)
    home_x(2)
    home_y(1)
    home_rows(2)
    home_x(1)
    home_last(2)
    home_rows(1)
    home_last(1)
    for b in range(3):
        home_done(b)
    rows_back_done(normed.at[2], acts, 0)
    rows_back_done(normed.at[0], g_tok, 1)
    enc_back_done()
    for key in list(sent):
        settle(key)


def layer(tok, enc, cot, w_in, w_out, w_up, w_down, ids, gain, shift, *adapters):
    any_ = pl.BlockSpec(memory_space=pl.ANY)
    r, d = 448, tok.shape[2]
    padded = enc.shape[1]
    dma = pltpu.SemaphoreType.DMA

    def vm(*shape, dtype=bf16):
        return pltpu.VMEM(shape, dtype)

    n = 16
    halves = (1, 2, 2)
    splits = (8, 4, 4)
    widths = [s * 128 + w * 256 for s, w in zip(splits, halves, strict=True)]
    return pl.pallas_call(
        layer_kernel,
        out_shape=[
            sds((2, r // 4, d), bf16), sds((2, r // 4, d), bf16), sds((2, padded // 4, d), bf16),
            sds((16, 32, 256), f32), sds((4, 10, 8, 256), f32),
        ],
        in_specs=[any_] * 7 + [VM] * 11,
        out_specs=[any_] * 3 + [VM, any_],
        scratch_shapes=[
            vm(10 * d, 512), vm(6, 4, 128, d), vm(r, d), vm(r, d), vm(padded, d), vm(3, r, d),
            vm(r, 512), vm(r, 512), vm(r, 512), vm(2, r, 512), vm(r, 512), vm(padded, 512), vm(padded, 512),
            vm(2, 4, 2, r, dtype=f32), vm(2, r, d, dtype=f32), vm(r, d, dtype=f32), vm(2, r, 512), vm(2, 512, 512),
            vm(2, r, d, dtype=f32), vm(2, r, d, dtype=f32),
            vm(4, 8, 128, dtype=f32), vm(512, 512), vm(320, 512), vm(64, 2048), vm(16, 5120), vm(2, 64, 2048), vm(2, 16, 5120),
            vm(4, 16, 2048), vm(2, 16, 5120), vm(16, r, dtype=f32), vm(16, r, dtype=f32), vm(2, 16, r),
            vm(16, 16, 512), vm(10, 16, d), vm(4, 10, 8, 256, dtype=f32),
            *[vm(w, 16, d) for w in halves], *[vm(4, s, 16, 128) for s in splits], *[vm(4, w, 16, 256) for w in halves],
            *[vm(64, w) for w in widths], *[vm(64, w) for w in widths], *[vm(64, w) for w in widths], *[vm(32, w) for w in widths],
            dma((n,)), dma((n,)), dma((n, 4)), dma((n, 4)), dma((n, 4)), dma((n,)), dma((n,)), dma((n, 2)), dma((n, 2)),
            dma((3, 16)), dma((3, 16)), dma((n + 24,)), dma((12,)), dma((12,)), dma((7,)), dma((7,)),
            dma((3, 16)), dma((3, 16)), dma((4, 4)), dma((4, 4)),
        ],
        compiler_params=pltpu.CompilerParams(
            collective_id=1, has_side_effects=True, vmem_limit_bytes=int(62.5 * 1024 * 1024)
        ),
        name="layer",
    )(tok, enc, cot, w_in, w_out, w_up, w_down, ids, gain, shift, *adapters)


def swap_core(rows):
    return lax.ppermute(rows, "core", SWAP)


def core_sum(part):
    return part + swap_core(part)


def own_and_other(stacked):
    core = lax.axis_index("core")
    keep = lax.dynamic_index_in_dim(stacked, core, 0, keepdims=False)
    send = lax.dynamic_index_in_dim(stacked, 1 - core, 0, keepdims=False)
    return keep, swap_core(send)


def in_core_order(own, other):
    first = lax.axis_index("core") == 0
    return jnp.stack([jnp.where(first, own, other), jnp.where(first, other, own)])


def scatter_sh(stacked):
    n = lax.axis_size("sh")
    if n == 2:
        me = lax.axis_index("sh")
        keep = lax.dynamic_index_in_dim(stacked, me, 0, keepdims=False)
        send = lax.dynamic_index_in_dim(stacked, 1 - me, 0, keepdims=False)
        return keep + lax.ppermute(send, "sh", SWAP)
    return lax.psum_scatter(stacked, "sh", scatter_dimension=0, tiled=False)


def over_z(stacked):
    return lax.all_to_all(stacked, "tp", 0, 0, tiled=True)


def half_columns(rows):
    width = rows.shape[-1] // 2
    return lax.dynamic_slice_in_dim(rows, lax.axis_index("core") * width, width, rows.ndim - 1)


def rows_home(half):
    tp = lax.axis_size("tp")
    moved = over_z(half.reshape(tp, half.shape[0] // tp, half.shape[1]))
    own, other = own_and_other(moved.reshape(2, tp // 2, *moved.shape[1:]))
    both = in_core_order(own, other)
    return jnp.moveaxis(both, 0, 2).reshape(both.shape[1], both.shape[2], 2 * half.shape[1])


def rows_here(rows):
    tp = lax.axis_size("tp")
    both = in_core_order(rows, swap_core(rows)).reshape(4, *rows.shape[1:])
    moved = over_z(half_columns(both))
    moved = moved.reshape(tp * rows.shape[1], rows.shape[2] // 2)
    pair = in_core_order(moved, swap_core(moved))
    return jnp.concatenate([pair[0], pair[1]], axis=-1)


def gather_weights(w_attn_in, w_attn_out, w_up, w_down):
    def over_shard(block, axis):
        return lax.all_gather(block, ("sh", "core"), axis=axis, tiled=True)

    def over_tp(block, axis):
        return lax.all_gather(block, "tp", axis=axis, tiled=True)

    core = lax.axis_index("core")

    def half(block, axis):
        width = block.shape[axis] // 2
        return lax.dynamic_slice_in_dim(block, core * width, width, axis)

    w_in = over_tp(half(over_shard(w_attn_in.reshape(6, *w_attn_in.shape[3:]), 1), 2), 2)
    w_out = over_tp(half(over_shard(w_attn_out[0], 2), 1), 1)
    w_first = over_tp(half(over_shard(w_up[0], 0), 1), 1)
    w_second = over_tp(half(over_shard(w_down[0], 1), 0), 0)
    return w_in, w_out, w_first, w_second


def wide_parts(args):
    (
        tokens, encoded, cotangent, adapter_of, w_attn_in, w_attn_out, w_up, w_down, norm_gain, norm_shift,
        down_attn_in, up_attn_in, down_feed_in, up_feed_in, down_attn_out, up_attn_out, down_feed_out, up_feed_out,
    ) = args
    n, tp = lax.axis_size("sh"), lax.axis_size("tp")
    sh, core, z = lax.axis_index("sh"), lax.axis_index("core"), lax.axis_index("tp")
    width = w_attn_in.shape[3] * 2 * n
    held_rows = down_feed_in.shape[1]
    quarter = width // tp
    piece = quarter // 2

    ids = lax.all_gather(adapter_of, ("sh", "core"), tiled=True)

    row_ids = (sh * 2 + core) * held_rows + jnp.arange(held_rows)
    wanted = ids.reshape(n, tp)[:, :, None] * RANK + jnp.arange(RANK)
    picks = (wanted[..., None] == row_ids).astype(bf16)
    whole = jnp.concatenate(
        [
            down_attn_in.reshape(6, held_rows, width),
            down_feed_in,
            up_attn_out[0],
            up_feed_out,
        ]
    )
    def in_quarters(rows):
        return jnp.moveaxis(rows.reshape(held_rows, tp, quarter), 1, 0)

    split = jnp.concatenate(
        [
            up_attn_in.reshape(6, held_rows, quarter),
            in_quarters(up_feed_in[0]),
            down_attn_out[0],
            in_quarters(down_feed_out[0]),
        ]
    )
    picks_z = lax.dynamic_index_in_dim(picks, z, 1, keepdims=False)
    chosen_whole = jnp.einsum("srk,mkd->smrd", picks_z, whole, preferred_element_type=f32).astype(bf16)
    chosen_split = jnp.einsum("szrk,mkd->szmrd", picks, split, preferred_element_type=f32).astype(bf16)
    chosen_whole = core_sum(scatter_sh(chosen_whole))
    chosen_split = over_z(core_sum(scatter_sh(chosen_split)))

    def columns(first, count):
        mine = half_columns(chosen_split[:, first : first + count])
        return jnp.moveaxis(mine, 0, 2).reshape(count, RANK, tp * piece)

    def wide_columns(first):
        mine = lax.dynamic_slice_in_dim(chosen_split[:, first : first + tp], core * 2, 2, 1)
        return jnp.moveaxis(mine, 2, 0).reshape(RANK, tp * 2 * quarter)

    a_in, a_up, b_out, b_down = chosen_whole[:6], chosen_whole[6], chosen_whole[7:9], chosen_whole[9]
    b_in, b_up, a_out, a_down = columns(0, 6), wide_columns(6), columns(6 + tp, 2), wide_columns(8 + tp)

    w_in, w_out, w_first, w_second = gather_weights(w_attn_in, w_attn_out, w_up, w_down)
    taken = rows_here(tokens)
    upstream = rows_here(cotangent)
    mine = lax.dynamic_index_in_dim(encoded, z % 2, 0, keepdims=False)
    memory = jnp.where(core == z // 2, mine, swap_core(mine))

    def merge(weight, down_rows, up_rows):
        return (weight.astype(f32) + t_mm(down_rows, up_rows)).astype(bf16)

    w_in = [merge(w_in[i], a_in[i], b_in[i]) for i in range(6)]
    w_out = [merge(w_out[i], a_out[i], b_out[i]) for i in range(2)]
    w_first = merge(w_first, a_up, b_up)
    w_second = merge(w_second, a_down, b_down)

    gain, shift = norm_gain[0][:, None], norm_shift[0][:, None]
    frames = memory.shape[0]
    w_in = jnp.stack(w_in)
    normed0, q0, k0, v0, lse0, mix0, part = self_forward(taken, gain[0], shift[0], w_in[:3], w_out[0])
    k1, v1 = memory_project(memory, w_in[4:])
    hidden1, normed1, q1, lse1, mix1, part1 = cross_forward(
        taken, part, swap_core(part), gain[1], shift[1], w_in[3], k1, v1, w_out[1], frames
    )
    hidden2, part2, back, g_aup, g_bup, g_adown, g_bdown = feed(
        hidden1, part1, swap_core(part1), gain[2], shift[2], w_first, w_second, upstream, a_up, b_up, a_down, b_down
    )
    result = (hidden2 + core_sum(part2)).astype(bf16)
    grad, e1, dq1, dk1, dv1, back1 = cross_backward(
        hidden2, gain[2], upstream, back, swap_core(back), w_out[1], w_in[3], q1, k1, v1, lse1, frames
    )
    part = memory_backward(dk1, dv1, w_in[4:], frames)
    own, other = own_and_other(jnp.moveaxis(part.reshape(part.shape[0], 2, -1), 1, 0))
    memory_rows = (own.astype(f32) + other.astype(f32)).astype(bf16)
    grad, e0, dq0, dk0, dv0, back0 = self_backward(
        hidden1, gain[1], grad, back1, swap_core(back1), w_out[0], w_in[:3], q0, k0, v0, lse0
    )
    grad = final_norm(taken, gain[0], grad, back0, swap_core(back0))
    ranks1 = attention_ranks(normed1, memory, mix1, dq1, dk1, dv1, e1, a_in[3:], b_in[3:], a_out[1], b_out[1])
    ranks0 = attention_ranks(normed0, None, mix0, dq0, dk0, dv0, e0, a_in[:3], b_in[:3], a_out[0], b_out[0])
    feed_up = jnp.moveaxis(g_bup.reshape(RANK, tp, tp, piece), 2, 0).reshape(tp, RANK, tp * piece)
    feed_down = jnp.moveaxis(g_adown.reshape(RANK, tp, tp, piece), 2, 0).reshape(tp, RANK, tp * piece)
    out_split = jnp.stack([ranks0[2], ranks1[2]])
    out_whole = jnp.stack([ranks0[3], ranks1[3]])
    split_grads = jnp.concatenate([ranks0[1], ranks1[1], feed_up.astype(bf16), out_split, feed_down.astype(bf16)])
    whole_grads = jnp.concatenate(
        [ranks0[0], ranks1[0], g_aup.astype(bf16)[None], out_whole, g_bdown.astype(bf16)[None]]
    )
    here = ids.reshape(n, tp)[sh]
    return result, grad, memory_rows, split_grads, whole_grads, here


def narrow_parts(args):
    (
        tokens, encoded, cotangent, adapter_of, w_attn_in, w_attn_out, w_up, w_down, norm_gain, norm_shift,
        down_attn_in, up_attn_in, down_feed_in, up_feed_in, down_attn_out, up_attn_out, down_feed_out, up_feed_out,
    ) = args

    def six(rows):
        return rows.reshape(6, *rows.shape[3:])

    lines = jnp.pad(adapter_of.astype(f32), (0, 6))[:, None] * jnp.ones((1, 128), f32)
    _, frames, d = encoded.shape
    step = frames // 4
    spaced = jnp.pad(encoded.reshape(2, 4, step, d), ((0, 0), (0, 0), (0, 384 - step), (0, 0)))
    spaced = spaced.reshape(2, 1536, d)
    acts, g_tok, g_enc, split_sum, whole_sum = layer(
        tokens, spaced, cotangent, six(w_attn_in), w_attn_out[0], w_up[0], w_down[0], lines,
        norm_gain[0][:, None], norm_shift[0][:, None], six(down_attn_in), six(up_attn_in), down_feed_in[0],
        up_feed_in[0], down_attn_out[0], up_attn_out[0], down_feed_out[0], up_feed_out[0],
    )
    held = split_sum.shape[1]

    def wide_of(first):
        block = split_sum[first : first + 4].reshape(4, held, 2, 128)
        return jnp.moveaxis(block, 0, 2).reshape(1, held, 1024)

    whole = jnp.moveaxis(whole_sum, 0, 2).reshape(10, whole_sum.shape[2], d)
    cross_side, self_side = split_sum[8:12], split_sum[12:16]
    return (
        acts,
        g_tok.astype(f32),
        g_enc[:, :step].astype(f32),
        jnp.stack([whole[6:9], whole[2:5]])[None],
        jnp.stack([self_side[:3], cross_side[:3]])[None],
        whole[0:1],
        wide_of(0),
        jnp.stack([self_side[3], cross_side[3]])[None],
        jnp.stack([whole[9], whole[5]])[None],
        wide_of(4),
        whole[1:2],
    )


def on_device(*args):
    if lax.axis_size("sh") == 2:
        return narrow_parts(args)
    n, tp = lax.axis_size("sh"), lax.axis_size("tp")
    held_rows, quarter = args[12].shape[1], args[11].shape[4]
    width, piece = quarter * tp, quarter // 2
    result, grad, memory_rows, split_grads, whole_grads, here = wide_parts(args)
    activations = rows_home(half_columns(result))
    grad_encoded = rows_home(memory_rows).astype(f32)
    grad_tokens = rows_home(half_columns(grad)).astype(f32)
    compact = jnp.moveaxis(split_grads.reshape(-1, RANK, tp, piece), 2, 0)
    own, other = own_and_other(jnp.moveaxis(whole_grads.reshape(-1, RANK, tp, 2, piece), (3, 2), (0, 1)))
    compact = jnp.concatenate([compact, own + other], axis=1)
    compact = over_z(compact)
    rows = jnp.arange(2 * n * held_rows)
    place = (here[:, None] * RANK + jnp.arange(RANK))[None] == rows[:, None, None]
    dense = jnp.einsum("gkr,kmrp->gmp", place.astype(bf16), compact, preferred_element_type=f32)
    dense = dense.astype(bf16).reshape(n, 2, held_rows, *dense.shape[1:])
    dense = scatter_sh(dense)
    dense = dense + lax.ppermute(dense, "rep", SWAP)
    both = in_core_order(*own_and_other(dense))
    done = jnp.moveaxis(both, 0, 2)
    count = 8 + 2 * tp
    sums = done[:, :count].astype(f32)

    def narrow(first, number):
        block = sums[:, first : first + number].reshape(held_rows, number, quarter)
        return jnp.moveaxis(block, 1, 0)

    def wide_of(first):
        block = jnp.moveaxis(sums[:, first : first + tp], 2, 1)
        return block.reshape(held_rows, 2 * tp * piece)

    grad_up_attn_in = narrow(0, 6).reshape(1, 2, 3, held_rows, quarter)
    grad_up_feed_in = wide_of(6)[None]
    grad_down_attn_out = narrow(6 + tp, 2)[None]
    grad_down_feed_out = wide_of(8 + tp)[None]
    rest = done[:, count:].reshape(tp, held_rows // tp, 10, quarter)
    rest = jnp.moveaxis(over_z(rest), 0, 2)
    rest = jnp.moveaxis(rest.reshape(held_rows // tp, 10, width), 1, 0).astype(f32)
    return (
        activations,
        grad_tokens,
        grad_encoded,
        rest[:6].reshape(1, 2, 3, held_rows // tp, width),
        grad_up_attn_in,
        rest[6:7],
        grad_up_feed_in,
        grad_down_attn_out,
        rest[7:9][None],
        grad_down_feed_out,
        rest[9:10],
    )


def solution(mesh):
    rep, shard, tp = (mesh.shape[name] for name in ("rep", "shard", "tp"))
    fine = Mesh(mesh.devices.reshape(rep, shard // 2, 2, tp), ("rep", "sh", "core", "tp"))
    shard = ("sh", "core")
    clips = ("rep", "sh", "core")
    both = ("sh", "core", "tp")
    placed = (
        P(clips, "tp", None),
        P(clips, None, None),
        P(clips, "tp", None),
        P(clips),
        P(None, None, None, shard, "tp"),
        P(None, None, "tp", shard),
        P(None, shard, "tp"),
        P(None, "tp", shard),
        P(),
        P(),
        P(None, None, None, shard, None),
        P(None, None, None, shard, "tp"),
        P(None, shard, None),
        P(None, shard, "tp"),
        P(None, None, shard, "tp"),
        P(None, None, shard, None),
        P(None, shard, "tp"),
        P(None, shard, None),
    )
    return jax.shard_map(
        on_device,
        mesh=fine,
        in_specs=placed,
        out_specs=(
            P(clips, "tp", None),
            P(clips, "tp", None),
            P(clips, "tp", None),
            P(None, None, None, both, None),
            P(None, None, None, shard, "tp"),
            P(None, both, None),
            P(None, shard, "tp"),
            P(None, None, shard, "tp"),
            P(None, None, both, None),
            P(None, shard, "tp"),
            P(None, both, None),
        ),
        check_vma=False,
    )
```

```python
import functools

import jax
import jax.numpy as jnp
from jax import lax
from jax.experimental import pallas as pl
from jax.experimental.pallas import tpu as pltpu
from jax.sharding import Mesh, PartitionSpec as P

HD = 64
RANK = 16
epsilon = 1e-05
masked_score = -1e30
f32, bf16 = jnp.float32, jnp.bfloat16
SWAP = ((0, 1), (1, 0))
MESH = pl.DeviceIdType.MESH


def dot(a, b, dims):
    return lax.dot_general(a, b, (dims, ((), ())), preferred_element_type=f32)


def mm(a, b):
    return dot(a, b, ((1,), (0,)))


def mm_t(a, b):
    return dot(a, b, ((1,), (1,)))


def t_mm(a, b):
    return dot(a, b, ((0,), (0,)))


HIDE = -1e30
SCALE = HD**-0.5
EPS = 1e-05
VM = pl.BlockSpec(memory_space=pltpu.VMEM)


def nn(a, b):
    return lax.dot_general(a, b, (((1,), (0,)), ((), ())), preferred_element_type=f32)


def nt(a, b):
    return lax.dot_general(a, b, (((1,), (1,)), ((), ())), preferred_element_type=f32)


def normalize(rows):
    centered = rows - jnp.mean(rows, axis=-1, keepdims=True)
    variance = jnp.mean(centered * centered, axis=-1, keepdims=True)
    inverse = lax.rsqrt(variance + EPS)
    return centered * inverse, inverse


def norm_back(rows, gain, grad):
    unit, inverse = normalize(rows)
    scaled = grad * gain
    first = jnp.mean(scaled, axis=-1, keepdims=True)
    second = jnp.mean(scaled * unit, axis=-1, keepdims=True)
    return (scaled - first - unit * second) * inverse


def pair_lanes(p):
    return pl.ds(pl.multiple_of(p * 128, 128), 128)


def scores_t(keys, queries, frames, causal, groups=1):
    s = nt(keys, queries) * SCALE
    if causal:
        key = lax.broadcasted_iota(jnp.int32, s.shape, 0)
        query = lax.broadcasted_iota(jnp.int32, s.shape, 1)
        s = jnp.where(query >= key, s, HIDE)
    elif frames < s.shape[0]:
        step, used = s.shape[0] // groups, frames // groups
        kept = used // 16 * 16
        key = kept + lax.broadcasted_iota(jnp.int32, (step - kept, s.shape[1]), 0)
        blocks = [s[g * step : (g + 1) * step] for g in range(groups)]
        s = jnp.concatenate([part for b in blocks for part in (b[:kept], jnp.where(key < used, b[kept:], HIDE))])
    return s


def attend_forward(q, k, v, mix, lse, frames, causal, start=0, number=None, groups=1):
    def pair(p, carry):
        lanes = pair_lanes(p)
        qp, kp = q[:, lanes], k[:, lanes]
        vt = v[:, lanes].T
        first = lax.broadcasted_iota(jnp.int32, qp.shape, 1) < HD
        outs, logs = [], []
        for h in (0, 1):
            s = scores_t(kp, jnp.where(first == (h == 0), qp, 0), frames, causal, groups)
            top = jnp.max(s, axis=0, keepdims=True)
            e = jnp.exp(s - top)
            total = jnp.sum(e, axis=0, keepdims=True)
            probs = (e * (1.0 / total)).astype(bf16)
            outs.append(nn(vt, probs)[h * HD : (h + 1) * HD])
            logs.append(top + jnp.log(total))
        mix[:, lanes] = jnp.concatenate(outs).T.astype(bf16)
        lse[p] = jnp.concatenate(logs)
        return carry

    lax.fori_loop(start, start + (number or q.shape[1] // 128), pair, 0)


def attend_backward(q, k, v, do, lse, dq, dk, dv, frames, causal, start=0, number=None, groups=1):
    def pair(p, carry):
        lanes = pair_lanes(p)
        qp, kp, vp, dop = q[:, lanes], k[:, lanes], v[:, lanes], do[:, lanes]
        kt = kp.T
        logs = lse[p]
        first = lax.broadcasted_iota(jnp.int32, qp.shape, 1) < HD
        dqs, dks, dvs = [], [], []
        for h in (0, 1):
            mine = first == (h == 0)
            s = scores_t(kp, jnp.where(mine, qp, 0), frames, causal, groups)
            probs = jnp.exp(s - logs[h : h + 1])
            dvs.append(nn(probs.astype(bf16), dop))
            dp = nt(vp, jnp.where(mine, dop, 0))
            t = probs * dp
            ds = (t - probs * jnp.sum(t, axis=0, keepdims=True)).astype(bf16)
            dks.append(nn(ds, qp))
            dqs.append(nn(kt, ds)[h * HD : (h + 1) * HD])
        first_k = lax.broadcasted_iota(jnp.int32, kp.shape, 1) < HD
        dv[:, lanes] = jnp.where(first_k, dvs[0], dvs[1]).astype(bf16)
        dk[:, lanes] = (jnp.where(first_k, dks[0], dks[1]) * SCALE).astype(bf16)
        dq[:, lanes] = (jnp.concatenate(dqs).T * SCALE).astype(bf16)
        return carry

    lax.fori_loop(start, start + (number or q.shape[1] // 128), pair, 0)


def params():
    return pltpu.CompilerParams(vmem_limit_bytes=60 * 1024 * 1024)


def sds(shape, dtype):
    return jax.ShapeDtypeStruct(shape, dtype)


def self_forward(tok, gain, shift, wi, wo):
    def kernel(tok, gain, shift, wi, wo, normed, q, k, v, lse, mix, part):
        unit, _ = normalize(tok[...].astype(f32))
        normed[...] = (unit * gain[...] + shift[...]).astype(bf16)
        for i, out in enumerate((q, k, v)):
            out[...] = nn(normed[...], wi[i]).astype(bf16)
        attend_forward(q, k, v, mix, lse, tok.shape[0], True)
        part[...] = nn(mix[...], wo[...])

    r, d = tok.shape
    w = wi.shape[2]
    return pl.pallas_call(kernel, out_shape=[sds((r, d), bf16)] + [sds((r, w), bf16)] * 3 + [sds((w // 128, 2, r), f32), sds((r, w), bf16), sds((r, d), f32)],
        in_specs=[VM] * 5, out_specs=[VM] * 7, compiler_params=params(), name="self_forward")(tok, gain, shift, wi, wo)


def memory_project(enc, wi):
    def kernel(enc, wi, k, v):
        frames = enc.shape[0]
        for i, out in enumerate((k, v)):
            out[:frames] = nn(enc[...], wi[i]).astype(bf16)
            out[frames:] = jnp.zeros((out.shape[0] - frames, out.shape[1]), bf16)
    frames = -(-enc.shape[0] // 128) * 128
    return pl.pallas_call(kernel, out_shape=[sds((frames, wi.shape[2]), bf16)] * 2, in_specs=[VM] * 2, out_specs=[VM] * 2, compiler_params=params(), name="memory_project")(enc, wi)


def cross_forward(hid, part, other, gain, shift, wq, k, v, wo, frames):
    def kernel(hid, part, other, gain, shift, wq, k, v, wo, hidden, normed, q, lse, mix, out):
        hidden[...] = hid[...].astype(f32) + part[...] + other[...]
        unit, _ = normalize(hidden[...])
        normed[...] = (unit * gain[...] + shift[...]).astype(bf16)
        q[...] = nn(normed[...], wq[...]).astype(bf16)
        attend_forward(q, k, v, mix, lse, frames, False)
        out[...] = nn(mix[...], wo[...])

    r, d = hid.shape
    w = wq.shape[1]
    return pl.pallas_call(kernel, out_shape=[sds((r, d), f32), sds((r, d), bf16), sds((r, w), bf16), sds((w // 128, 2, r), f32), sds((r, w), bf16), sds((r, d), f32)],
        in_specs=[VM] * 9, out_specs=[VM] * 6, compiler_params=params(), name="cross_forward")(hid, part, other, gain, shift, wq, k, v, wo)


def rank_t(rows16, inputs):
    return nt(rows16, inputs).astype(bf16)


def feed(hid, part, other, gain, shift, up, down, e, a_up, b_up, a_down, b_down):
    CH = 512

    def kernel(hid, part, other, gain, shift, up, down, e, a_up, b_up, a_down, b_down, hidden, out, back, g_aup, g_bup, g_adown, g_bdown, normed):
        hidden[...] = hid[...] + part[...] + other[...]
        unit, _ = normalize(hidden[...])
        normed[...] = (unit * gain[...] + shift[...]).astype(bf16)
        t_in = rank_t(a_up[...], normed[...])
        r_out = rank_t(b_down[...], e[...])
        r_in = jnp.zeros((16, hid.shape[0]), f32)
        t_out = jnp.zeros((16, hid.shape[0]), f32)
        for j in range(up.shape[1] // CH):
            cols = slice(j * CH, (j + 1) * CH)
            pre = nn(normed[...], up[:, cols])
            cdf = 0.5 * (1.0 + lax.erf(pre * (2**-0.5)))
            active = (pre * cdf).astype(bf16)
            slope = cdf + pre * jnp.exp(-0.5 * pre * pre) * 0.3989422804014327
            grad = (nt(e[...], down[cols]) * slope).astype(bf16)
            term, term_b = nn(active, down[cols]), nt(grad, up[:, cols])
            if j == 0:
                out[...], back[...] = term, term_b
            else:
                out[...] += term
                back[...] += term_b
            g_bup[:, cols] = nn(t_in, grad)
            g_adown[:, cols] = nn(r_out, active)
            r_in += nt(b_up[:, cols], grad)
            t_out += nt(a_down[:, cols], active)
        g_aup[...] = nn(r_in.astype(bf16), normed[...])
        g_bdown[...] = nn(t_out.astype(bf16), e[...])

    r, d = hid.shape
    w = up.shape[1]
    return pl.pallas_call(kernel, out_shape=[sds((r, d), f32)] * 3 + [sds((16, d), f32), sds((16, w), f32), sds((16, w), f32), sds((16, d), f32)],
        in_specs=[VM] * 12, out_specs=[VM] * 7, scratch_shapes=[pltpu.VMEM((r, d), bf16)], compiler_params=params(), name="feed")(
            hid, part, other, gain, shift, up, down, e, a_up, b_up, a_down, b_down)


def cross_backward(hid3, gain3, g, part, other, wo, wq, q, k, v, lse, frames):
    def kernel(hid3, gain3, g, part, other, wo, wq, q, k, v, lse, g_out, e, dq, dk, dv, back, do):
        g_out[...] = g[...].astype(f32) + norm_back(hid3[...], gain3[...], part[...] + other[...])
        e[...] = g_out[...].astype(bf16)
        do[...] = nt(e[...], wo[...]).astype(bf16)
        attend_backward(q, k, v, do, lse, dq, dk, dv, frames, False)
        back[...] = nt(dq[...], wq[...])

    r, d = hid3.shape
    w, f = q.shape[1], k.shape[0]
    return pl.pallas_call(kernel, out_shape=[sds((r, d), f32), sds((r, d), bf16), sds((r, w), bf16), sds((f, w), bf16), sds((f, w), bf16), sds((r, d), f32)],
        in_specs=[VM] * 11, out_specs=[VM] * 6, scratch_shapes=[pltpu.VMEM((r, w), bf16)], compiler_params=params(), name="cross_backward")(
            hid3, gain3, g, part, other, wo, wq, q, k, v, lse)


def self_backward(hid2, gain2, g, part, other, wo, wi, q, k, v, lse):
    def kernel(hid2, gain2, g, part, other, wo, wi, q, k, v, lse, g_out, e, dq, dk, dv, back, do):
        g_out[...] = g[...] + norm_back(hid2[...], gain2[...], part[...] + other[...])
        e[...] = g_out[...].astype(bf16)
        do[...] = nt(e[...], wo[...]).astype(bf16)
        attend_backward(q, k, v, do, lse, dq, dk, dv, q.shape[0], True)
        back[...] = nt(dq[...], wi[0])
        back[...] += nt(dk[...], wi[1])
        back[...] += nt(dv[...], wi[2])

    r, d = hid2.shape
    w = q.shape[1]
    return pl.pallas_call(kernel, out_shape=[sds((r, d), f32), sds((r, d), bf16)] + [sds((r, w), bf16)] * 3 + [sds((r, d), f32)],
        in_specs=[VM] * 11, out_specs=[VM] * 6, scratch_shapes=[pltpu.VMEM((r, w), bf16)], compiler_params=params(), name="self_backward")(
            hid2, gain2, g, part, other, wo, wi, q, k, v, lse)


def final_norm(hid, gain, g, part, other):
    def kernel(hid, gain, g, part, other, out):
        out[...] = (g[...] + norm_back(hid[...].astype(f32), gain[...], part[...] + other[...])).astype(bf16)

    return pl.pallas_call(kernel, out_shape=sds(hid.shape, bf16), in_specs=[VM] * 5, out_specs=VM, compiler_params=params(), name="final_norm")(hid, gain, g, part, other)


def memory_backward(dk, dv, wi, frames):
    def kernel(dk, dv, wi, out):
        out[...] = (nt(dk[:frames], wi[0]) + nt(dv[:frames], wi[1])).astype(bf16)
    d = wi.shape[1]
    return pl.pallas_call(kernel, out_shape=sds((frames, d), bf16), in_specs=[VM] * 3, out_specs=VM, compiler_params=params(), name="memory_backward")(dk, dv, wi)


def attention_ranks(normed, source, mix, dq, dk, dv, e, a_in, b_in, a_out, b_out):
    def kernel(*refs):
        operands, results = refs[:-4], refs[-4:]
        given = operands[:7] if source is not None else operands[:1] + operands[:1] + operands[1:6]
        normed, source_, mix, dq, dk, dv, e = given
        a_in, b_in, a_out, b_out = operands[-4:]
        ga_in, gb_in, ga_out, gb_out = results
        for i, (u, g) in enumerate(((normed, dq), (source_, dk), (source_, dv))):
            rows = u.shape[0]
            inner = rank_t(a_in[i], u[...])
            back = rank_t(b_in[i], g[:rows])
            gb_in[i] = nn(inner, g[:rows]).astype(bf16)
            ga_in[i] = nn(back, u[...]).astype(bf16)
        ga_out[...] = nn(rank_t(b_out[...], e[...]), mix[...]).astype(bf16)
        gb_out[...] = nn(rank_t(a_out[...], mix[...]), e[...]).astype(bf16)

    args = [normed] + ([source] if source is not None else []) + [mix, dq, dk, dv, e, a_in, b_in, a_out, b_out]
    return pl.pallas_call(kernel, out_shape=[sds(t.shape, bf16) for t in (a_in, b_in, a_out, b_out)],
        in_specs=[VM] * len(args), out_specs=[VM] * 4, compiler_params=params(), name="attention_ranks")(*args)


OFFS = (2, 4, 6, 8, 10)


class Unit:
    def __init__(self, place, kind, index):
        self.place, self.tall, self.index = place, kind == "a", index
        self.rows = 512 if self.tall else 128
        late = place >= 10
        if self.tall:
            self.most, self.via_y = (496, 400) if late else (400, 304)
        else:
            self.most, self.via_y = (112, 96) if late else (96, 80)


def make_units():
    order = [("a", 0), ("a", 1), ("a", 2), ("b", 0), ("a", 3), ("a", 4), ("a", 5), ("b", 1)]
    for j in range(4):
        order += [("a", 6 + j), ("b", 2 + j)]
    return [Unit(i, kind, index) for i, (kind, index) in enumerate(order)]


def layer_kernel(
    tok, enc, cot, w_in, w_out, w_up, w_down, ids, gain, shift,
    d_ai, u_ai, d_fi, u_fi, d_ao, u_ao, d_fo, u_fo,
    acts, g_tok, g_enc, split_sum, whole_sum,
    ga, gb, rows, grads, memory, normed, q0, k0, v0, mix, q1, k1, v1, lse, hidden, g_now, dd, dkv,
    outbox, inbox, idbuf, rs, rw, ys, yw, ys_own, yw_own, fz, fw, r_in, t_out, r_up, gsplit, gwhole, wz, dsum,
    rwb0, rwb1, rwb2, czs0, czs1, czs2, czw0, czw1, czw2, sb0, sb1, sb2, yb0, yb1, yb2, xb0, xb1, xb2, cb0, cb1, cb2,
    core_s, core_r, up_s, dn_s, z_r, y_s, y_r, x_s, x_r, row_s, row_r, loc, ad_s, ad_r, ex_s, ex_r, b_s, b_r, home_s, home_r,
):
    units = make_units()
    count = len(units)
    frames, groups = 1500 * enc.shape[1] // 1536, 4
    do, dq = dd.at[0], dd.at[1]
    x, y, c, z = (lax.axis_index(a) for a in ("rep", "sh", "core", "tp"))
    al = pl.multiple_of
    sent = {}

    def when(cond, fn):
        fn() if cond is None else pl.when(cond)(fn)

    def remote(src, dst, s, r, dev):
        return pltpu.make_async_remote_copy(
            src_ref=src, dst_ref=dst, send_sem=s, recv_sem=r, device_id=dev, device_id_type=MESH
        )

    def send(key, cond, src, dst, s, r, dev):
        when(cond, lambda: remote(src, dst, s, r, dev).start())
        sent.setdefault(key, []).append((cond, lambda: remote(src, dst, s, r, dev).wait_send()))

    def settle(key):
        for cond, fn in sent.pop(key, []):
            when(cond, fn)

    X, Y, C = {"rep": 1 - x}, {"sh": 1 - y}, {"core": 1 - c}
    YC = {"sh": 1 - y, "core": 1 - c}
    UP, DOWN = {"tp": z + 1}, {"tp": z - 1}
    others = [lax.rem(z + k, 4) for k in (1, 2, 3)]

    def got(dst, r):
        remote(dst, dst, r, r, X).wait_recv()

    bar = pltpu.get_barrier_semaphore()
    for dev in [X, Y, C, YC] + [{"tp": j} for j in others] + [{"tp": j, "core": 1 - c} for j in others]:
        pl.semaphore_signal(bar, inc=1, device_id=dev, device_id_type=MESH)
    pl.semaphore_wait(bar, 10)

    def block(u, yy, zz, first, size):
        if u.tall:
            return ga.at[pl.ds(al(u.index * 1024 + yy * 512 + first, 16), size), pl.ds(al(zz * 128, 128), 128)]
        return gb.at[u.index, zz, pl.ds(al(first, 16), size), pl.ds(al(yy * 512, 512), 512)]

    def across(u, yy, first, size):
        if u.tall:
            return ga.at[pl.ds(al(u.index * 1024 + yy * 512 + first, 16), size)]
        return gb.at[u.index, :, pl.ds(al(first, 16), size), pl.ds(al(yy * 512, 512), 512)]

    def three(u, first, size):
        if u.tall:
            return ga.at[pl.ds(al(u.index * 1024 + y * 512 + first, 16), size), 0:384]
        return gb.at[u.index, 0:3, pl.ds(al(first, 16), size), pl.ds(al(y * 512, 512), 512)]

    def half_src(u, cc):
        m = u.index
        if u.tall:
            if m < 6:
                return w_in.at[m, :, pl.ds(al(cc * 128, 128), 128)]
            return w_up.at[:, pl.ds(al(cc * 512 + (m - 6) * 128, 128), 128)]
        if m < 2:
            return w_out.at[m, pl.ds(al(cc * 128, 128), 128)]
        return w_down.at[pl.ds(al(cc * 512 + (m - 2) * 128, 128), 128)]

    def half_dst(u, cc):
        if u.tall:
            return block(u, y, z, cc * 256, 256)
        return gb.at[u.index, z, :, pl.ds(al(y * 512 + cc * 256, 256), 256)]

    def core_exchange(u):
        i = u.place
        send("core", None, half_src(u, 1 - c), half_dst(u, c), core_s.at[i], core_r.at[i], C)
        pltpu.make_async_copy(half_src(u, c), half_dst(u, c), loc.at[i]).start()

    def to_y(u, j):
        b = block(u, y, j, x * (u.rows - u.via_y), u.via_y)
        remote(b, b, y_s.at[u.place], y_r.at[u.place], Y).start()

    def own(u):
        i = u.place
        got(half_dst(u, 1 - c), core_r.at[i])
        pltpu.make_async_copy(half_src(u, c), half_dst(u, c), loc.at[i]).wait()
        zb = block(u, y, z, x * (u.rows - u.most), u.most)
        send(i, z < 3, zb, zb, up_s.at[i, z], z_r.at[i, z], UP)
        send(i, z > 0, zb, zb, dn_s.at[i, z], z_r.at[i, z], DOWN)
        to_y(u, z)

    def hop(u, k):
        i = u.place
        ways = (
            (z >= k, z - k, (z >= k) & (z < 3), UP, up_s),
            (z + k <= 3, z + k, (z + k <= 3) & (z > 0), DOWN, dn_s),
        )
        for ok, j, more, dev, sems in ways:
            zb = block(u, y, j, x * (u.rows - u.most), u.most)

            def arrive(zb=zb, j=j):
                got(zb, z_r.at[i, j])
                to_y(u, j)
                b = block(u, y, j, x * u.most, u.rows - u.most)
                remote(b, b, x_s.at[i, 0], x_r.at[i, 0], X).start()

            when(ok, arrive)
            send(i, more, zb, zb, sems.at[i, j], z_r.at[i, j], dev)

    def cross(u):
        i = u.place
        got(across(u, 1 - y, x * (u.rows - u.via_y), u.via_y), y_r.at[i])
        b = across(u, 1 - y, x * u.via_y, u.rows - u.via_y)
        send(i, None, b, b, x_s.at[i, 1], x_r.at[i, 1], X)

    def last(u):
        i = u.place
        got(three(u, (1 - x) * u.most, u.rows - u.most), x_r.at[i, 0])
        got(across(u, 1 - y, (1 - x) * u.via_y, u.rows - u.via_y), x_r.at[i, 1])
        b = across(u, y, x * (u.rows - u.via_y), u.via_y)
        remote(b, b, y_s.at[i], y_r.at[i], Y).wait_send()
        b = three(u, x * u.most, u.rows - u.most)
        remote(b, b, x_s.at[i, 0], x_r.at[i, 0], X).wait_send()
        settle(i)

    mine = c == z // 2

    def rows_out(src, dst, slot):
        for i in (0, 1):
            zd = 2 * c + i
            d = dst.at[pl.ds(al(z * 112, 16), 112)]
            send("rows", zd != z, src.at[i], d, row_s.at[slot, i], row_r.at[slot, z], {"tp": zd})
            when(
                zd == z,
                lambda i=i, d=d: pltpu.make_async_copy(src.at[i], d, loc.at[count + slot]).start(),
            )

    def rows_in(dst, slot):
        def wait():
            for j in others:
                got(dst.at[pl.ds(al(j * 112, 16), 112)], row_r.at[slot, j])
            d = dst.at[pl.ds(al(z * 112, 16), 112)]
            pltpu.make_async_copy(d, d, loc.at[count + slot]).wait()

        when(mine, wait)
        send("rows", mine, dst, dst, row_s.at[slot, 2], row_r.at[slot, 4], C)

    def rows_have(dst, slot):
        when(c != z // 2, lambda: got(dst, row_r.at[slot, 4]))

    parts = [slice(t * 96, (t + 1) * 96) for t in range(16)]

    def enc_local(t):
        return pltpu.make_async_copy(
            enc.at[lax.rem(z, 2), parts[t]], memory.at[parts[t]], loc.at[count + 2 + t]
        )

    def enc_send(t):
        send(
            "enc", mine, enc.at[lax.rem(z, 2), parts[t]], memory.at[parts[t]], row_s.at[2, t], row_r.at[2, t], C
        )
        when(mine, lambda: enc_local(t).start())

    def enc_have():
        for t in range(16):
            when(mine, lambda: enc_local(t).wait())
            when(c != z // 2, lambda: got(memory.at[parts[t]], row_r.at[2, t]))

    me = 2 * y + c

    def ids_out():
        for k, dev in enumerate((C, Y, YC)):
            send("ids", None, ids, idbuf.at[me], ad_s.at[k], ad_r.at[k], dev)
        idbuf[pl.ds(me, 1)] = ids[...][None]

    def adapters_pick():
        for k, s in enumerate((2 * y + 1 - c, 2 * (1 - y) + c, 2 * (1 - y) + 1 - c)):
            got(idbuf.at[s], ad_r.at[k])
        held = lax.broadcasted_iota(jnp.int32, (128, 32), 1) + me * 32
        rank = lax.rem(lax.broadcasted_iota(jnp.int32, (128, 32), 0), 16)
        lines = [
            [jnp.broadcast_to(idbuf[2 * s + k // 2, k % 2 : k % 2 + 1, :32], (16, 32)) for k in range(4)]
            for s in range(2)
        ]
        wanted = jnp.concatenate([line for pair in lines for line in pair])
        target = held.astype(f32) - rank.astype(f32)
        picks = jnp.where(wanted * 16.0 == target, 1.0, 0.0).astype(bf16)
        here = []
        for s in range(2):
            line = lines[s][0]
            for k in (1, 2, 3):
                line = jnp.where(z == k, lines[s][k], line)
            here.append(line)
        picks_z = jnp.where(jnp.concatenate(here) * 16.0 == target[:32], 1.0, 0.0).astype(bf16)
        for h in range(2):
            cols = slice(h * 128, h * 128 + 128)
            wide = slice(h * 512, h * 512 + 512)
            given = [u_ai[m][:, cols] for m in range(6)] + [u_fi[:, wide]]
            given += [d_ao[m][:, cols] for m in range(2)] + [d_fo[:, wide]]
            for b in range(4):
                block_of = jnp.concatenate(given, axis=1)[:, b * 512 : b * 512 + 512]
                dkv[h, b * 128 : b * 128 + 128] = nn(picks, block_of).astype(bf16)
            if h == 0:
                given = [d_ai[m] for m in range(5)]
            else:
                given = [d_ai[5], d_fi, u_ao[0], u_ao[1], u_fo]
            for b in range(10):
                block_of = given[b // 2][:, b % 2 * 512 : b % 2 * 512 + 512]
                dd[h, b * 32 : b * 32 + 32] = nn(picks_z, block_of).astype(bf16)
        send("pick", None, dkv.at[1 - c], rs, ad_s.at[3], ad_r.at[3], C)
        send("pick", None, dd.at[1 - c, 0:320], rw, ad_s.at[4], ad_r.at[4], C)

    def adapters_y():
        got(rs, ad_r.at[3])
        got(rw, ad_r.at[4])
        rs[...] += dkv[pl.ds(c, 1)][0]
        rw[...] += dd[pl.ds(c, 1), 0:320][0]
        for b in range(4):
            for k in range(2):
                ys_own[k, :, b * 512 : b * 512 + 512] = rs[b * 128 + k * 64 : b * 128 + k * 64 + 64]
        for b in range(10):
            for k in range(2):
                yw_own[k, :, b * 512 : b * 512 + 512] = rw[b * 32 + k * 16 : b * 32 + k * 16 + 16]
        send("pick", None, ys_own.at[1 - y], ys, ad_s.at[5], ad_r.at[5], Y)
        send("pick", None, yw_own.at[1 - y], yw, ad_s.at[6], ad_r.at[6], Y)

    def adapters_z():
        got(ys, ad_r.at[5])
        got(yw, ad_r.at[6])
        ys[...] += ys_own[pl.ds(y, 1)][0]
        fw[pl.ds(c, 1)] = (yw[...] + yw_own[pl.ds(y, 1)][0])[None]
        for k, j in enumerate(others):
            send("pick", None, ys.at[pl.ds(al(j * 16, 16), 16)], fz.at[z], ad_s.at[7 + k], ad_r.at[7 + z], {"tp": j})
        fz[pl.ds(z, 1)] = ys[pl.ds(al(z * 16, 16), 16)][None]
        send("pick", None, fw.at[c], fw.at[c], ad_s.at[11], ad_r.at[11], C)

    def adapters_have():
        for j in others:
            got(fz.at[j], ad_r.at[7 + j])
        got(fw.at[1 - c], ad_r.at[11])
        settle("pick")
        settle("ids")

    def whole(m):
        return fw[m // 5, :, (m % 5) * 1024 : (m % 5) * 1024 + 1024]

    def split(s):
        return jnp.concatenate([fz[k, :, s * 128 : s * 128 + 128] for k in range(4)], axis=1)

    def merge(u):
        m = u.index
        if u.tall:
            down_t = whole(min(m, 6)).T
            up_rows = split(m)
            for b in range(4):
                place = slice(m * 1024 + b * 256, m * 1024 + b * 256 + 256)
                ga[place] = (ga[place].astype(f32) + nn(down_t[b * 256 : b * 256 + 256], up_rows)).astype(bf16)
        else:
            down_t = split(10 + m).T
            up_rows = whole(7 + m if m < 2 else 9)
            for k in range(4):
                gb[m, k] = (gb[m, k].astype(f32) + nn(down_t[k * 128 : k * 128 + 128], up_rows)).astype(bf16)

    def wa(m):
        return ga[m * 1024 : (m + 1) * 1024]

    def wb(m):
        return gb[m].reshape(512, 1024)

    def part_out(e, slot):
        send(("part", e), None, outbox.at[slot], inbox.at[slot], ex_s.at[e], ex_r.at[e], C)

    def part_sum(e, slot):
        got(inbox.at[slot], ex_r.at[e])
        return outbox[slot] + inbox[slot]

    def norm_rows(side, source):
        unit, _ = normalize(source)
        normed[side] = (unit * gain[side] + shift[side]).astype(bf16)

    def start_rows():
        rows_have(rows, 0)
        norm_rows(0, rows[...].astype(f32))

    def project(m, source, out, length):
        def run():
            out[:length] = nn(source(), wa(m)).astype(bf16)
        return run

    def attention(side, first, number):
        q, k, v = ((q0, k0, v0), (q1, k1, v1))[side]
        length = (rows.shape[0], frames)[side]
        return lambda: attend_forward(q, k, v, mix.at[side], lse.at[side], length, side == 0, first, number, groups)

    def part0():
        outbox[0] = nn(mix[0], wb(0))
        part_out(0, 0)

    def second_rows():
        hidden[0] = rows[...].astype(f32) + part_sum(0, 0)
        norm_rows(1, hidden[0])

    def part1():
        outbox[1] = nn(mix[1], wb(1))
        part_out(1, 1)

    def third_rows():
        hidden[1] = hidden[0] + part_sum(1, 1)
        norm_rows(2, hidden[1])
        rows_have(grads, 1)

    def feed_first():
        settle(("part", 0))
        settle(("part", 1))
        r_up[0] = rank_t(whole(6), normed[2])
        r_up[1] = rank_t(whole(9), grads[...])

    def chunk(j):
        def run():
            up, down = wa(6 + j), wb(2 + j)
            pre = nn(normed[2], up)
            cdf = 0.5 * (1.0 + lax.erf(pre * (2**-0.5)))
            active = (pre * cdf).astype(bf16)
            slope = cdf + pre * jnp.exp(-0.5 * pre * pre) * 0.3989422804014327
            grad = (nt(grads[...], down) * slope).astype(bf16)
            if j == 0:
                outbox[1] = nn(active, down)
                outbox[0] = nt(grad, up)
                r_in[...] = nt(split(6 + j), grad)
                t_out[...] = nt(split(12 + j), active)
            else:
                outbox[1] += nn(active, down)
                outbox[0] += nt(grad, up)
                r_in[...] += nt(split(6 + j), grad)
                t_out[...] += nt(split(12 + j), active)
            gsplit[j] = nn(r_up[0], grad).astype(bf16)
            gsplit[4 + j] = nn(r_up[1], active).astype(bf16)
        return run

    tasks = {}

    def task(tick, fn):
        tasks.setdefault(tick, []).append(fn)

    task(1, adapters_pick)
    task(4, adapters_y)
    task(8, adapters_z)
    task(12, adapters_have)
    task(12, lambda: rows_in(rows, 0))
    first = 13
    task(first, start_rows)
    for u in units:
        task(max(first, 2 * u.place + OFFS[4]), functools.partial(merge, u))
    for tick, fn in (
        (first + 1, project(0, lambda: normed[0], q0, 448)),
        (first + 2, project(1, lambda: normed[0], k0, 448)),
        (first + 2, project(2, lambda: normed[0], v0, 448)),
        (first + 3, attention(0, 0, 2)),
        (first + 4, attention(0, 2, 2)),
        (first + 5, part0),
        (first + 7, second_rows),
        (first + 7, project(3, lambda: normed[1], q1, 448)),
        (first + 8, enc_have),
        (first + 8, project(4, lambda: memory[...], k1, 1536)),
        (first + 10, project(5, lambda: memory[...], v1, 1536)),
        (first + 11, attention(1, 0, 1)),
        (first + 12, attention(1, 1, 1)),
        (first + 13, attention(1, 2, 1)),
        (first + 14, attention(1, 3, 1)),
        (first + 15, part1),
        (first + 17, third_rows),
        (first + 17, feed_first),
        (12, lambda: rows_out(cot, grads, 1)),
        (22, lambda: rows_in(grads, 1)),
    ):
        task(tick, fn)
    for j in range(4):
        task(max(first + 18 + j, 2 * (9 + 2 * j) + OFFS[4] + 1), chunk(j))

    ids_out()
    rows_out(tok, rows, 0)
    for u in units:
        core_exchange(u)
    for t in range(max(2 * count + OFFS[4], max(tasks)) + 1):
        def at(offset):
            i, odd = divmod(t - offset, 2)
            return units[i] if not odd and 0 <= i < count else None

        if t == 0:
            own(units[0])
        if at(-2):
            own(at(-2))
        for k in (1, 2, 3):
            if at(OFFS[k - 1]):
                hop(at(OFFS[k - 1]), k)
        if at(OFFS[3]):
            cross(at(OFFS[3]))
        if at(OFFS[4]):
            last(at(OFFS[4]))
        if t < 16:
            enc_send(t)
        for fn in tasks.get(t, []):
            fn()

    boxes = list(
        zip(
            (rwb0, rwb1, rwb2), (czs0, czs1, czs2), (czw0, czw1, czw2), (sb0, sb1, sb2), (yb0, yb1, yb2),
            (xb0, xb1, xb2), (cb0, cb1, cb2), ((0, 8, 0, 1), (8, 4, 2, 2), (12, 4, 6, 2)), strict=True,
        )
    )

    def home_core(b):
        rwb, first, half = boxes[b][0], boxes[b][7][2], boxes[b][7][3]
        send(("home", b), None, gwhole.at[pl.ds(first + (1 - c) * half, half)], rwb, b_s.at[b, 0], b_r.at[b, 0], C)

    def home_z(b):
        rwb, czs, czw = boxes[b][:3]
        s0, ns, first, half = boxes[b][7]
        got(rwb, b_r.at[b, 0])
        rwb[...] += gwhole[pl.ds(first + c * half, half)]

        def cuts(j):
            return gsplit.at[s0 : s0 + ns, :, pl.ds(al(j * 128, 128), 128)], rwb.at[:, :, pl.ds(al(j * 256, 256), 256)]

        for k, j in enumerate(others):
            one, two = cuts(j)
            send(("home", b), None, one, czs.at[z], b_s.at[b, 1 + k], b_r.at[b, 1 + z], {"tp": j})
            send(("home", b), None, two, czw.at[z], b_s.at[b, 5 + k], b_r.at[b, 5 + z], {"tp": j})
        one, two = cuts(z)
        czs[pl.ds(z, 1)] = one[...][None]
        czw[pl.ds(z, 1)] = two[...][None]

    def dense_rows(b, to):
        czs, czw, (_, ns, _, half) = boxes[b][1], boxes[b][2], boxes[b][7]
        stack = jnp.concatenate(
            [jnp.concatenate([czs[k, s] for s in range(ns)] + [czw[k, w] for w in range(half)], axis=1) for k in range(4)]
        )
        row = lax.broadcasted_iota(jnp.int32, (64, 64), 0)
        col = lax.broadcasted_iota(jnp.int32, (64, 64), 1)
        clip = col // 16
        chosen = jnp.zeros((64, 64), f32)
        for k in range(4):
            line = idbuf[pl.ds(2 * y + k // 2, 1), k % 2 : k % 2 + 1, :64][0]
            chosen = jnp.where(clip == k, jnp.broadcast_to(line, (64, 64)), chosen)
        target = (row + 64 * to - lax.rem(col, 16)).astype(f32)
        return nn(jnp.where(chosen * 16.0 == target, 1.0, 0.0).astype(bf16), stack)

    def home_y(b):
        _, czs, czw, sb, yb = boxes[b][:5]
        for j in others:
            got(czs.at[j], b_r.at[b, 1 + j])
            got(czw.at[j], b_r.at[b, 5 + j])
        sb[...] = dense_rows(b, 1 - y).astype(bf16)
        send(("home", b), None, sb, yb, b_s.at[b, 9], b_r.at[b, 9], Y)

    def home_x(b):
        yb, xb = boxes[b][4:6]
        got(yb, b_r.at[b, 9])
        yb[...] = (dense_rows(b, y) + yb[...].astype(f32)).astype(bf16)
        send(("home", b), None, yb, xb, b_s.at[b, 10], b_r.at[b, 10], X)

    def home_rows(b):
        yb, xb, cb = boxes[b][4:7]
        got(xb, b_r.at[b, 10])
        xb[...] += yb[...]
        send(("home", b), None, xb.at[pl.ds(al((1 - c) * 32, 32), 32)], cb, b_s.at[b, 11], b_r.at[b, 11], C)

    def home_last(b):
        xb, cb = boxes[b][5:7]
        s0, ns, first, half = boxes[b][7]
        got(cb, b_r.at[b, 11])
        here, there = xb[pl.ds(al(c * 32, 32), 32)].astype(f32), cb[...].astype(f32)
        low, high = jnp.where(c == 0, here, there), jnp.where(c == 0, there, here)
        for s in range(ns):
            lanes = slice(s * 128, s * 128 + 128)
            split_sum[s0 + s] = jnp.concatenate([low[:, lanes], high[:, lanes]], axis=1)
        for w in range(half):
            lanes = slice(ns * 128 + w * 256, ns * 128 + w * 256 + 256)
            for q in range(4):
                wz[q, first + w] = low[q * 8 : q * 8 + 8, lanes]
                wz[q, first + half + w] = high[q * 8 : q * 8 + 8, lanes]
        slots = pl.ds(first, 2 * half)
        for k, j in enumerate(others):
            send(("home", b), None, wz.at[j, slots], whole_sum.at[z, slots], b_s.at[b, 12 + k], b_r.at[b, 12 + z], {"tp": j})
        pltpu.make_async_copy(wz.at[z, slots], whole_sum.at[z, slots], loc.at[count + 18 + b]).start()

    def home_done(b):
        first, half = boxes[b][7][2:]
        slots = pl.ds(first, 2 * half)
        for j in others:
            got(whole_sum.at[j, slots], b_r.at[b, 12 + j])
        pltpu.make_async_copy(wz.at[z, slots], whole_sum.at[z, slots], loc.at[count + 18 + b]).wait()

    def rows_back(src, dst, slot):
        def go():
            for k, j in enumerate(others):
                part = src.at[pl.ds(al(j * 112, 16), 112)]
                remote(part, dst.at[lax.rem(z, 2)], home_s.at[slot, k], home_r.at[slot, z], {"tp": j}).start()
            own_part(src, dst, slot).start()

        when(mine, go)

    def own_part(src, dst, slot):
        part = src.at[pl.ds(al(z * 112, 16), 112)]
        return pltpu.make_async_copy(part, dst.at[lax.rem(z, 2)], loc.at[count + 21 + slot])

    def rows_back_done(src, dst, slot):
        def go():
            for k, j in enumerate(others):
                part = src.at[pl.ds(al(j * 112, 16), 112)]
                remote(part, part, home_s.at[slot, k], home_r.at[slot, z], {"tp": j}).wait_send()
            own_part(src, dst, slot).wait()

        when(mine, go)
        for i in (0, 1):
            source = 2 * c + i
            when(source != z, lambda: got(dst.at[i], home_r.at[slot, source]))

    def enc_dst(quarter_of):
        return g_enc.at[lax.rem(z, 2), :, :, pl.ds(al(c * 512, 512), 512)]

    def enc_copy(j):
        part = gb.at[2 + j, 0:3, :, 0:512]
        owner = z // 2
        sems = home_s.at[2, j], home_r.at[2 + c, z]
        return part, owner, sems

    def enc_back(j):
        part, owner, (s, r) = enc_copy(j)
        when((j != z) | (c != owner), lambda: remote(part, enc_dst(j), s, r, {"tp": j, "core": owner}).start())
        when((j == z) & (c == owner), lambda: pltpu.make_async_copy(part, enc_dst(j), loc.at[count + 23]).start())

    def enc_back_done():
        for step in range(4):
            j = lax.rem(z + 1 + step, 4)
            part, owner, (s, r) = enc_copy(j)
            when((j != z) | (c != owner), lambda: remote(part, enc_dst(j), s, r, {"tp": j, "core": owner}).wait_send())
            when((j == z) & (c == owner), lambda: pltpu.make_async_copy(part, enc_dst(j), loc.at[count + 23]).wait())
        for i in (0, 1):
            for other in (0, 1):
                source = 2 * c + i
                when(
                    (source != z) | (c != other),
                    lambda: got(g_enc.at[i, :, :, other * 512 : other * 512 + 512], home_r.at[2 + other, source]),
                )

    def rank_pair(side, i, u, g):
        s0, w0 = (12, 6) if side == 0 else (8, 2)
        m = 3 * side + i
        inner = rank_t(whole(m), u[...])
        back = rank_t(split(m), g[...])
        gsplit[s0 + i] = nn(inner, g[...]).astype(bf16)
        gwhole[w0 + i] = nn(back, u[...]).astype(bf16)

    def rank_out(side):
        s0, w0 = (12, 6) if side == 0 else (8, 2)
        gsplit[s0 + 3] = nn(rank_t(whole(7 + side), grads[...]), mix[side]).astype(bf16)
        gwhole[w0 + 3] = nn(rank_t(split(10 + side), mix[side]), grads[...]).astype(bf16)

    def memory_half(h, q):
        rows_of = [pl.ds(al(m * 1024 + h * 512, 512), 512) for m in (4, 5)]
        place = pl.ds(al(q * 384, 128), 384)
        return nt(dk1[place], ga[rows_of[0]]) + nt(dv1[place], ga[rows_of[1]])

    def accumulator(p):
        return outbox.at[0, pl.ds(al(p // 2 * 128, 128), 128), pl.ds(al(lax.rem(p, 2) * 512, 512), rows.shape[0])]

    def cross_start():
        head = lax.broadcasted_iota(jnp.int32, (8, 128), 1) // HD
        pick_head = jnp.where(head == lax.broadcasted_iota(jnp.int32, (8, 128), 0), 1.0, 0.0).astype(bf16)

        def pair(p, carry):
            lanes = pair_lanes(p)
            both = do[:, lanes].astype(f32) * mix[1, :, lanes].astype(f32)
            high = both.astype(bf16)
            dsum[p] = nt(pick_head, high) + nt(pick_head, (both - high.astype(f32)).astype(bf16))
            accumulator(p)[...] = jnp.zeros((128, rows.shape[0]), f32)
            return carry

        lax.fori_loop(0, 4, pair, 0)

    def cross_block(q):
        place = pl.ds(al(q * 384, 128), 384)

        def pair(p, carry):
            lanes = pair_lanes(p)
            qp, dop = q1[:, lanes], do[:, lanes]
            kp, vp = k1[place, lanes], v1[place, lanes]
            kt = kp.T
            logs, totals = lse[1, p], dsum[p]
            first = lax.broadcasted_iota(jnp.int32, qp.shape, 1) < HD
            dqs, dks, dvs = [], [], []
            for h in (0, 1):
                this = first == (h == 0)
                sc = scores_t(kp, jnp.where(this, qp, 0), frames // groups, False)
                probs = jnp.exp(sc - logs[h : h + 1])
                dvs.append(nn(probs.astype(bf16), dop))
                dp = nt(vp, jnp.where(this, dop, 0))
                ds = (probs * (dp - totals[h : h + 1])).astype(bf16)
                dks.append(nn(ds, qp))
                dqs.append(nn(kt, ds)[h * HD : (h + 1) * HD])
            first_k = lax.broadcasted_iota(jnp.int32, kp.shape, 1) < HD
            dv1[place, lanes] = jnp.where(first_k, dvs[0], dvs[1]).astype(bf16)
            dk1[place, lanes] = (jnp.where(first_k, dks[0], dks[1]) * SCALE).astype(bf16)
            accumulator(p)[...] += jnp.concatenate(dqs)
            return carry

        lax.fori_loop(0, 4, pair, 0)

    def cross_end():
        def pair(p, carry):
            dq[:, pair_lanes(p)] = (accumulator(p)[...].T * SCALE).astype(bf16)
            return carry

        lax.fori_loop(0, 4, pair, 0)

    def enc_part(step):
        q = lax.rem(z + 1 + step, 4)
        sent_part = gb.at[2 + q, 0:3, :, 512:1024]
        sent_part[...] = memory_half(1 - c, q).astype(bf16).reshape(3, 128, 512)
        send("enc", None, sent_part, gb.at[2 + q, 0:3, :, 0:512], ex_s.at[6 + step], ex_r.at[6 + step], C)

    def enc_whole(step):
        q = lax.rem(z + 1 + step, 4)
        kept = gb.at[2 + q, 0:3, :, 0:512]
        got(kept, ex_r.at[6 + step])
        kept[...] = (memory_half(c, q).reshape(3, 128, 512) + kept[...].astype(f32)).astype(bf16)
        enc_back(q)

    dk1, dv1 = ga.at[pl.ds(6144, 1536)], ga.at[pl.ds(7680, 1536)]
    dk0, dv0 = dkv.at[0, 0:448], dkv.at[1, 0:448]
    part_out(3, 0)
    gwhole[0] = nn(r_in[...].astype(bf16), normed[2]).astype(bf16)
    gwhole[1] = nn(t_out[...].astype(bf16), grads[...]).astype(bf16)
    home_core(0)
    g_now[...] = grads[...].astype(f32) + norm_back(hidden[1], gain[2], part_sum(3, 0))
    part_out(2, 1)
    settle("rows")
    grads[...] = g_now[...].astype(bf16)
    do[...] = nt(grads[...], wb(1)).astype(bf16)
    home_z(0)
    settle(("part", 3))
    cross_start()
    cross_block(lax.rem(z + 1, 4))
    enc_part(0)
    cross_block(lax.rem(z + 2, 4))
    enc_part(1)
    enc_whole(0)
    normed[2] = (hidden[1] + part_sum(2, 1)).astype(bf16)
    rows_back(normed.at[2], acts, 0)
    home_y(0)
    cross_block(lax.rem(z + 3, 4))
    enc_part(2)
    enc_whole(1)
    rank_out(1)
    cross_block(z)
    cross_end()
    outbox[0] = nt(dq[...], wa(3))
    part_out(4, 0)
    enc_part(3)
    enc_whole(2)
    home_x(0)
    g_now[...] += norm_back(hidden[0], gain[1], part_sum(4, 0))
    grads[...] = g_now[...].astype(bf16)
    do[...] = nt(grads[...], wb(0)).astype(bf16)
    enc_whole(3)
    rank_pair(1, 0, normed.at[1], dq)
    home_rows(0)
    attend_backward(q0, k0, v0, do, lse.at[0], dq, dk0, dv0, rows.shape[0], True)
    settle(("part", 2))
    outbox[1] = nt(dq[...], wa(0))
    outbox[1] += nt(dk0[...], wa(1))
    outbox[1] += nt(dv0[...], wa(2))
    part_out(5, 1)
    home_last(0)
    rank_pair(0, 0, normed.at[0], dq)
    rank_pair(0, 1, normed.at[0], dk0)
    rank_pair(0, 2, normed.at[0], dv0)
    rank_out(0)
    home_core(2)
    normed[0] = (g_now[...] + norm_back(rows[...].astype(f32), gain[0], part_sum(5, 1))).astype(bf16)
    rows_back(normed.at[0], g_tok, 1)
    home_z(2)
    rank_pair(1, 1, memory, dk1)
    rank_pair(1, 2, memory, dv1)
    home_core(1)
    home_y(2)
    home_z(1)
    home_x(2)
    home_y(1)
    home_rows(2)
    home_x(1)
    home_last(2)
    home_rows(1)
    home_last(1)
    for b in range(3):
        home_done(b)
    rows_back_done(normed.at[2], acts, 0)
    rows_back_done(normed.at[0], g_tok, 1)
    enc_back_done()
    for key in list(sent):
        settle(key)


def layer(tok, enc, cot, w_in, w_out, w_up, w_down, ids, gain, shift, *adapters):
    any_ = pl.BlockSpec(memory_space=pl.ANY)
    r, d = 448, tok.shape[2]
    padded = enc.shape[1]
    dma = pltpu.SemaphoreType.DMA

    def vm(*shape, dtype=bf16):
        return pltpu.VMEM(shape, dtype)

    n = 16
    halves = (1, 2, 2)
    splits = (8, 4, 4)
    widths = [s * 128 + w * 256 for s, w in zip(splits, halves, strict=True)]
    return pl.pallas_call(
        layer_kernel,
        out_shape=[
            sds((2, r // 4, d), bf16), sds((2, r // 4, d), bf16), sds((2, 3, padded // 12, d), bf16),
            sds((16, 32, 256), f32), sds((4, 10, 8, 256), f32),
        ],
        in_specs=[any_] * 7 + [VM] * 11,
        out_specs=[any_] * 3 + [VM, any_],
        scratch_shapes=[
            vm(10 * d, 512), vm(6, 4, 128, d), vm(r, d), vm(r, d), vm(padded, d), vm(3, r, d),
            vm(r, 512), vm(r, 512), vm(r, 512), vm(2, r, 512), vm(r, 512), vm(padded, 512), vm(padded, 512),
            vm(2, 4, 2, r, dtype=f32), vm(2, r, d, dtype=f32), vm(r, d, dtype=f32), vm(2, r, 512), vm(2, 512, 512),
            vm(2, r, d, dtype=f32), vm(2, r, d, dtype=f32),
            vm(4, 8, 128, dtype=f32), vm(512, 512), vm(320, 512), vm(64, 2048), vm(16, 5120), vm(2, 64, 2048), vm(2, 16, 5120),
            vm(4, 16, 2048), vm(2, 16, 5120), vm(16, r, dtype=f32), vm(16, r, dtype=f32), vm(2, 16, r),
            vm(16, 16, 512), vm(10, 16, d), vm(4, 10, 8, 256, dtype=f32), vm(4, 8, r, dtype=f32),
            *[vm(w, 16, d) for w in halves], *[vm(4, s, 16, 128) for s in splits], *[vm(4, w, 16, 256) for w in halves],
            *[vm(64, w) for w in widths], *[vm(64, w) for w in widths], *[vm(64, w) for w in widths], *[vm(32, w) for w in widths],
            dma((n,)), dma((n,)), dma((n, 4)), dma((n, 4)), dma((n, 4)), dma((n,)), dma((n,)), dma((n, 2)), dma((n, 2)),
            dma((3, 16)), dma((3, 16)), dma((n + 24,)), dma((12,)), dma((12,)), dma((10,)), dma((10,)),
            dma((3, 16)), dma((3, 16)), dma((4, 4)), dma((4, 4)),
        ],
        compiler_params=pltpu.CompilerParams(
            collective_id=1, has_side_effects=True, vmem_limit_bytes=int(62.5 * 1024 * 1024)
        ),
        name="layer",
    )(tok, enc, cot, w_in, w_out, w_up, w_down, ids, gain, shift, *adapters)


def swap_core(rows):
    return lax.ppermute(rows, "core", SWAP)


def core_sum(part):
    return part + swap_core(part)


def own_and_other(stacked):
    core = lax.axis_index("core")
    keep = lax.dynamic_index_in_dim(stacked, core, 0, keepdims=False)
    send = lax.dynamic_index_in_dim(stacked, 1 - core, 0, keepdims=False)
    return keep, swap_core(send)


def in_core_order(own, other):
    first = lax.axis_index("core") == 0
    return jnp.stack([jnp.where(first, own, other), jnp.where(first, other, own)])


def scatter_sh(stacked):
    n = lax.axis_size("sh")
    if n == 2:
        me = lax.axis_index("sh")
        keep = lax.dynamic_index_in_dim(stacked, me, 0, keepdims=False)
        send = lax.dynamic_index_in_dim(stacked, 1 - me, 0, keepdims=False)
        return keep + lax.ppermute(send, "sh", SWAP)
    return lax.psum_scatter(stacked, "sh", scatter_dimension=0, tiled=False)


def over_z(stacked):
    return lax.all_to_all(stacked, "tp", 0, 0, tiled=True)


def half_columns(rows):
    width = rows.shape[-1] // 2
    return lax.dynamic_slice_in_dim(rows, lax.axis_index("core") * width, width, rows.ndim - 1)


def rows_home(half):
    tp = lax.axis_size("tp")
    moved = over_z(half.reshape(tp, half.shape[0] // tp, half.shape[1]))
    own, other = own_and_other(moved.reshape(2, tp // 2, *moved.shape[1:]))
    both = in_core_order(own, other)
    return jnp.moveaxis(both, 0, 2).reshape(both.shape[1], both.shape[2], 2 * half.shape[1])


def rows_here(rows):
    tp = lax.axis_size("tp")
    both = in_core_order(rows, swap_core(rows)).reshape(4, *rows.shape[1:])
    moved = over_z(half_columns(both))
    moved = moved.reshape(tp * rows.shape[1], rows.shape[2] // 2)
    pair = in_core_order(moved, swap_core(moved))
    return jnp.concatenate([pair[0], pair[1]], axis=-1)


def gather_weights(w_attn_in, w_attn_out, w_up, w_down):
    def over_shard(block, axis):
        return lax.all_gather(block, ("sh", "core"), axis=axis, tiled=True)

    def over_tp(block, axis):
        return lax.all_gather(block, "tp", axis=axis, tiled=True)

    core = lax.axis_index("core")

    def half(block, axis):
        width = block.shape[axis] // 2
        return lax.dynamic_slice_in_dim(block, core * width, width, axis)

    w_in = over_tp(half(over_shard(w_attn_in.reshape(6, *w_attn_in.shape[3:]), 1), 2), 2)
    w_out = over_tp(half(over_shard(w_attn_out[0], 2), 1), 1)
    w_first = over_tp(half(over_shard(w_up[0], 0), 1), 1)
    w_second = over_tp(half(over_shard(w_down[0], 1), 0), 0)
    return w_in, w_out, w_first, w_second


def wide_parts(args):
    (
        tokens, encoded, cotangent, adapter_of, w_attn_in, w_attn_out, w_up, w_down, norm_gain, norm_shift,
        down_attn_in, up_attn_in, down_feed_in, up_feed_in, down_attn_out, up_attn_out, down_feed_out, up_feed_out,
    ) = args
    n, tp = lax.axis_size("sh"), lax.axis_size("tp")
    sh, core, z = lax.axis_index("sh"), lax.axis_index("core"), lax.axis_index("tp")
    width = w_attn_in.shape[3] * 2 * n
    held_rows = down_feed_in.shape[1]
    quarter = width // tp
    piece = quarter // 2

    ids = lax.all_gather(adapter_of, ("sh", "core"), tiled=True)

    row_ids = (sh * 2 + core) * held_rows + jnp.arange(held_rows)
    wanted = ids.reshape(n, tp)[:, :, None] * RANK + jnp.arange(RANK)
    picks = (wanted[..., None] == row_ids).astype(bf16)
    whole = jnp.concatenate(
        [
            down_attn_in.reshape(6, held_rows, width),
            down_feed_in,
            up_attn_out[0],
            up_feed_out,
        ]
    )
    def in_quarters(rows):
        return jnp.moveaxis(rows.reshape(held_rows, tp, quarter), 1, 0)

    split = jnp.concatenate(
        [
            up_attn_in.reshape(6, held_rows, quarter),
            in_quarters(up_feed_in[0]),
            down_attn_out[0],
            in_quarters(down_feed_out[0]),
        ]
    )
    picks_z = lax.dynamic_index_in_dim(picks, z, 1, keepdims=False)
    chosen_whole = jnp.einsum("srk,mkd->smrd", picks_z, whole, preferred_element_type=f32).astype(bf16)
    chosen_split = jnp.einsum("szrk,mkd->szmrd", picks, split, preferred_element_type=f32).astype(bf16)
    chosen_whole = core_sum(scatter_sh(chosen_whole))
    chosen_split = over_z(core_sum(scatter_sh(chosen_split)))

    def columns(first, count):
        mine = half_columns(chosen_split[:, first : first + count])
        return jnp.moveaxis(mine, 0, 2).reshape(count, RANK, tp * piece)

    def wide_columns(first):
        mine = lax.dynamic_slice_in_dim(chosen_split[:, first : first + tp], core * 2, 2, 1)
        return jnp.moveaxis(mine, 2, 0).reshape(RANK, tp * 2 * quarter)

    a_in, a_up, b_out, b_down = chosen_whole[:6], chosen_whole[6], chosen_whole[7:9], chosen_whole[9]
    b_in, b_up, a_out, a_down = columns(0, 6), wide_columns(6), columns(6 + tp, 2), wide_columns(8 + tp)

    w_in, w_out, w_first, w_second = gather_weights(w_attn_in, w_attn_out, w_up, w_down)
    taken = rows_here(tokens)
    upstream = rows_here(cotangent)
    mine = lax.dynamic_index_in_dim(encoded, z % 2, 0, keepdims=False)
    memory = jnp.where(core == z // 2, mine, swap_core(mine))

    def merge(weight, down_rows, up_rows):
        return (weight.astype(f32) + t_mm(down_rows, up_rows)).astype(bf16)

    w_in = [merge(w_in[i], a_in[i], b_in[i]) for i in range(6)]
    w_out = [merge(w_out[i], a_out[i], b_out[i]) for i in range(2)]
    w_first = merge(w_first, a_up, b_up)
    w_second = merge(w_second, a_down, b_down)

    gain, shift = norm_gain[0][:, None], norm_shift[0][:, None]
    frames = memory.shape[0]
    w_in = jnp.stack(w_in)
    normed0, q0, k0, v0, lse0, mix0, part = self_forward(taken, gain[0], shift[0], w_in[:3], w_out[0])
    k1, v1 = memory_project(memory, w_in[4:])
    hidden1, normed1, q1, lse1, mix1, part1 = cross_forward(
        taken, part, swap_core(part), gain[1], shift[1], w_in[3], k1, v1, w_out[1], frames
    )
    hidden2, part2, back, g_aup, g_bup, g_adown, g_bdown = feed(
        hidden1, part1, swap_core(part1), gain[2], shift[2], w_first, w_second, upstream, a_up, b_up, a_down, b_down
    )
    result = (hidden2 + core_sum(part2)).astype(bf16)
    grad, e1, dq1, dk1, dv1, back1 = cross_backward(
        hidden2, gain[2], upstream, back, swap_core(back), w_out[1], w_in[3], q1, k1, v1, lse1, frames
    )
    part = memory_backward(dk1, dv1, w_in[4:], frames)
    own, other = own_and_other(jnp.moveaxis(part.reshape(part.shape[0], 2, -1), 1, 0))
    memory_rows = (own.astype(f32) + other.astype(f32)).astype(bf16)
    grad, e0, dq0, dk0, dv0, back0 = self_backward(
        hidden1, gain[1], grad, back1, swap_core(back1), w_out[0], w_in[:3], q0, k0, v0, lse0
    )
    grad = final_norm(taken, gain[0], grad, back0, swap_core(back0))
    ranks1 = attention_ranks(normed1, memory, mix1, dq1, dk1, dv1, e1, a_in[3:], b_in[3:], a_out[1], b_out[1])
    ranks0 = attention_ranks(normed0, None, mix0, dq0, dk0, dv0, e0, a_in[:3], b_in[:3], a_out[0], b_out[0])
    feed_up = jnp.moveaxis(g_bup.reshape(RANK, tp, tp, piece), 2, 0).reshape(tp, RANK, tp * piece)
    feed_down = jnp.moveaxis(g_adown.reshape(RANK, tp, tp, piece), 2, 0).reshape(tp, RANK, tp * piece)
    out_split = jnp.stack([ranks0[2], ranks1[2]])
    out_whole = jnp.stack([ranks0[3], ranks1[3]])
    split_grads = jnp.concatenate([ranks0[1], ranks1[1], feed_up.astype(bf16), out_split, feed_down.astype(bf16)])
    whole_grads = jnp.concatenate(
        [ranks0[0], ranks1[0], g_aup.astype(bf16)[None], out_whole, g_bdown.astype(bf16)[None]]
    )
    here = ids.reshape(n, tp)[sh]
    return result, grad, memory_rows, split_grads, whole_grads, here


def narrow_parts(args):
    (
        tokens, encoded, cotangent, adapter_of, w_attn_in, w_attn_out, w_up, w_down, norm_gain, norm_shift,
        down_attn_in, up_attn_in, down_feed_in, up_feed_in, down_attn_out, up_attn_out, down_feed_out, up_feed_out,
    ) = args

    def six(rows):
        return rows.reshape(6, *rows.shape[3:])

    lines = jnp.pad(adapter_of.astype(f32), (0, 6))[:, None] * jnp.ones((1, 128), f32)
    _, frames, d = encoded.shape
    step = frames // 4
    spaced = jnp.pad(encoded.reshape(2, 4, step, d), ((0, 0), (0, 0), (0, 384 - step), (0, 0)))
    spaced = spaced.reshape(2, 1536, d)
    acts, g_tok, g_enc, split_sum, whole_sum = layer(
        tokens, spaced, cotangent, six(w_attn_in), w_attn_out[0], w_up[0], w_down[0], lines,
        norm_gain[0][:, None], norm_shift[0][:, None], six(down_attn_in), six(up_attn_in), down_feed_in[0],
        up_feed_in[0], down_attn_out[0], up_attn_out[0], down_feed_out[0], up_feed_out[0],
    )
    held = split_sum.shape[1]

    def wide_of(first):
        block = split_sum[first : first + 4].reshape(4, held, 2, 128)
        return jnp.moveaxis(block, 0, 2).reshape(1, held, 1024)

    whole = jnp.moveaxis(whole_sum, 0, 2).reshape(10, whole_sum.shape[2], d)
    cross_side, self_side = split_sum[8:12], split_sum[12:16]
    return (
        acts,
        g_tok.astype(f32),
        g_enc.reshape(2, 384, d)[:, :step].astype(f32),
        jnp.stack([whole[6:9], whole[2:5]])[None],
        jnp.stack([self_side[:3], cross_side[:3]])[None],
        whole[0:1],
        wide_of(0),
        jnp.stack([self_side[3], cross_side[3]])[None],
        jnp.stack([whole[9], whole[5]])[None],
        wide_of(4),
        whole[1:2],
    )


def on_device(*args):
    if lax.axis_size("sh") == 2:
        return narrow_parts(args)
    n, tp = lax.axis_size("sh"), lax.axis_size("tp")
    held_rows, quarter = args[12].shape[1], args[11].shape[4]
    width, piece = quarter * tp, quarter // 2
    result, grad, memory_rows, split_grads, whole_grads, here = wide_parts(args)
    activations = rows_home(half_columns(result))
    grad_encoded = rows_home(memory_rows).astype(f32)
    grad_tokens = rows_home(half_columns(grad)).astype(f32)
    compact = jnp.moveaxis(split_grads.reshape(-1, RANK, tp, piece), 2, 0)
    own, other = own_and_other(jnp.moveaxis(whole_grads.reshape(-1, RANK, tp, 2, piece), (3, 2), (0, 1)))
    compact = jnp.concatenate([compact, own + other], axis=1)
    compact = over_z(compact)
    rows = jnp.arange(2 * n * held_rows)
    place = (here[:, None] * RANK + jnp.arange(RANK))[None] == rows[:, None, None]
    dense = jnp.einsum("gkr,kmrp->gmp", place.astype(bf16), compact, preferred_element_type=f32)
    dense = dense.astype(bf16).reshape(n, 2, held_rows, *dense.shape[1:])
    dense = scatter_sh(dense)
    dense = dense + lax.ppermute(dense, "rep", SWAP)
    both = in_core_order(*own_and_other(dense))
    done = jnp.moveaxis(both, 0, 2)
    count = 8 + 2 * tp
    sums = done[:, :count].astype(f32)

    def narrow(first, number):
        block = sums[:, first : first + number].reshape(held_rows, number, quarter)
        return jnp.moveaxis(block, 1, 0)

    def wide_of(first):
        block = jnp.moveaxis(sums[:, first : first + tp], 2, 1)
        return block.reshape(held_rows, 2 * tp * piece)

    grad_up_attn_in = narrow(0, 6).reshape(1, 2, 3, held_rows, quarter)
    grad_up_feed_in = wide_of(6)[None]
    grad_down_attn_out = narrow(6 + tp, 2)[None]
    grad_down_feed_out = wide_of(8 + tp)[None]
    rest = done[:, count:].reshape(tp, held_rows // tp, 10, quarter)
    rest = jnp.moveaxis(over_z(rest), 0, 2)
    rest = jnp.moveaxis(rest.reshape(held_rows // tp, 10, width), 1, 0).astype(f32)
    return (
        activations,
        grad_tokens,
        grad_encoded,
        rest[:6].reshape(1, 2, 3, held_rows // tp, width),
        grad_up_attn_in,
        rest[6:7],
        grad_up_feed_in,
        grad_down_attn_out,
        rest[7:9][None],
        grad_down_feed_out,
        rest[9:10],
    )


def solution(mesh):
    rep, shard, tp = (mesh.shape[name] for name in ("rep", "shard", "tp"))
    fine = Mesh(mesh.devices.reshape(rep, shard // 2, 2, tp), ("rep", "sh", "core", "tp"))
    shard = ("sh", "core")
    clips = ("rep", "sh", "core")
    both = ("sh", "core", "tp")
    placed = (
        P(clips, "tp", None),
        P(clips, None, None),
        P(clips, "tp", None),
        P(clips),
        P(None, None, None, shard, "tp"),
        P(None, None, "tp", shard),
        P(None, shard, "tp"),
        P(None, "tp", shard),
        P(),
        P(),
        P(None, None, None, shard, None),
        P(None, None, None, shard, "tp"),
        P(None, shard, None),
        P(None, shard, "tp"),
        P(None, None, shard, "tp"),
        P(None, None, shard, None),
        P(None, shard, "tp"),
        P(None, shard, None),
    )
    return jax.shard_map(
        on_device,
        mesh=fine,
        in_specs=placed,
        out_specs=(
            P(clips, "tp", None),
            P(clips, "tp", None),
            P(clips, "tp", None),
            P(None, None, None, both, None),
            P(None, None, None, shard, "tp"),
            P(None, both, None),
            P(None, shard, "tp"),
            P(None, None, shard, "tp"),
            P(None, None, both, None),
            P(None, shard, "tp"),
            P(None, both, None),
        ),
        check_vma=False,
    )
```

```python
import functools

import jax
import jax.numpy as jnp
from jax import lax
from jax.experimental import pallas as pl
from jax.experimental.pallas import tpu as pltpu
from jax.sharding import Mesh, PartitionSpec as P

HD = 64
RANK = 16
epsilon = 1e-05
masked_score = -1e30
f32, bf16 = jnp.float32, jnp.bfloat16
SWAP = ((0, 1), (1, 0))
MESH = pl.DeviceIdType.MESH


def dot(a, b, dims):
    return lax.dot_general(a, b, (dims, ((), ())), preferred_element_type=f32)


def mm(a, b):
    return dot(a, b, ((1,), (0,)))


def mm_t(a, b):
    return dot(a, b, ((1,), (1,)))


def t_mm(a, b):
    return dot(a, b, ((0,), (0,)))


HIDE = -1e30
SCALE = HD**-0.5
EPS = 1e-05
VM = pl.BlockSpec(memory_space=pltpu.VMEM)


def nn(a, b):
    return lax.dot_general(a, b, (((1,), (0,)), ((), ())), preferred_element_type=f32)


def nt(a, b):
    return lax.dot_general(a, b, (((1,), (1,)), ((), ())), preferred_element_type=f32)


def normalize(rows):
    centered = rows - jnp.mean(rows, axis=-1, keepdims=True)
    variance = jnp.mean(centered * centered, axis=-1, keepdims=True)
    inverse = lax.rsqrt(variance + EPS)
    return centered * inverse, inverse


def norm_back(rows, gain, grad):
    unit, inverse = normalize(rows)
    scaled = grad * gain
    first = jnp.mean(scaled, axis=-1, keepdims=True)
    second = jnp.mean(scaled * unit, axis=-1, keepdims=True)
    return (scaled - first - unit * second) * inverse


def pair_lanes(p):
    return pl.ds(pl.multiple_of(p * 128, 128), 128)


def scores_t(keys, queries, frames, causal, groups=1):
    s = nt(keys, queries) * SCALE
    if causal:
        key = lax.broadcasted_iota(jnp.int32, s.shape, 0)
        query = lax.broadcasted_iota(jnp.int32, s.shape, 1)
        s = jnp.where(query >= key, s, HIDE)
    elif frames < s.shape[0]:
        step, used = s.shape[0] // groups, frames // groups
        kept = used // 16 * 16
        key = kept + lax.broadcasted_iota(jnp.int32, (step - kept, s.shape[1]), 0)
        blocks = [s[g * step : (g + 1) * step] for g in range(groups)]
        s = jnp.concatenate([part for b in blocks for part in (b[:kept], jnp.where(key < used, b[kept:], HIDE))])
    return s


def attend_forward(q, k, v, mix, lse, frames, causal, start=0, number=None, groups=1):
    def pair(p, carry):
        lanes = pair_lanes(p)
        qp, kp = q[:, lanes], k[:, lanes]
        vt = v[:, lanes].T
        first = lax.broadcasted_iota(jnp.int32, qp.shape, 1) < HD
        outs, logs = [], []
        for h in (0, 1):
            s = scores_t(kp, jnp.where(first == (h == 0), qp, 0), frames, causal, groups)
            top = jnp.max(s, axis=0, keepdims=True)
            e = jnp.exp(s - top)
            total = jnp.sum(e, axis=0, keepdims=True)
            probs = (e * (1.0 / total)).astype(bf16)
            outs.append(nn(vt, probs)[h * HD : (h + 1) * HD])
            logs.append(top + jnp.log(total))
        mix[:, lanes] = jnp.concatenate(outs).T.astype(bf16)
        lse[p] = jnp.concatenate(logs)
        return carry

    lax.fori_loop(start, start + (number or q.shape[1] // 128), pair, 0)


def attend_backward(q, k, v, do, lse, dq, dk, dv, frames, causal, start=0, number=None, groups=1):
    def pair(p, carry):
        lanes = pair_lanes(p)
        qp, kp, vp, dop = q[:, lanes], k[:, lanes], v[:, lanes], do[:, lanes]
        kt = kp.T
        logs = lse[p]
        first = lax.broadcasted_iota(jnp.int32, qp.shape, 1) < HD
        dqs, dks, dvs = [], [], []
        for h in (0, 1):
            mine = first == (h == 0)
            s = scores_t(kp, jnp.where(mine, qp, 0), frames, causal, groups)
            probs = jnp.exp(s - logs[h : h + 1])
            dvs.append(nn(probs.astype(bf16), dop))
            dp = nt(vp, jnp.where(mine, dop, 0))
            t = probs * dp
            ds = (t - probs * jnp.sum(t, axis=0, keepdims=True)).astype(bf16)
            dks.append(nn(ds, qp))
            dqs.append(nn(kt, ds)[h * HD : (h + 1) * HD])
        first_k = lax.broadcasted_iota(jnp.int32, kp.shape, 1) < HD
        dv[:, lanes] = jnp.where(first_k, dvs[0], dvs[1]).astype(bf16)
        dk[:, lanes] = (jnp.where(first_k, dks[0], dks[1]) * SCALE).astype(bf16)
        dq[:, lanes] = (jnp.concatenate(dqs).T * SCALE).astype(bf16)
        return carry

    lax.fori_loop(start, start + (number or q.shape[1] // 128), pair, 0)


def params():
    return pltpu.CompilerParams(vmem_limit_bytes=60 * 1024 * 1024)


def sds(shape, dtype):
    return jax.ShapeDtypeStruct(shape, dtype)


def self_forward(tok, gain, shift, wi, wo):
    def kernel(tok, gain, shift, wi, wo, normed, q, k, v, lse, mix, part):
        unit, _ = normalize(tok[...].astype(f32))
        normed[...] = (unit * gain[...] + shift[...]).astype(bf16)
        for i, out in enumerate((q, k, v)):
            out[...] = nn(normed[...], wi[i]).astype(bf16)
        attend_forward(q, k, v, mix, lse, tok.shape[0], True)
        part[...] = nn(mix[...], wo[...])

    r, d = tok.shape
    w = wi.shape[2]
    return pl.pallas_call(kernel, out_shape=[sds((r, d), bf16)] + [sds((r, w), bf16)] * 3 + [sds((w // 128, 2, r), f32), sds((r, w), bf16), sds((r, d), f32)],
        in_specs=[VM] * 5, out_specs=[VM] * 7, compiler_params=params(), name="self_forward")(tok, gain, shift, wi, wo)


def memory_project(enc, wi):
    def kernel(enc, wi, k, v):
        frames = enc.shape[0]
        for i, out in enumerate((k, v)):
            out[:frames] = nn(enc[...], wi[i]).astype(bf16)
            out[frames:] = jnp.zeros((out.shape[0] - frames, out.shape[1]), bf16)
    frames = -(-enc.shape[0] // 128) * 128
    return pl.pallas_call(kernel, out_shape=[sds((frames, wi.shape[2]), bf16)] * 2, in_specs=[VM] * 2, out_specs=[VM] * 2, compiler_params=params(), name="memory_project")(enc, wi)


def cross_forward(hid, part, other, gain, shift, wq, k, v, wo, frames):
    def kernel(hid, part, other, gain, shift, wq, k, v, wo, hidden, normed, q, lse, mix, out):
        hidden[...] = hid[...].astype(f32) + part[...] + other[...]
        unit, _ = normalize(hidden[...])
        normed[...] = (unit * gain[...] + shift[...]).astype(bf16)
        q[...] = nn(normed[...], wq[...]).astype(bf16)
        attend_forward(q, k, v, mix, lse, frames, False)
        out[...] = nn(mix[...], wo[...])

    r, d = hid.shape
    w = wq.shape[1]
    return pl.pallas_call(kernel, out_shape=[sds((r, d), f32), sds((r, d), bf16), sds((r, w), bf16), sds((w // 128, 2, r), f32), sds((r, w), bf16), sds((r, d), f32)],
        in_specs=[VM] * 9, out_specs=[VM] * 6, compiler_params=params(), name="cross_forward")(hid, part, other, gain, shift, wq, k, v, wo)


def rank_t(rows16, inputs):
    return nt(rows16, inputs).astype(bf16)


def feed(hid, part, other, gain, shift, up, down, e, a_up, b_up, a_down, b_down):
    CH = 512

    def kernel(hid, part, other, gain, shift, up, down, e, a_up, b_up, a_down, b_down, hidden, out, back, g_aup, g_bup, g_adown, g_bdown, normed):
        hidden[...] = hid[...] + part[...] + other[...]
        unit, _ = normalize(hidden[...])
        normed[...] = (unit * gain[...] + shift[...]).astype(bf16)
        t_in = rank_t(a_up[...], normed[...])
        r_out = rank_t(b_down[...], e[...])
        r_in = jnp.zeros((16, hid.shape[0]), f32)
        t_out = jnp.zeros((16, hid.shape[0]), f32)
        for j in range(up.shape[1] // CH):
            cols = slice(j * CH, (j + 1) * CH)
            pre = nn(normed[...], up[:, cols])
            cdf = 0.5 * (1.0 + lax.erf(pre * (2**-0.5)))
            active = (pre * cdf).astype(bf16)
            slope = cdf + pre * jnp.exp(-0.5 * pre * pre) * 0.3989422804014327
            grad = (nt(e[...], down[cols]) * slope).astype(bf16)
            term, term_b = nn(active, down[cols]), nt(grad, up[:, cols])
            if j == 0:
                out[...], back[...] = term, term_b
            else:
                out[...] += term
                back[...] += term_b
            g_bup[:, cols] = nn(t_in, grad)
            g_adown[:, cols] = nn(r_out, active)
            r_in += nt(b_up[:, cols], grad)
            t_out += nt(a_down[:, cols], active)
        g_aup[...] = nn(r_in.astype(bf16), normed[...])
        g_bdown[...] = nn(t_out.astype(bf16), e[...])

    r, d = hid.shape
    w = up.shape[1]
    return pl.pallas_call(kernel, out_shape=[sds((r, d), f32)] * 3 + [sds((16, d), f32), sds((16, w), f32), sds((16, w), f32), sds((16, d), f32)],
        in_specs=[VM] * 12, out_specs=[VM] * 7, scratch_shapes=[pltpu.VMEM((r, d), bf16)], compiler_params=params(), name="feed")(
            hid, part, other, gain, shift, up, down, e, a_up, b_up, a_down, b_down)


def cross_backward(hid3, gain3, g, part, other, wo, wq, q, k, v, lse, frames):
    def kernel(hid3, gain3, g, part, other, wo, wq, q, k, v, lse, g_out, e, dq, dk, dv, back, do):
        g_out[...] = g[...].astype(f32) + norm_back(hid3[...], gain3[...], part[...] + other[...])
        e[...] = g_out[...].astype(bf16)
        do[...] = nt(e[...], wo[...]).astype(bf16)
        attend_backward(q, k, v, do, lse, dq, dk, dv, frames, False)
        back[...] = nt(dq[...], wq[...])

    r, d = hid3.shape
    w, f = q.shape[1], k.shape[0]
    return pl.pallas_call(kernel, out_shape=[sds((r, d), f32), sds((r, d), bf16), sds((r, w), bf16), sds((f, w), bf16), sds((f, w), bf16), sds((r, d), f32)],
        in_specs=[VM] * 11, out_specs=[VM] * 6, scratch_shapes=[pltpu.VMEM((r, w), bf16)], compiler_params=params(), name="cross_backward")(
            hid3, gain3, g, part, other, wo, wq, q, k, v, lse)


def self_backward(hid2, gain2, g, part, other, wo, wi, q, k, v, lse):
    def kernel(hid2, gain2, g, part, other, wo, wi, q, k, v, lse, g_out, e, dq, dk, dv, back, do):
        g_out[...] = g[...] + norm_back(hid2[...], gain2[...], part[...] + other[...])
        e[...] = g_out[...].astype(bf16)
        do[...] = nt(e[...], wo[...]).astype(bf16)
        attend_backward(q, k, v, do, lse, dq, dk, dv, q.shape[0], True)
        back[...] = nt(dq[...], wi[0])
        back[...] += nt(dk[...], wi[1])
        back[...] += nt(dv[...], wi[2])

    r, d = hid2.shape
    w = q.shape[1]
    return pl.pallas_call(kernel, out_shape=[sds((r, d), f32), sds((r, d), bf16)] + [sds((r, w), bf16)] * 3 + [sds((r, d), f32)],
        in_specs=[VM] * 11, out_specs=[VM] * 6, scratch_shapes=[pltpu.VMEM((r, w), bf16)], compiler_params=params(), name="self_backward")(
            hid2, gain2, g, part, other, wo, wi, q, k, v, lse)


def final_norm(hid, gain, g, part, other):
    def kernel(hid, gain, g, part, other, out):
        out[...] = (g[...] + norm_back(hid[...].astype(f32), gain[...], part[...] + other[...])).astype(bf16)

    return pl.pallas_call(kernel, out_shape=sds(hid.shape, bf16), in_specs=[VM] * 5, out_specs=VM, compiler_params=params(), name="final_norm")(hid, gain, g, part, other)


def memory_backward(dk, dv, wi, frames):
    def kernel(dk, dv, wi, out):
        out[...] = (nt(dk[:frames], wi[0]) + nt(dv[:frames], wi[1])).astype(bf16)
    d = wi.shape[1]
    return pl.pallas_call(kernel, out_shape=sds((frames, d), bf16), in_specs=[VM] * 3, out_specs=VM, compiler_params=params(), name="memory_backward")(dk, dv, wi)


def attention_ranks(normed, source, mix, dq, dk, dv, e, a_in, b_in, a_out, b_out):
    def kernel(*refs):
        operands, results = refs[:-4], refs[-4:]
        given = operands[:7] if source is not None else operands[:1] + operands[:1] + operands[1:6]
        normed, source_, mix, dq, dk, dv, e = given
        a_in, b_in, a_out, b_out = operands[-4:]
        ga_in, gb_in, ga_out, gb_out = results
        for i, (u, g) in enumerate(((normed, dq), (source_, dk), (source_, dv))):
            rows = u.shape[0]
            inner = rank_t(a_in[i], u[...])
            back = rank_t(b_in[i], g[:rows])
            gb_in[i] = nn(inner, g[:rows]).astype(bf16)
            ga_in[i] = nn(back, u[...]).astype(bf16)
        ga_out[...] = nn(rank_t(b_out[...], e[...]), mix[...]).astype(bf16)
        gb_out[...] = nn(rank_t(a_out[...], mix[...]), e[...]).astype(bf16)

    args = [normed] + ([source] if source is not None else []) + [mix, dq, dk, dv, e, a_in, b_in, a_out, b_out]
    return pl.pallas_call(kernel, out_shape=[sds(t.shape, bf16) for t in (a_in, b_in, a_out, b_out)],
        in_specs=[VM] * len(args), out_specs=[VM] * 4, compiler_params=params(), name="attention_ranks")(*args)


OFFS = (2, 4, 6, 8, 10)


class Unit:
    def __init__(self, place, kind, index):
        self.place, self.tall, self.index = place, kind == "a", index
        self.rows = 512 if self.tall else 128
        late = place >= 12
        if self.tall:
            self.most, self.via_y = (448, 352) if late else (384, 288)
        else:
            self.most, self.via_y = (112, 96) if late else (96, 64)


def make_units():
    order = [("a", 0), ("a", 1), ("a", 2), ("b", 0), ("a", 3), ("a", 4), ("a", 5), ("b", 1)]
    for j in range(4):
        order += [("a", 6 + j), ("b", 2 + j)]
    return [Unit(i, kind, index) for i, (kind, index) in enumerate(order)]


def layer_kernel(
    tok, enc, cot, w_in, w_out, w_up, w_down, ids, gain, shift,
    d_ai, u_ai, d_fi, u_fi, d_ao, u_ao, d_fo, u_fo,
    acts, g_tok, g_enc, split_sum, whole_sum,
    ga, gb, rows, grads, memory, normed, q0, k0, v0, mix, q1, k1, v1, lse, hidden, g_now, dd, dkv,
    outbox, inbox, idbuf, rs, rw, ys, yw, ys_own, yw_own, fz, fw, r_in, t_out, r_up, gsplit, gwhole, wz, dsum, t_self, t_query, t_memory, t_mix,
    rwb0, rwb1, rwb2, czs0, czs1, czs2, czw0, czw1, czw2, sb0, sb1, sb2, yb0, yb1, yb2, xb0, xb1, xb2, cb0, cb1, cb2,
    core_s, core_r, up_s, dn_s, z_r, y_s, y_r, x_s, x_r, row_s, row_r, loc, ad_s, ad_r, ex_s, ex_r, b_s, b_r, home_s, home_r,
):
    units = make_units()
    count = len(units)
    frames, groups = 1500 * enc.shape[1] // 1536, 4
    do, dq = dd.at[0], dd.at[1]
    x, y, c, z = (lax.axis_index(a) for a in ("rep", "sh", "core", "tp"))
    al = pl.multiple_of
    sent = {}

    def when(cond, fn):
        fn() if cond is None else pl.when(cond)(fn)

    def remote(src, dst, s, r, dev):
        return pltpu.make_async_remote_copy(
            src_ref=src, dst_ref=dst, send_sem=s, recv_sem=r, device_id=dev, device_id_type=MESH
        )

    def send(key, cond, src, dst, s, r, dev):
        when(cond, lambda: remote(src, dst, s, r, dev).start())
        sent.setdefault(key, []).append((cond, lambda: remote(src, dst, s, r, dev).wait_send()))

    def settle(key):
        for cond, fn in sent.pop(key, []):
            when(cond, fn)

    X, Y, C = {"rep": 1 - x}, {"sh": 1 - y}, {"core": 1 - c}
    YC = {"sh": 1 - y, "core": 1 - c}
    UP, DOWN = {"tp": z + 1}, {"tp": z - 1}
    others = [lax.rem(z + k, 4) for k in (1, 2, 3)]

    def got(dst, r):
        remote(dst, dst, r, r, X).wait_recv()

    bar = pltpu.get_barrier_semaphore()
    for dev in [X, Y, C, YC] + [{"tp": j} for j in others] + [{"tp": j, "core": 1 - c} for j in others]:
        pl.semaphore_signal(bar, inc=1, device_id=dev, device_id_type=MESH)
    pl.semaphore_wait(bar, 10)

    def block(u, yy, zz, first, size):
        if u.tall:
            return ga.at[pl.ds(al(u.index * 1024 + yy * 512 + first, 16), size), pl.ds(al(zz * 128, 128), 128)]
        return gb.at[u.index, zz, pl.ds(al(first, 16), size), pl.ds(al(yy * 512, 512), 512)]

    def across(u, yy, first, size):
        if u.tall:
            return ga.at[pl.ds(al(u.index * 1024 + yy * 512 + first, 16), size)]
        return gb.at[u.index, :, pl.ds(al(first, 16), size), pl.ds(al(yy * 512, 512), 512)]

    def three(u, first, size):
        if u.tall:
            return ga.at[pl.ds(al(u.index * 1024 + y * 512 + first, 16), size), 0:384]
        return gb.at[u.index, 0:3, pl.ds(al(first, 16), size), pl.ds(al(y * 512, 512), 512)]

    def half_src(u, cc):
        m = u.index
        if u.tall:
            if m < 6:
                return w_in.at[m, :, pl.ds(al(cc * 128, 128), 128)]
            return w_up.at[:, pl.ds(al(cc * 512 + (m - 6) * 128, 128), 128)]
        if m < 2:
            return w_out.at[m, pl.ds(al(cc * 128, 128), 128)]
        return w_down.at[pl.ds(al(cc * 512 + (m - 2) * 128, 128), 128)]

    def half_dst(u, cc):
        if u.tall:
            return block(u, y, z, cc * 256, 256)
        return gb.at[u.index, z, :, pl.ds(al(y * 512 + cc * 256, 256), 256)]

    def core_exchange(u):
        i = u.place
        send("core", None, half_src(u, 1 - c), half_dst(u, c), core_s.at[i], core_r.at[i], C)
        pltpu.make_async_copy(half_src(u, c), half_dst(u, c), loc.at[i]).start()

    def to_y(u, j):
        b = block(u, y, j, x * (u.rows - u.via_y), u.via_y)
        remote(b, b, y_s.at[u.place], y_r.at[u.place], Y).start()

    def own(u):
        i = u.place
        got(half_dst(u, 1 - c), core_r.at[i])
        pltpu.make_async_copy(half_src(u, c), half_dst(u, c), loc.at[i]).wait()
        zb = block(u, y, z, x * (u.rows - u.most), u.most)
        send(i, z < 3, zb, zb, up_s.at[i, z], z_r.at[i, z], UP)
        send(i, z > 0, zb, zb, dn_s.at[i, z], z_r.at[i, z], DOWN)
        to_y(u, z)

    def hop(u, k):
        i = u.place
        ways = (
            (z >= k, z - k, (z >= k) & (z < 3), UP, up_s),
            (z + k <= 3, z + k, (z + k <= 3) & (z > 0), DOWN, dn_s),
        )
        for ok, j, more, dev, sems in ways:
            zb = block(u, y, j, x * (u.rows - u.most), u.most)

            def arrive(zb=zb, j=j):
                got(zb, z_r.at[i, j])
                to_y(u, j)
                b = block(u, y, j, x * u.most, u.rows - u.most)
                remote(b, b, x_s.at[i, 0], x_r.at[i, 0], X).start()

            when(ok, arrive)
            send(i, more, zb, zb, sems.at[i, j], z_r.at[i, j], dev)

    def cross(u):
        i = u.place
        got(across(u, 1 - y, x * (u.rows - u.via_y), u.via_y), y_r.at[i])
        b = across(u, 1 - y, x * u.via_y, u.rows - u.via_y)
        send(i, None, b, b, x_s.at[i, 1], x_r.at[i, 1], X)

    def last(u):
        i = u.place
        got(three(u, (1 - x) * u.most, u.rows - u.most), x_r.at[i, 0])
        got(across(u, 1 - y, (1 - x) * u.via_y, u.rows - u.via_y), x_r.at[i, 1])
        b = across(u, y, x * (u.rows - u.via_y), u.via_y)
        remote(b, b, y_s.at[i], y_r.at[i], Y).wait_send()
        b = three(u, x * u.most, u.rows - u.most)
        remote(b, b, x_s.at[i, 0], x_r.at[i, 0], X).wait_send()
        settle(i)

    mine = c == z // 2

    def rows_out(src, dst, slot):
        for i in (0, 1):
            zd = 2 * c + i
            d = dst.at[pl.ds(al(z * 112, 16), 112)]
            send("rows", zd != z, src.at[i], d, row_s.at[slot, i], row_r.at[slot, z], {"tp": zd})
            when(
                zd == z,
                lambda i=i, d=d: pltpu.make_async_copy(src.at[i], d, loc.at[count + slot]).start(),
            )

    def rows_in(dst, slot):
        def wait():
            for j in others:
                got(dst.at[pl.ds(al(j * 112, 16), 112)], row_r.at[slot, j])
            d = dst.at[pl.ds(al(z * 112, 16), 112)]
            pltpu.make_async_copy(d, d, loc.at[count + slot]).wait()

        when(mine, wait)
        send("rows", mine, dst, dst, row_s.at[slot, 2], row_r.at[slot, 4], C)

    def rows_have(dst, slot):
        when(c != z // 2, lambda: got(dst, row_r.at[slot, 4]))

    parts = [slice(t * 96, (t + 1) * 96) for t in range(16)]

    def enc_local(t):
        return pltpu.make_async_copy(
            enc.at[lax.rem(z, 2), parts[t]], memory.at[parts[t]], loc.at[count + 2 + t]
        )

    def enc_send(t):
        send(
            "enc", mine, enc.at[lax.rem(z, 2), parts[t]], memory.at[parts[t]], row_s.at[2, t], row_r.at[2, t], C
        )
        when(mine, lambda: enc_local(t).start())

    def enc_have():
        for t in range(16):
            when(mine, lambda: enc_local(t).wait())
            when(c != z // 2, lambda: got(memory.at[parts[t]], row_r.at[2, t]))

    me = 2 * y + c

    def ids_out():
        for k, dev in enumerate((C, Y, YC)):
            send("ids", None, ids, idbuf.at[me], ad_s.at[k], ad_r.at[k], dev)
        idbuf[pl.ds(me, 1)] = ids[...][None]

    def adapters_pick():
        for k, s in enumerate((2 * y + 1 - c, 2 * (1 - y) + c, 2 * (1 - y) + 1 - c)):
            got(idbuf.at[s], ad_r.at[k])
        held = lax.broadcasted_iota(jnp.int32, (128, 32), 1) + me * 32
        rank = lax.rem(lax.broadcasted_iota(jnp.int32, (128, 32), 0), 16)
        lines = [
            [jnp.broadcast_to(idbuf[2 * s + k // 2, k % 2 : k % 2 + 1, :32], (16, 32)) for k in range(4)]
            for s in range(2)
        ]
        wanted = jnp.concatenate([line for pair in lines for line in pair])
        target = held.astype(f32) - rank.astype(f32)
        picks = jnp.where(wanted * 16.0 == target, 1.0, 0.0).astype(bf16)
        here = []
        for s in range(2):
            line = lines[s][0]
            for k in (1, 2, 3):
                line = jnp.where(z == k, lines[s][k], line)
            here.append(line)
        picks_z = jnp.where(jnp.concatenate(here) * 16.0 == target[:32], 1.0, 0.0).astype(bf16)
        for h in range(2):
            cols = slice(h * 128, h * 128 + 128)
            wide = slice(h * 512, h * 512 + 512)
            given = [u_ai[m][:, cols] for m in range(6)] + [u_fi[:, wide]]
            given += [d_ao[m][:, cols] for m in range(2)] + [d_fo[:, wide]]
            for b in range(4):
                block_of = jnp.concatenate(given, axis=1)[:, b * 512 : b * 512 + 512]
                dkv[h, b * 128 : b * 128 + 128] = nn(picks, block_of).astype(bf16)
            if h == 0:
                given = [d_ai[m] for m in range(5)]
            else:
                given = [d_ai[5], d_fi, u_ao[0], u_ao[1], u_fo]
            for b in range(10):
                block_of = given[b // 2][:, b % 2 * 512 : b % 2 * 512 + 512]
                dd[h, b * 32 : b * 32 + 32] = nn(picks_z, block_of).astype(bf16)
        send("pick", None, dkv.at[1 - c], rs, ad_s.at[3], ad_r.at[3], C)
        send("pick", None, dd.at[1 - c, 0:320], rw, ad_s.at[4], ad_r.at[4], C)

    def adapters_y():
        got(rs, ad_r.at[3])
        got(rw, ad_r.at[4])
        rs[...] += dkv[pl.ds(c, 1)][0]
        rw[...] += dd[pl.ds(c, 1), 0:320][0]
        for b in range(4):
            for k in range(2):
                ys_own[k, :, b * 512 : b * 512 + 512] = rs[b * 128 + k * 64 : b * 128 + k * 64 + 64]
        for b in range(10):
            for k in range(2):
                yw_own[k, :, b * 512 : b * 512 + 512] = rw[b * 32 + k * 16 : b * 32 + k * 16 + 16]
        send("pick", None, ys_own.at[1 - y], ys, ad_s.at[5], ad_r.at[5], Y)
        send("pick", None, yw_own.at[1 - y], yw, ad_s.at[6], ad_r.at[6], Y)

    def adapters_z():
        got(ys, ad_r.at[5])
        got(yw, ad_r.at[6])
        ys[...] += ys_own[pl.ds(y, 1)][0]
        fw[pl.ds(c, 1)] = (yw[...] + yw_own[pl.ds(y, 1)][0])[None]
        for k, j in enumerate(others):
            send("pick", None, ys.at[pl.ds(al(j * 16, 16), 16)], fz.at[z], ad_s.at[7 + k], ad_r.at[7 + z], {"tp": j})
        fz[pl.ds(z, 1)] = ys[pl.ds(al(z * 16, 16), 16)][None]
        send("pick", None, fw.at[c], fw.at[c], ad_s.at[11], ad_r.at[11], C)

    def adapters_have():
        for j in others:
            got(fz.at[j], ad_r.at[7 + j])
        got(fw.at[1 - c], ad_r.at[11])
        settle("pick")
        settle("ids")

    def whole(m):
        return fw[m // 5, :, (m % 5) * 1024 : (m % 5) * 1024 + 1024]

    def split(s):
        return jnp.concatenate([fz[k, :, s * 128 : s * 128 + 128] for k in range(4)], axis=1)

    def merge(u):
        m = u.index
        if u.tall:
            down_t = whole(min(m, 6)).T
            up_rows = split(m)
            for b in range(4):
                place = slice(m * 1024 + b * 256, m * 1024 + b * 256 + 256)
                ga[place] = (ga[place].astype(f32) + nn(down_t[b * 256 : b * 256 + 256], up_rows)).astype(bf16)
        else:
            down_t = split(10 + m).T
            up_rows = whole(7 + m if m < 2 else 9)
            for k in range(4):
                gb[m, k] = (gb[m, k].astype(f32) + nn(down_t[k * 128 : k * 128 + 128], up_rows)).astype(bf16)

    def wa(m):
        return ga[m * 1024 : (m + 1) * 1024]

    def wb(m):
        return gb[m].reshape(512, 1024)

    def part_out(e, slot):
        send(("part", e), None, outbox.at[slot], inbox.at[slot], ex_s.at[e], ex_r.at[e], C)

    def part_sum(e, slot):
        got(inbox.at[slot], ex_r.at[e])
        return outbox[slot] + inbox[slot]

    def norm_rows(side, source):
        unit, _ = normalize(source)
        normed[side] = (unit * gain[side] + shift[side]).astype(bf16)

    def start_rows():
        rows_have(rows, 0)
        norm_rows(0, rows[...].astype(f32))

    def project(m, source, out, length):
        def run():
            out[:length] = nn(source(), wa(m)).astype(bf16)
        return run

    def attention(side, first, number):
        q, k, v = ((q0, k0, v0), (q1, k1, v1))[side]
        length = (rows.shape[0], frames)[side]
        return lambda: attend_forward(q, k, v, mix.at[side], lse.at[side], length, side == 0, first, number, groups)

    def part0():
        outbox[0] = nn(mix[0], wb(0))
        part_out(0, 0)

    def second_rows():
        hidden[0] = rows[...].astype(f32) + part_sum(0, 0)
        norm_rows(1, hidden[0])

    def part1():
        outbox[1] = nn(mix[1], wb(1))
        part_out(1, 1)

    def third_rows():
        hidden[1] = hidden[0] + part_sum(1, 1)
        norm_rows(2, hidden[1])
        rows_have(grads, 1)

    def feed_first():
        settle(("part", 0))
        settle(("part", 1))
        r_up[0] = rank_t(whole(6), normed[2])
        r_up[1] = rank_t(whole(9), grads[...])

    def chunk(j):
        def run():
            up, down = wa(6 + j), wb(2 + j)
            pre = nn(normed[2], up)
            cdf = 0.5 * (1.0 + lax.erf(pre * (2**-0.5)))
            active = (pre * cdf).astype(bf16)
            slope = cdf + pre * jnp.exp(-0.5 * pre * pre) * 0.3989422804014327
            grad = (nt(grads[...], down) * slope).astype(bf16)
            if j == 0:
                outbox[1] = nn(active, down)
                outbox[0] = nt(grad, up)
                r_in[...] = nt(split(6 + j), grad)
                t_out[...] = nt(split(12 + j), active)
            else:
                outbox[1] += nn(active, down)
                outbox[0] += nt(grad, up)
                r_in[...] += nt(split(6 + j), grad)
                t_out[...] += nt(split(12 + j), active)
            gsplit[j] = nn(r_up[0], grad).astype(bf16)
            gsplit[4 + j] = nn(r_up[1], active).astype(bf16)
        return run

    def ranks_of(out, first, number, source):
        def run():
            stack = jnp.concatenate([whole(first + i) for i in range(number)])
            out[...] = rank_t(stack, source())
        return run

    def mix_rank(side):
        def run():
            t_mix[side] = rank_t(split(10 + side), mix[side])
        return run

    tasks = {}

    def task(tick, fn):
        tasks.setdefault(tick, []).append(fn)

    task(1, adapters_pick)
    task(4, adapters_y)
    task(8, adapters_z)
    task(12, adapters_have)
    task(12, lambda: rows_in(rows, 0))
    first = 13
    task(first, start_rows)
    for u in units:
        task(max(first, 2 * u.place + OFFS[4]), functools.partial(merge, u))
    for tick, fn in (
        (first + 1, project(0, lambda: normed[0], q0, 448)),
        (first + 2, project(1, lambda: normed[0], k0, 448)),
        (first + 2, project(2, lambda: normed[0], v0, 448)),
        (first + 3, attention(0, 0, 2)),
        (first + 4, attention(0, 2, 2)),
        (first + 5, part0),
        (first + 6, ranks_of(t_self, 0, 3, lambda: normed[0])),
        (first + 6, mix_rank(0)),
        (first + 7, second_rows),
        (first + 7, project(3, lambda: normed[1], q1, 448)),
        (first + 8, ranks_of(t_query, 3, 1, lambda: normed[1])),
        (first + 8, enc_have),
        (first + 8, project(4, lambda: memory[...], k1, 1536)),
        (first + 9, ranks_of(t_memory, 4, 2, lambda: memory[...])),
        (first + 10, project(5, lambda: memory[...], v1, 1536)),
        (first + 11, attention(1, 0, 1)),
        (first + 12, attention(1, 1, 1)),
        (first + 13, attention(1, 2, 1)),
        (first + 14, attention(1, 3, 1)),
        (first + 15, part1),
        (first + 16, mix_rank(1)),
        (first + 17, third_rows),
        (first + 17, feed_first),
        (12, lambda: rows_out(cot, grads, 1)),
        (22, lambda: rows_in(grads, 1)),
    ):
        task(tick, fn)
    for j in range(4):
        task(max(first + 18 + j, 2 * (9 + 2 * j) + OFFS[4] + 1), chunk(j))

    ids_out()
    rows_out(tok, rows, 0)
    for u in units:
        core_exchange(u)
    for t in range(max(2 * count + OFFS[4], max(tasks)) + 1):
        def at(offset):
            i, odd = divmod(t - offset, 2)
            return units[i] if not odd and 0 <= i < count else None

        if t == 0:
            own(units[0])
        if at(-2):
            own(at(-2))
        for k in (1, 2, 3):
            if at(OFFS[k - 1]):
                hop(at(OFFS[k - 1]), k)
        if at(OFFS[3]):
            cross(at(OFFS[3]))
        if at(OFFS[4]):
            last(at(OFFS[4]))
        if t < 16:
            enc_send(t)
        for fn in tasks.get(t, []):
            fn()

    boxes = list(
        zip(
            (rwb0, rwb1, rwb2), (czs0, czs1, czs2), (czw0, czw1, czw2), (sb0, sb1, sb2), (yb0, yb1, yb2),
            (xb0, xb1, xb2), (cb0, cb1, cb2), ((0, 8, 0, 1), (8, 4, 2, 2), (12, 4, 6, 2)), strict=True,
        )
    )

    def home_core(b):
        rwb, first, half = boxes[b][0], boxes[b][7][2], boxes[b][7][3]
        send(("home", b), None, gwhole.at[pl.ds(first + (1 - c) * half, half)], rwb, b_s.at[b, 0], b_r.at[b, 0], C)

    def home_z(b):
        rwb, czs, czw = boxes[b][:3]
        s0, ns, first, half = boxes[b][7]
        got(rwb, b_r.at[b, 0])
        rwb[...] += gwhole[pl.ds(first + c * half, half)]

        def cuts(j):
            return gsplit.at[s0 : s0 + ns, :, pl.ds(al(j * 128, 128), 128)], rwb.at[:, :, pl.ds(al(j * 256, 256), 256)]

        for k, j in enumerate(others):
            one, two = cuts(j)
            send(("home", b), None, one, czs.at[z], b_s.at[b, 1 + k], b_r.at[b, 1 + z], {"tp": j})
            send(("home", b), None, two, czw.at[z], b_s.at[b, 5 + k], b_r.at[b, 5 + z], {"tp": j})
        one, two = cuts(z)
        czs[pl.ds(z, 1)] = one[...][None]
        czw[pl.ds(z, 1)] = two[...][None]

    def dense_rows(b, to):
        czs, czw, (_, ns, _, half) = boxes[b][1], boxes[b][2], boxes[b][7]
        stack = jnp.concatenate(
            [jnp.concatenate([czs[k, s] for s in range(ns)] + [czw[k, w] for w in range(half)], axis=1) for k in range(4)]
        )
        row = lax.broadcasted_iota(jnp.int32, (64, 64), 0)
        col = lax.broadcasted_iota(jnp.int32, (64, 64), 1)
        clip = col // 16
        chosen = jnp.zeros((64, 64), f32)
        for k in range(4):
            line = idbuf[pl.ds(2 * y + k // 2, 1), k % 2 : k % 2 + 1, :64][0]
            chosen = jnp.where(clip == k, jnp.broadcast_to(line, (64, 64)), chosen)
        target = (row + 64 * to - lax.rem(col, 16)).astype(f32)
        return nn(jnp.where(chosen * 16.0 == target, 1.0, 0.0).astype(bf16), stack)

    def home_y(b):
        _, czs, czw, sb, yb = boxes[b][:5]
        for j in others:
            got(czs.at[j], b_r.at[b, 1 + j])
            got(czw.at[j], b_r.at[b, 5 + j])
        sb[...] = dense_rows(b, 1 - y).astype(bf16)
        send(("home", b), None, sb, yb, b_s.at[b, 9], b_r.at[b, 9], Y)

    def home_x(b):
        yb, xb = boxes[b][4:6]
        got(yb, b_r.at[b, 9])
        yb[...] = (dense_rows(b, y) + yb[...].astype(f32)).astype(bf16)
        send(("home", b), None, yb, xb, b_s.at[b, 10], b_r.at[b, 10], X)

    def home_rows(b):
        yb, xb, cb = boxes[b][4:7]
        got(xb, b_r.at[b, 10])
        xb[...] += yb[...]
        send(("home", b), None, xb.at[pl.ds(al((1 - c) * 32, 32), 32)], cb, b_s.at[b, 11], b_r.at[b, 11], C)

    def home_last(b):
        xb, cb = boxes[b][5:7]
        s0, ns, first, half = boxes[b][7]
        got(cb, b_r.at[b, 11])
        here, there = xb[pl.ds(al(c * 32, 32), 32)].astype(f32), cb[...].astype(f32)
        low, high = jnp.where(c == 0, here, there), jnp.where(c == 0, there, here)
        for s in range(ns):
            lanes = slice(s * 128, s * 128 + 128)
            split_sum[s0 + s] = jnp.concatenate([low[:, lanes], high[:, lanes]], axis=1)
        for w in range(half):
            lanes = slice(ns * 128 + w * 256, ns * 128 + w * 256 + 256)
            for q in range(4):
                wz[q, first + w] = low[q * 8 : q * 8 + 8, lanes]
                wz[q, first + half + w] = high[q * 8 : q * 8 + 8, lanes]
        slots = pl.ds(first, 2 * half)
        for k, j in enumerate(others):
            send(("home", b), None, wz.at[j, slots], whole_sum.at[z, slots], b_s.at[b, 12 + k], b_r.at[b, 12 + z], {"tp": j})
        pltpu.make_async_copy(wz.at[z, slots], whole_sum.at[z, slots], loc.at[count + 18 + b]).start()

    def home_done(b):
        first, half = boxes[b][7][2:]
        slots = pl.ds(first, 2 * half)
        for j in others:
            got(whole_sum.at[j, slots], b_r.at[b, 12 + j])
        pltpu.make_async_copy(wz.at[z, slots], whole_sum.at[z, slots], loc.at[count + 18 + b]).wait()

    def rows_back(src, dst, slot):
        def go():
            for k, j in enumerate(others):
                part = src.at[pl.ds(al(j * 112, 16), 112)]
                remote(part, dst.at[lax.rem(z, 2)], home_s.at[slot, k], home_r.at[slot, z], {"tp": j}).start()
            own_part(src, dst, slot).start()

        when(mine, go)

    def own_part(src, dst, slot):
        part = src.at[pl.ds(al(z * 112, 16), 112)]
        return pltpu.make_async_copy(part, dst.at[lax.rem(z, 2)], loc.at[count + 21 + slot])

    def rows_back_done(src, dst, slot):
        def go():
            for k, j in enumerate(others):
                part = src.at[pl.ds(al(j * 112, 16), 112)]
                remote(part, part, home_s.at[slot, k], home_r.at[slot, z], {"tp": j}).wait_send()
            own_part(src, dst, slot).wait()

        when(mine, go)
        for i in (0, 1):
            source = 2 * c + i
            when(source != z, lambda: got(dst.at[i], home_r.at[slot, source]))

    def enc_dst(quarter_of):
        return g_enc.at[lax.rem(z, 2), :, :, pl.ds(al(c * 512, 512), 512)]

    def enc_copy(j):
        part = gb.at[2 + j, 0:3, :, 0:512]
        owner = z // 2
        sems = home_s.at[2, j], home_r.at[2 + c, z]
        return part, owner, sems

    def enc_back(j):
        part, owner, (s, r) = enc_copy(j)
        when((j != z) | (c != owner), lambda: remote(part, enc_dst(j), s, r, {"tp": j, "core": owner}).start())
        when((j == z) & (c == owner), lambda: pltpu.make_async_copy(part, enc_dst(j), loc.at[count + 23]).start())

    def enc_back_done():
        for step in range(4):
            j = lax.rem(z + 1 + step, 4)
            part, owner, (s, r) = enc_copy(j)
            when((j != z) | (c != owner), lambda: remote(part, enc_dst(j), s, r, {"tp": j, "core": owner}).wait_send())
            when((j == z) & (c == owner), lambda: pltpu.make_async_copy(part, enc_dst(j), loc.at[count + 23]).wait())
        for i in (0, 1):
            for other in (0, 1):
                source = 2 * c + i
                when(
                    (source != z) | (c != other),
                    lambda: got(g_enc.at[i, :, :, other * 512 : other * 512 + 512], home_r.at[2 + other, source]),
                )

    def rank_in(first, s0, w0, inner, source, given):
        backs = jnp.concatenate([rank_t(split(first + i), g[...]) for i, g in enumerate(given)])
        down = nn(backs, source[...]).astype(bf16)
        for i, g in enumerate(given):
            gwhole[w0 + i] = down[16 * i : 16 * i + 16]
            gsplit[s0 + i] = nn(inner[16 * i : 16 * i + 16], g[...]).astype(bf16)

    def rank_out(side):
        s0, w0 = (12, 6) if side == 0 else (8, 2)
        gsplit[s0 + 3] = nn(rank_t(whole(7 + side), grads[...]), mix[side]).astype(bf16)
        gwhole[w0 + 3] = nn(t_mix[side], grads[...]).astype(bf16)

    def lane_sums(both):
        head = lax.broadcasted_iota(jnp.int32, (8, 128), 1) // HD
        pick_head = jnp.where(head == lax.broadcasted_iota(jnp.int32, (8, 128), 0), 1.0, 0.0).astype(bf16)
        high = both.astype(bf16)
        return nt(pick_head, high) + nt(pick_head, (both - high.astype(f32)).astype(bf16))

    def self_block():
        edge = 256
        length = rows.shape[0]

        def pair(p, carry):
            lanes = pair_lanes(p)
            qp, dop, kp, vp = q0[:, lanes], do[:, lanes], k0[:, lanes], v0[:, lanes]
            kt = kp.T
            logs = lse[0, p]
            totals = lane_sums(dop.astype(f32) * mix[0, :, lanes].astype(f32))
            first = lax.broadcasted_iota(jnp.int32, qp.shape, 1) < HD
            dqs, dks, dvs = [], [[], []], [[], []]
            for h in (0, 1):
                this = first == (h == 0)
                qm, dom = jnp.where(this, qp, 0), jnp.where(this, dop, 0)
                terms = []
                for b, (low, high, start) in enumerate(((0, edge, 0), (edge, length, edge))):
                    sc = nt(kp[low:high], qm[start:]) * SCALE
                    key = low + lax.broadcasted_iota(jnp.int32, sc.shape, 0)
                    query = start + lax.broadcasted_iota(jnp.int32, sc.shape, 1)
                    sc = jnp.where(query >= key, sc, HIDE)
                    probs = jnp.exp(sc - logs[h : h + 1, start:])
                    dvs[b].append(nn(probs.astype(bf16), dop[start:]))
                    dp = nt(vp[low:high], dom[start:])
                    ds = (probs * (dp - totals[h : h + 1, start:])).astype(bf16)
                    dks[b].append(nn(ds, qp[start:]))
                    terms.append(nn(kt[:, low:high], ds))
                joined = jnp.concatenate([terms[0][:, :edge], terms[0][:, edge:] + terms[1]], axis=1)
                dqs.append(joined[h * HD : (h + 1) * HD])
            for b, place in enumerate((slice(0, edge), slice(edge, length))):
                first_k = lax.broadcasted_iota(jnp.int32, dks[b][0].shape, 1) < HD
                dv0[place, lanes] = jnp.where(first_k, dvs[b][0], dvs[b][1]).astype(bf16)
                dk0[place, lanes] = (jnp.where(first_k, dks[b][0], dks[b][1]) * SCALE).astype(bf16)
            dq[:, lanes] = (jnp.concatenate(dqs).T * SCALE).astype(bf16)
            return carry

        lax.fori_loop(0, 4, pair, 0)

    def memory_half(h, q):
        rows_of = [pl.ds(al(m * 1024 + h * 512, 512), 512) for m in (4, 5)]
        place = pl.ds(al(q * 384, 128), 384)
        return nt(dk1[place], ga[rows_of[0]]) + nt(dv1[place], ga[rows_of[1]])

    def accumulator(p):
        return outbox.at[0, pl.ds(al(p // 2 * 128, 128), 128), pl.ds(al(lax.rem(p, 2) * 512, 512), rows.shape[0])]

    def cross_start():
        def pair(p, carry):
            lanes = pair_lanes(p)
            dsum[p] = lane_sums(do[:, lanes].astype(f32) * mix[1, :, lanes].astype(f32))
            accumulator(p)[...] = jnp.zeros((128, rows.shape[0]), f32)
            return carry

        lax.fori_loop(0, 4, pair, 0)

    def cross_block(q):
        place = pl.ds(al(q * 384, 128), 384)

        def pair(p, carry):
            lanes = pair_lanes(p)
            qp, dop = q1[:, lanes], do[:, lanes]
            kp, vp = k1[place, lanes], v1[place, lanes]
            kt = kp.T
            logs, totals = lse[1, p], dsum[p]
            first = lax.broadcasted_iota(jnp.int32, qp.shape, 1) < HD
            dqs, dks, dvs = [], [], []
            for h in (0, 1):
                this = first == (h == 0)
                sc = scores_t(kp, jnp.where(this, qp, 0), frames // groups, False)
                probs = jnp.exp(sc - logs[h : h + 1])
                dvs.append(nn(probs.astype(bf16), dop))
                dp = nt(vp, jnp.where(this, dop, 0))
                ds = (probs * (dp - totals[h : h + 1])).astype(bf16)
                dks.append(nn(ds, qp))
                dqs.append(nn(kt, ds)[h * HD : (h + 1) * HD])
            first_k = lax.broadcasted_iota(jnp.int32, kp.shape, 1) < HD
            dv1[place, lanes] = jnp.where(first_k, dvs[0], dvs[1]).astype(bf16)
            dk1[place, lanes] = (jnp.where(first_k, dks[0], dks[1]) * SCALE).astype(bf16)
            accumulator(p)[...] += jnp.concatenate(dqs)
            return carry

        lax.fori_loop(0, 4, pair, 0)

    def cross_end():
        def pair(p, carry):
            dq[:, pair_lanes(p)] = (accumulator(p)[...].T * SCALE).astype(bf16)
            return carry

        lax.fori_loop(0, 4, pair, 0)

    def enc_part(step):
        q = lax.rem(z + 1 + step, 4)
        sent_part = gb.at[2 + q, 0:3, :, 512:1024]
        sent_part[...] = memory_half(1 - c, q).astype(bf16).reshape(3, 128, 512)
        send("enc", None, sent_part, gb.at[2 + q, 0:3, :, 0:512], ex_s.at[6 + step], ex_r.at[6 + step], C)

    def enc_whole(step):
        q = lax.rem(z + 1 + step, 4)
        kept = gb.at[2 + q, 0:3, :, 0:512]
        got(kept, ex_r.at[6 + step])
        kept[...] = (memory_half(c, q).reshape(3, 128, 512) + kept[...].astype(f32)).astype(bf16)
        enc_back(q)

    dk1, dv1 = ga.at[pl.ds(6144, 1536)], ga.at[pl.ds(7680, 1536)]
    dk0, dv0 = dkv.at[0, 0:448], dkv.at[1, 0:448]
    part_out(3, 0)
    gwhole[0] = nn(r_in[...].astype(bf16), normed[2]).astype(bf16)
    gwhole[1] = nn(t_out[...].astype(bf16), grads[...]).astype(bf16)
    home_core(0)
    g_now[...] = grads[...].astype(f32) + norm_back(hidden[1], gain[2], part_sum(3, 0))
    part_out(2, 1)
    settle("rows")
    grads[...] = g_now[...].astype(bf16)
    do[...] = nt(grads[...], wb(1)).astype(bf16)
    home_z(0)
    normed[2] = (hidden[1] + part_sum(2, 1)).astype(bf16)
    rows_back(normed.at[2], acts, 0)
    settle(("part", 3))
    cross_start()
    cross_block(lax.rem(z + 1, 4))
    enc_part(0)
    cross_block(lax.rem(z + 2, 4))
    enc_part(1)
    enc_whole(0)
    home_y(0)
    cross_block(lax.rem(z + 3, 4))
    enc_part(2)
    enc_whole(1)
    rank_out(1)
    cross_block(z)
    cross_end()
    outbox[0] = nt(dq[...], wa(3))
    part_out(4, 0)
    enc_part(3)
    enc_whole(2)
    home_x(0)
    g_now[...] += norm_back(hidden[0], gain[1], part_sum(4, 0))
    grads[...] = g_now[...].astype(bf16)
    do[...] = nt(grads[...], wb(0)).astype(bf16)
    enc_whole(3)
    rank_in(3, 8, 2, t_query, normed.at[1], [dq])
    home_rows(0)
    self_block()
    settle(("part", 2))
    outbox[1] = nt(dq[...], wa(0))
    outbox[1] += nt(dk0[...], wa(1))
    outbox[1] += nt(dv0[...], wa(2))
    part_out(5, 1)
    home_last(0)
    rank_in(0, 12, 6, t_self, normed.at[0], [dq, dk0, dv0])
    rank_out(0)
    home_core(2)
    normed[0] = (g_now[...] + norm_back(rows[...].astype(f32), gain[0], part_sum(5, 1))).astype(bf16)
    rows_back(normed.at[0], g_tok, 1)
    home_z(2)
    rank_in(4, 9, 3, t_memory, memory, [dk1, dv1])
    home_core(1)
    home_y(2)
    home_z(1)
    home_x(2)
    home_y(1)
    home_rows(2)
    home_x(1)
    home_last(2)
    home_rows(1)
    home_last(1)
    for b in range(3):
        home_done(b)
    rows_back_done(normed.at[2], acts, 0)
    rows_back_done(normed.at[0], g_tok, 1)
    enc_back_done()
    for key in list(sent):
        settle(key)


def layer(tok, enc, cot, w_in, w_out, w_up, w_down, ids, gain, shift, *adapters):
    any_ = pl.BlockSpec(memory_space=pl.ANY)
    r, d = 448, tok.shape[2]
    padded = enc.shape[1]
    dma = pltpu.SemaphoreType.DMA

    def vm(*shape, dtype=bf16):
        return pltpu.VMEM(shape, dtype)

    n = 16
    halves = (1, 2, 2)
    splits = (8, 4, 4)
    widths = [s * 128 + w * 256 for s, w in zip(splits, halves, strict=True)]
    return pl.pallas_call(
        layer_kernel,
        out_shape=[
            sds((2, r // 4, d), bf16), sds((2, r // 4, d), bf16), sds((2, 3, padded // 12, d), bf16),
            sds((16, 32, 256), f32), sds((4, 10, 8, 256), f32),
        ],
        in_specs=[any_] * 7 + [VM] * 11,
        out_specs=[any_] * 3 + [VM, any_],
        scratch_shapes=[
            vm(10 * d, 512), vm(6, 4, 128, d), vm(r, d), vm(r, d), vm(padded, d), vm(3, r, d),
            vm(r, 512), vm(r, 512), vm(r, 512), vm(2, r, 512), vm(r, 512), vm(padded, 512), vm(padded, 512),
            vm(2, 4, 2, r, dtype=f32), vm(2, r, d, dtype=f32), vm(r, d, dtype=f32), vm(2, r, 512), vm(2, 512, 512),
            vm(2, r, d, dtype=f32), vm(2, r, d, dtype=f32),
            vm(4, 8, 128, dtype=f32), vm(512, 512), vm(320, 512), vm(64, 2048), vm(16, 5120), vm(2, 64, 2048), vm(2, 16, 5120),
            vm(4, 16, 2048), vm(2, 16, 5120), vm(16, r, dtype=f32), vm(16, r, dtype=f32), vm(2, 16, r),
            vm(16, 16, 512), vm(10, 16, d), vm(4, 10, 8, 256, dtype=f32), vm(4, 8, r, dtype=f32),
            vm(48, r), vm(16, r), vm(32, padded), vm(2, 16, r),
            *[vm(w, 16, d) for w in halves], *[vm(4, s, 16, 128) for s in splits], *[vm(4, w, 16, 256) for w in halves],
            *[vm(64, w) for w in widths], *[vm(64, w) for w in widths], *[vm(64, w) for w in widths], *[vm(32, w) for w in widths],
            dma((n,)), dma((n,)), dma((n, 4)), dma((n, 4)), dma((n, 4)), dma((n,)), dma((n,)), dma((n, 2)), dma((n, 2)),
            dma((3, 16)), dma((3, 16)), dma((n + 24,)), dma((12,)), dma((12,)), dma((10,)), dma((10,)),
            dma((3, 16)), dma((3, 16)), dma((4, 4)), dma((4, 4)),
        ],
        compiler_params=pltpu.CompilerParams(
            collective_id=1, has_side_effects=True, vmem_limit_bytes=int(62.5 * 1024 * 1024)
        ),
        name="layer",
    )(tok, enc, cot, w_in, w_out, w_up, w_down, ids, gain, shift, *adapters)


def swap_core(rows):
    return lax.ppermute(rows, "core", SWAP)


def core_sum(part):
    return part + swap_core(part)


def own_and_other(stacked):
    core = lax.axis_index("core")
    keep = lax.dynamic_index_in_dim(stacked, core, 0, keepdims=False)
    send = lax.dynamic_index_in_dim(stacked, 1 - core, 0, keepdims=False)
    return keep, swap_core(send)


def in_core_order(own, other):
    first = lax.axis_index("core") == 0
    return jnp.stack([jnp.where(first, own, other), jnp.where(first, other, own)])


def scatter_sh(stacked):
    n = lax.axis_size("sh")
    if n == 2:
        me = lax.axis_index("sh")
        keep = lax.dynamic_index_in_dim(stacked, me, 0, keepdims=False)
        send = lax.dynamic_index_in_dim(stacked, 1 - me, 0, keepdims=False)
        return keep + lax.ppermute(send, "sh", SWAP)
    return lax.psum_scatter(stacked, "sh", scatter_dimension=0, tiled=False)


def over_z(stacked):
    return lax.all_to_all(stacked, "tp", 0, 0, tiled=True)


def half_columns(rows):
    width = rows.shape[-1] // 2
    return lax.dynamic_slice_in_dim(rows, lax.axis_index("core") * width, width, rows.ndim - 1)


def rows_home(half):
    tp = lax.axis_size("tp")
    moved = over_z(half.reshape(tp, half.shape[0] // tp, half.shape[1]))
    own, other = own_and_other(moved.reshape(2, tp // 2, *moved.shape[1:]))
    both = in_core_order(own, other)
    return jnp.moveaxis(both, 0, 2).reshape(both.shape[1], both.shape[2], 2 * half.shape[1])


def rows_here(rows):
    tp = lax.axis_size("tp")
    both = in_core_order(rows, swap_core(rows)).reshape(4, *rows.shape[1:])
    moved = over_z(half_columns(both))
    moved = moved.reshape(tp * rows.shape[1], rows.shape[2] // 2)
    pair = in_core_order(moved, swap_core(moved))
    return jnp.concatenate([pair[0], pair[1]], axis=-1)


def gather_weights(w_attn_in, w_attn_out, w_up, w_down):
    def over_shard(block, axis):
        return lax.all_gather(block, ("sh", "core"), axis=axis, tiled=True)

    def over_tp(block, axis):
        return lax.all_gather(block, "tp", axis=axis, tiled=True)

    core = lax.axis_index("core")

    def half(block, axis):
        width = block.shape[axis] // 2
        return lax.dynamic_slice_in_dim(block, core * width, width, axis)

    w_in = over_tp(half(over_shard(w_attn_in.reshape(6, *w_attn_in.shape[3:]), 1), 2), 2)
    w_out = over_tp(half(over_shard(w_attn_out[0], 2), 1), 1)
    w_first = over_tp(half(over_shard(w_up[0], 0), 1), 1)
    w_second = over_tp(half(over_shard(w_down[0], 1), 0), 0)
    return w_in, w_out, w_first, w_second


def wide_parts(args):
    (
        tokens, encoded, cotangent, adapter_of, w_attn_in, w_attn_out, w_up, w_down, norm_gain, norm_shift,
        down_attn_in, up_attn_in, down_feed_in, up_feed_in, down_attn_out, up_attn_out, down_feed_out, up_feed_out,
    ) = args
    n, tp = lax.axis_size("sh"), lax.axis_size("tp")
    sh, core, z = lax.axis_index("sh"), lax.axis_index("core"), lax.axis_index("tp")
    width = w_attn_in.shape[3] * 2 * n
    held_rows = down_feed_in.shape[1]
    quarter = width // tp
    piece = quarter // 2

    ids = lax.all_gather(adapter_of, ("sh", "core"), tiled=True)

    row_ids = (sh * 2 + core) * held_rows + jnp.arange(held_rows)
    wanted = ids.reshape(n, tp)[:, :, None] * RANK + jnp.arange(RANK)
    picks = (wanted[..., None] == row_ids).astype(bf16)
    whole = jnp.concatenate(
        [
            down_attn_in.reshape(6, held_rows, width),
            down_feed_in,
            up_attn_out[0],
            up_feed_out,
        ]
    )
    def in_quarters(rows):
        return jnp.moveaxis(rows.reshape(held_rows, tp, quarter), 1, 0)

    split = jnp.concatenate(
        [
            up_attn_in.reshape(6, held_rows, quarter),
            in_quarters(up_feed_in[0]),
            down_attn_out[0],
            in_quarters(down_feed_out[0]),
        ]
    )
    picks_z = lax.dynamic_index_in_dim(picks, z, 1, keepdims=False)
    chosen_whole = jnp.einsum("srk,mkd->smrd", picks_z, whole, preferred_element_type=f32).astype(bf16)
    chosen_split = jnp.einsum("szrk,mkd->szmrd", picks, split, preferred_element_type=f32).astype(bf16)
    chosen_whole = core_sum(scatter_sh(chosen_whole))
    chosen_split = over_z(core_sum(scatter_sh(chosen_split)))

    def columns(first, count):
        mine = half_columns(chosen_split[:, first : first + count])
        return jnp.moveaxis(mine, 0, 2).reshape(count, RANK, tp * piece)

    def wide_columns(first):
        mine = lax.dynamic_slice_in_dim(chosen_split[:, first : first + tp], core * 2, 2, 1)
        return jnp.moveaxis(mine, 2, 0).reshape(RANK, tp * 2 * quarter)

    a_in, a_up, b_out, b_down = chosen_whole[:6], chosen_whole[6], chosen_whole[7:9], chosen_whole[9]
    b_in, b_up, a_out, a_down = columns(0, 6), wide_columns(6), columns(6 + tp, 2), wide_columns(8 + tp)

    w_in, w_out, w_first, w_second = gather_weights(w_attn_in, w_attn_out, w_up, w_down)
    taken = rows_here(tokens)
    upstream = rows_here(cotangent)
    mine = lax.dynamic_index_in_dim(encoded, z % 2, 0, keepdims=False)
    memory = jnp.where(core == z // 2, mine, swap_core(mine))

    def merge(weight, down_rows, up_rows):
        return (weight.astype(f32) + t_mm(down_rows, up_rows)).astype(bf16)

    w_in = [merge(w_in[i], a_in[i], b_in[i]) for i in range(6)]
    w_out = [merge(w_out[i], a_out[i], b_out[i]) for i in range(2)]
    w_first = merge(w_first, a_up, b_up)
    w_second = merge(w_second, a_down, b_down)

    gain, shift = norm_gain[0][:, None], norm_shift[0][:, None]
    frames = memory.shape[0]
    w_in = jnp.stack(w_in)
    normed0, q0, k0, v0, lse0, mix0, part = self_forward(taken, gain[0], shift[0], w_in[:3], w_out[0])
    k1, v1 = memory_project(memory, w_in[4:])
    hidden1, normed1, q1, lse1, mix1, part1 = cross_forward(
        taken, part, swap_core(part), gain[1], shift[1], w_in[3], k1, v1, w_out[1], frames
    )
    hidden2, part2, back, g_aup, g_bup, g_adown, g_bdown = feed(
        hidden1, part1, swap_core(part1), gain[2], shift[2], w_first, w_second, upstream, a_up, b_up, a_down, b_down
    )
    result = (hidden2 + core_sum(part2)).astype(bf16)
    grad, e1, dq1, dk1, dv1, back1 = cross_backward(
        hidden2, gain[2], upstream, back, swap_core(back), w_out[1], w_in[3], q1, k1, v1, lse1, frames
    )
    part = memory_backward(dk1, dv1, w_in[4:], frames)
    own, other = own_and_other(jnp.moveaxis(part.reshape(part.shape[0], 2, -1), 1, 0))
    memory_rows = (own.astype(f32) + other.astype(f32)).astype(bf16)
    grad, e0, dq0, dk0, dv0, back0 = self_backward(
        hidden1, gain[1], grad, back1, swap_core(back1), w_out[0], w_in[:3], q0, k0, v0, lse0
    )
    grad = final_norm(taken, gain[0], grad, back0, swap_core(back0))
    ranks1 = attention_ranks(normed1, memory, mix1, dq1, dk1, dv1, e1, a_in[3:], b_in[3:], a_out[1], b_out[1])
    ranks0 = attention_ranks(normed0, None, mix0, dq0, dk0, dv0, e0, a_in[:3], b_in[:3], a_out[0], b_out[0])
    feed_up = jnp.moveaxis(g_bup.reshape(RANK, tp, tp, piece), 2, 0).reshape(tp, RANK, tp * piece)
    feed_down = jnp.moveaxis(g_adown.reshape(RANK, tp, tp, piece), 2, 0).reshape(tp, RANK, tp * piece)
    out_split = jnp.stack([ranks0[2], ranks1[2]])
    out_whole = jnp.stack([ranks0[3], ranks1[3]])
    split_grads = jnp.concatenate([ranks0[1], ranks1[1], feed_up.astype(bf16), out_split, feed_down.astype(bf16)])
    whole_grads = jnp.concatenate(
        [ranks0[0], ranks1[0], g_aup.astype(bf16)[None], out_whole, g_bdown.astype(bf16)[None]]
    )
    here = ids.reshape(n, tp)[sh]
    return result, grad, memory_rows, split_grads, whole_grads, here


def narrow_parts(args):
    (
        tokens, encoded, cotangent, adapter_of, w_attn_in, w_attn_out, w_up, w_down, norm_gain, norm_shift,
        down_attn_in, up_attn_in, down_feed_in, up_feed_in, down_attn_out, up_attn_out, down_feed_out, up_feed_out,
    ) = args

    def six(rows):
        return rows.reshape(6, *rows.shape[3:])

    lines = jnp.pad(adapter_of.astype(f32), (0, 6))[:, None] * jnp.ones((1, 128), f32)
    _, frames, d = encoded.shape
    step = frames // 4
    spaced = jnp.pad(encoded.reshape(2, 4, step, d), ((0, 0), (0, 0), (0, 384 - step), (0, 0)))
    spaced = spaced.reshape(2, 1536, d)
    acts, g_tok, g_enc, split_sum, whole_sum = layer(
        tokens, spaced, cotangent, six(w_attn_in), w_attn_out[0], w_up[0], w_down[0], lines,
        norm_gain[0][:, None], norm_shift[0][:, None], six(down_attn_in), six(up_attn_in), down_feed_in[0],
        up_feed_in[0], down_attn_out[0], up_attn_out[0], down_feed_out[0], up_feed_out[0],
    )
    return (acts, *finish(g_tok, g_enc.reshape(2, 384, d)[:, :step].astype(f32), split_sum, whole_sum))


def finish(g_tok, g_enc, split_sum, whole_sum):
    held, d = split_sum.shape[1], g_tok.shape[2]
    part = whole_sum.shape[2]

    def kernel(tok, split_ref, whole_ref, out_tok, down_in, up_in, down_feed, up_feed, down_out, up_out, down_last, up_last):
        out_tok[...] = tok[...].astype(f32)

        def put_whole(out, slot):
            for q in range(4):
                out[:, q * 256 : q * 256 + 256] = whole_ref[q, slot]

        def put_wide(out, first):
            for core in range(2):
                for q in range(4):
                    place = core * 512 + q * 128
                    out[:, place : place + 128] = split_ref[first + q, :, core * 128 : core * 128 + 128]

        for side, (s0, w0) in enumerate(((12, 6), (8, 2))):
            for i in range(3):
                up_in[0, side, i] = split_ref[s0 + i]
                put_whole(down_in.at[0, side, i], w0 + i)
            down_out[0, side] = split_ref[s0 + 3]
            put_whole(up_out.at[0, side], w0 + 3)
        put_whole(down_feed.at[0], 0)
        put_whole(up_last.at[0], 1)
        put_wide(up_feed.at[0], 0)
        put_wide(down_last.at[0], 4)

    outs = pl.pallas_call(
        kernel,
        out_shape=[
            sds(g_tok.shape, f32), sds((1, 2, 3, part, d), f32), sds((1, 2, 3, held, 256), f32), sds((1, part, d), f32),
            sds((1, held, 1024), f32), sds((1, 2, held, 256), f32), sds((1, 2, part, d), f32), sds((1, held, 1024), f32),
            sds((1, part, d), f32),
        ],
        in_specs=[VM] * 3,
        out_specs=[VM] * 9,
        name="finish",
    )(g_tok, split_sum, whole_sum)
    return (outs[0], g_enc, *outs[1:])


def on_device(*args):
    if lax.axis_size("sh") == 2:
        return narrow_parts(args)
    n, tp = lax.axis_size("sh"), lax.axis_size("tp")
    held_rows, quarter = args[12].shape[1], args[11].shape[4]
    width, piece = quarter * tp, quarter // 2
    result, grad, memory_rows, split_grads, whole_grads, here = wide_parts(args)
    activations = rows_home(half_columns(result))
    grad_encoded = rows_home(memory_rows).astype(f32)
    grad_tokens = rows_home(half_columns(grad)).astype(f32)
    compact = jnp.moveaxis(split_grads.reshape(-1, RANK, tp, piece), 2, 0)
    own, other = own_and_other(jnp.moveaxis(whole_grads.reshape(-1, RANK, tp, 2, piece), (3, 2), (0, 1)))
    compact = jnp.concatenate([compact, own + other], axis=1)
    compact = over_z(compact)
    rows = jnp.arange(2 * n * held_rows)
    place = (here[:, None] * RANK + jnp.arange(RANK))[None] == rows[:, None, None]
    dense = jnp.einsum("gkr,kmrp->gmp", place.astype(bf16), compact, preferred_element_type=f32)
    dense = dense.astype(bf16).reshape(n, 2, held_rows, *dense.shape[1:])
    dense = scatter_sh(dense)
    dense = dense + lax.ppermute(dense, "rep", SWAP)
    both = in_core_order(*own_and_other(dense))
    done = jnp.moveaxis(both, 0, 2)
    count = 8 + 2 * tp
    sums = done[:, :count].astype(f32)

    def narrow(first, number):
        block = sums[:, first : first + number].reshape(held_rows, number, quarter)
        return jnp.moveaxis(block, 1, 0)

    def wide_of(first):
        block = jnp.moveaxis(sums[:, first : first + tp], 2, 1)
        return block.reshape(held_rows, 2 * tp * piece)

    grad_up_attn_in = narrow(0, 6).reshape(1, 2, 3, held_rows, quarter)
    grad_up_feed_in = wide_of(6)[None]
    grad_down_attn_out = narrow(6 + tp, 2)[None]
    grad_down_feed_out = wide_of(8 + tp)[None]
    rest = done[:, count:].reshape(tp, held_rows // tp, 10, quarter)
    rest = jnp.moveaxis(over_z(rest), 0, 2)
    rest = jnp.moveaxis(rest.reshape(held_rows // tp, 10, width), 1, 0).astype(f32)
    return (
        activations,
        grad_tokens,
        grad_encoded,
        rest[:6].reshape(1, 2, 3, held_rows // tp, width),
        grad_up_attn_in,
        rest[6:7],
        grad_up_feed_in,
        grad_down_attn_out,
        rest[7:9][None],
        grad_down_feed_out,
        rest[9:10],
    )


def solution(mesh):
    rep, shard, tp = (mesh.shape[name] for name in ("rep", "shard", "tp"))
    fine = Mesh(mesh.devices.reshape(rep, shard // 2, 2, tp), ("rep", "sh", "core", "tp"))
    shard = ("sh", "core")
    clips = ("rep", "sh", "core")
    both = ("sh", "core", "tp")
    placed = (
        P(clips, "tp", None),
        P(clips, None, None),
        P(clips, "tp", None),
        P(clips),
        P(None, None, None, shard, "tp"),
        P(None, None, "tp", shard),
        P(None, shard, "tp"),
        P(None, "tp", shard),
        P(),
        P(),
        P(None, None, None, shard, None),
        P(None, None, None, shard, "tp"),
        P(None, shard, None),
        P(None, shard, "tp"),
        P(None, None, shard, "tp"),
        P(None, None, shard, None),
        P(None, shard, "tp"),
        P(None, shard, None),
    )
    return jax.shard_map(
        on_device,
        mesh=fine,
        in_specs=placed,
        out_specs=(
            P(clips, "tp", None),
            P(clips, "tp", None),
            P(clips, "tp", None),
            P(None, None, None, both, None),
            P(None, None, None, shard, "tp"),
            P(None, both, None),
            P(None, shard, "tp"),
            P(None, None, shard, "tp"),
            P(None, None, both, None),
            P(None, shard, "tp"),
            P(None, both, None),
        ),
        check_vma=False,
    )
```

```python
import functools

import jax
import jax.numpy as jnp
from jax import lax
from jax.experimental import pallas as pl
from jax.experimental.pallas import tpu as pltpu
from jax.sharding import Mesh, PartitionSpec as P

HD = 64
RANK = 16
epsilon = 1e-05
masked_score = -1e30
f32, bf16 = jnp.float32, jnp.bfloat16
SWAP = ((0, 1), (1, 0))
MESH = pl.DeviceIdType.MESH


def dot(a, b, dims):
    return lax.dot_general(a, b, (dims, ((), ())), preferred_element_type=f32)


def mm(a, b):
    return dot(a, b, ((1,), (0,)))


def mm_t(a, b):
    return dot(a, b, ((1,), (1,)))


def t_mm(a, b):
    return dot(a, b, ((0,), (0,)))


HIDE = -1e30
SCALE = HD**-0.5
EPS = 1e-05
VM = pl.BlockSpec(memory_space=pltpu.VMEM)


def nn(a, b):
    return lax.dot_general(a, b, (((1,), (0,)), ((), ())), preferred_element_type=f32)


def nt(a, b):
    return lax.dot_general(a, b, (((1,), (1,)), ((), ())), preferred_element_type=f32)


def normalize(rows):
    centered = rows - jnp.mean(rows, axis=-1, keepdims=True)
    variance = jnp.mean(centered * centered, axis=-1, keepdims=True)
    inverse = lax.rsqrt(variance + EPS)
    return centered * inverse, inverse


def norm_back(rows, gain, grad):
    unit, inverse = normalize(rows)
    scaled = grad * gain
    first = jnp.mean(scaled, axis=-1, keepdims=True)
    second = jnp.mean(scaled * unit, axis=-1, keepdims=True)
    return (scaled - first - unit * second) * inverse


def pair_lanes(p):
    return pl.ds(pl.multiple_of(p * 128, 128), 128)


def scores_t(keys, queries, frames, causal, groups=1):
    s = nt(keys, queries * SCALE)
    if causal:
        key = lax.broadcasted_iota(jnp.int32, s.shape, 0)
        query = lax.broadcasted_iota(jnp.int32, s.shape, 1)
        s = jnp.where(query >= key, s, HIDE)
    elif frames < s.shape[0]:
        step, used = s.shape[0] // groups, frames // groups
        kept = used // 16 * 16
        key = kept + lax.broadcasted_iota(jnp.int32, (step - kept, s.shape[1]), 0)
        blocks = [s[g * step : (g + 1) * step] for g in range(groups)]
        s = jnp.concatenate([part for b in blocks for part in (b[:kept], jnp.where(key < used, b[kept:], HIDE))])
    return s


def attend_forward(q, k, v, mix, lse, frames, causal, start=0, number=None, groups=1):
    def pair(p, carry):
        lanes = pair_lanes(p)
        qp, kp = q[:, lanes], k[:, lanes]
        vt = v[:, lanes].T
        first = lax.broadcasted_iota(jnp.int32, qp.shape, 1) < HD
        outs, logs = [], []
        for h in (0, 1):
            s = scores_t(kp, jnp.where(first == (h == 0), qp, 0), frames, causal, groups)
            top = jnp.max(s, axis=0, keepdims=True)
            e = jnp.exp(s - top)
            total = jnp.sum(e, axis=0, keepdims=True)
            probs = (e * (1.0 / total)).astype(bf16)
            outs.append(nn(vt, probs)[h * HD : (h + 1) * HD])
            logs.append(top + jnp.log(total))
        mix[:, lanes] = jnp.concatenate(outs).T.astype(bf16)
        lse[p] = jnp.concatenate(logs)
        return carry

    lax.fori_loop(start, start + (number or q.shape[1] // 128), pair, 0)


def attend_backward(q, k, v, do, lse, dq, dk, dv, frames, causal, start=0, number=None, groups=1):
    def pair(p, carry):
        lanes = pair_lanes(p)
        qp, kp, vp, dop = q[:, lanes], k[:, lanes], v[:, lanes], do[:, lanes]
        kt = kp.T
        logs = lse[p]
        first = lax.broadcasted_iota(jnp.int32, qp.shape, 1) < HD
        dqs, dks, dvs = [], [], []
        for h in (0, 1):
            mine = first == (h == 0)
            s = scores_t(kp, jnp.where(mine, qp, 0), frames, causal, groups)
            probs = jnp.exp(s - logs[h : h + 1])
            dvs.append(nn(probs.astype(bf16), dop))
            dp = nt(vp, jnp.where(mine, dop, 0))
            t = probs * dp
            ds = (t - probs * jnp.sum(t, axis=0, keepdims=True)).astype(bf16)
            dks.append(nn(ds, qp))
            dqs.append(nn(kt, ds)[h * HD : (h + 1) * HD])
        first_k = lax.broadcasted_iota(jnp.int32, kp.shape, 1) < HD
        dv[:, lanes] = jnp.where(first_k, dvs[0], dvs[1]).astype(bf16)
        dk[:, lanes] = (jnp.where(first_k, dks[0], dks[1]) * SCALE).astype(bf16)
        dq[:, lanes] = (jnp.concatenate(dqs).T * SCALE).astype(bf16)
        return carry

    lax.fori_loop(start, start + (number or q.shape[1] // 128), pair, 0)


def params():
    return pltpu.CompilerParams(vmem_limit_bytes=60 * 1024 * 1024)


def sds(shape, dtype):
    return jax.ShapeDtypeStruct(shape, dtype)


def self_forward(tok, gain, shift, wi, wo):
    def kernel(tok, gain, shift, wi, wo, normed, q, k, v, lse, mix, part):
        unit, _ = normalize(tok[...].astype(f32))
        normed[...] = (unit * gain[...] + shift[...]).astype(bf16)
        for i, out in enumerate((q, k, v)):
            out[...] = nn(normed[...], wi[i]).astype(bf16)
        attend_forward(q, k, v, mix, lse, tok.shape[0], True)
        part[...] = nn(mix[...], wo[...])

    r, d = tok.shape
    w = wi.shape[2]
    return pl.pallas_call(kernel, out_shape=[sds((r, d), bf16)] + [sds((r, w), bf16)] * 3 + [sds((w // 128, 2, r), f32), sds((r, w), bf16), sds((r, d), f32)],
        in_specs=[VM] * 5, out_specs=[VM] * 7, compiler_params=params(), name="self_forward")(tok, gain, shift, wi, wo)


def memory_project(enc, wi):
    def kernel(enc, wi, k, v):
        frames = enc.shape[0]
        for i, out in enumerate((k, v)):
            out[:frames] = nn(enc[...], wi[i]).astype(bf16)
            out[frames:] = jnp.zeros((out.shape[0] - frames, out.shape[1]), bf16)
    frames = -(-enc.shape[0] // 128) * 128
    return pl.pallas_call(kernel, out_shape=[sds((frames, wi.shape[2]), bf16)] * 2, in_specs=[VM] * 2, out_specs=[VM] * 2, compiler_params=params(), name="memory_project")(enc, wi)


def cross_forward(hid, part, other, gain, shift, wq, k, v, wo, frames):
    def kernel(hid, part, other, gain, shift, wq, k, v, wo, hidden, normed, q, lse, mix, out):
        hidden[...] = hid[...].astype(f32) + part[...] + other[...]
        unit, _ = normalize(hidden[...])
        normed[...] = (unit * gain[...] + shift[...]).astype(bf16)
        q[...] = nn(normed[...], wq[...]).astype(bf16)
        attend_forward(q, k, v, mix, lse, frames, False)
        out[...] = nn(mix[...], wo[...])

    r, d = hid.shape
    w = wq.shape[1]
    return pl.pallas_call(kernel, out_shape=[sds((r, d), f32), sds((r, d), bf16), sds((r, w), bf16), sds((w // 128, 2, r), f32), sds((r, w), bf16), sds((r, d), f32)],
        in_specs=[VM] * 9, out_specs=[VM] * 6, compiler_params=params(), name="cross_forward")(hid, part, other, gain, shift, wq, k, v, wo)


def rank_t(rows16, inputs):
    return nt(rows16, inputs).astype(bf16)


def feed(hid, part, other, gain, shift, up, down, e, a_up, b_up, a_down, b_down):
    CH = 512

    def kernel(hid, part, other, gain, shift, up, down, e, a_up, b_up, a_down, b_down, hidden, out, back, g_aup, g_bup, g_adown, g_bdown, normed):
        hidden[...] = hid[...] + part[...] + other[...]
        unit, _ = normalize(hidden[...])
        normed[...] = (unit * gain[...] + shift[...]).astype(bf16)
        t_in = rank_t(a_up[...], normed[...])
        r_out = rank_t(b_down[...], e[...])
        r_in = jnp.zeros((16, hid.shape[0]), f32)
        t_out = jnp.zeros((16, hid.shape[0]), f32)
        for j in range(up.shape[1] // CH):
            cols = slice(j * CH, (j + 1) * CH)
            pre = nn(normed[...], up[:, cols])
            cdf = 0.5 * (1.0 + lax.erf(pre * (2**-0.5)))
            active = (pre * cdf).astype(bf16)
            slope = cdf + pre * jnp.exp(-0.5 * pre * pre) * 0.3989422804014327
            grad = (nt(e[...], down[cols]) * slope).astype(bf16)
            term, term_b = nn(active, down[cols]), nt(grad, up[:, cols])
            if j == 0:
                out[...], back[...] = term, term_b
            else:
                out[...] += term
                back[...] += term_b
            g_bup[:, cols] = nn(t_in, grad)
            g_adown[:, cols] = nn(r_out, active)
            r_in += nt(b_up[:, cols], grad)
            t_out += nt(a_down[:, cols], active)
        g_aup[...] = nn(r_in.astype(bf16), normed[...])
        g_bdown[...] = nn(t_out.astype(bf16), e[...])

    r, d = hid.shape
    w = up.shape[1]
    return pl.pallas_call(kernel, out_shape=[sds((r, d), f32)] * 3 + [sds((16, d), f32), sds((16, w), f32), sds((16, w), f32), sds((16, d), f32)],
        in_specs=[VM] * 12, out_specs=[VM] * 7, scratch_shapes=[pltpu.VMEM((r, d), bf16)], compiler_params=params(), name="feed")(
            hid, part, other, gain, shift, up, down, e, a_up, b_up, a_down, b_down)


def cross_backward(hid3, gain3, g, part, other, wo, wq, q, k, v, lse, frames):
    def kernel(hid3, gain3, g, part, other, wo, wq, q, k, v, lse, g_out, e, dq, dk, dv, back, do):
        g_out[...] = g[...].astype(f32) + norm_back(hid3[...], gain3[...], part[...] + other[...])
        e[...] = g_out[...].astype(bf16)
        do[...] = nt(e[...], wo[...]).astype(bf16)
        attend_backward(q, k, v, do, lse, dq, dk, dv, frames, False)
        back[...] = nt(dq[...], wq[...])

    r, d = hid3.shape
    w, f = q.shape[1], k.shape[0]
    return pl.pallas_call(kernel, out_shape=[sds((r, d), f32), sds((r, d), bf16), sds((r, w), bf16), sds((f, w), bf16), sds((f, w), bf16), sds((r, d), f32)],
        in_specs=[VM] * 11, out_specs=[VM] * 6, scratch_shapes=[pltpu.VMEM((r, w), bf16)], compiler_params=params(), name="cross_backward")(
            hid3, gain3, g, part, other, wo, wq, q, k, v, lse)


def self_backward(hid2, gain2, g, part, other, wo, wi, q, k, v, lse):
    def kernel(hid2, gain2, g, part, other, wo, wi, q, k, v, lse, g_out, e, dq, dk, dv, back, do):
        g_out[...] = g[...] + norm_back(hid2[...], gain2[...], part[...] + other[...])
        e[...] = g_out[...].astype(bf16)
        do[...] = nt(e[...], wo[...]).astype(bf16)
        attend_backward(q, k, v, do, lse, dq, dk, dv, q.shape[0], True)
        back[...] = nt(dq[...], wi[0])
        back[...] += nt(dk[...], wi[1])
        back[...] += nt(dv[...], wi[2])

    r, d = hid2.shape
    w = q.shape[1]
    return pl.pallas_call(kernel, out_shape=[sds((r, d), f32), sds((r, d), bf16)] + [sds((r, w), bf16)] * 3 + [sds((r, d), f32)],
        in_specs=[VM] * 11, out_specs=[VM] * 6, scratch_shapes=[pltpu.VMEM((r, w), bf16)], compiler_params=params(), name="self_backward")(
            hid2, gain2, g, part, other, wo, wi, q, k, v, lse)


def final_norm(hid, gain, g, part, other):
    def kernel(hid, gain, g, part, other, out):
        out[...] = (g[...] + norm_back(hid[...].astype(f32), gain[...], part[...] + other[...])).astype(bf16)

    return pl.pallas_call(kernel, out_shape=sds(hid.shape, bf16), in_specs=[VM] * 5, out_specs=VM, compiler_params=params(), name="final_norm")(hid, gain, g, part, other)


def memory_backward(dk, dv, wi, frames):
    def kernel(dk, dv, wi, out):
        out[...] = (nt(dk[:frames], wi[0]) + nt(dv[:frames], wi[1])).astype(bf16)
    d = wi.shape[1]
    return pl.pallas_call(kernel, out_shape=sds((frames, d), bf16), in_specs=[VM] * 3, out_specs=VM, compiler_params=params(), name="memory_backward")(dk, dv, wi)


def attention_ranks(normed, source, mix, dq, dk, dv, e, a_in, b_in, a_out, b_out):
    def kernel(*refs):
        operands, results = refs[:-4], refs[-4:]
        given = operands[:7] if source is not None else operands[:1] + operands[:1] + operands[1:6]
        normed, source_, mix, dq, dk, dv, e = given
        a_in, b_in, a_out, b_out = operands[-4:]
        ga_in, gb_in, ga_out, gb_out = results
        for i, (u, g) in enumerate(((normed, dq), (source_, dk), (source_, dv))):
            rows = u.shape[0]
            inner = rank_t(a_in[i], u[...])
            back = rank_t(b_in[i], g[:rows])
            gb_in[i] = nn(inner, g[:rows]).astype(bf16)
            ga_in[i] = nn(back, u[...]).astype(bf16)
        ga_out[...] = nn(rank_t(b_out[...], e[...]), mix[...]).astype(bf16)
        gb_out[...] = nn(rank_t(a_out[...], mix[...]), e[...]).astype(bf16)

    args = [normed] + ([source] if source is not None else []) + [mix, dq, dk, dv, e, a_in, b_in, a_out, b_out]
    return pl.pallas_call(kernel, out_shape=[sds(t.shape, bf16) for t in (a_in, b_in, a_out, b_out)],
        in_specs=[VM] * len(args), out_specs=[VM] * 4, compiler_params=params(), name="attention_ranks")(*args)


OFFS = (1, 3, 5, 7, 9)


class Unit:
    def __init__(self, place, kind, index):
        self.place, self.tall, self.index = place, kind == "a", index
        self.rows = 512 if self.tall else 128
        late = place >= 12
        if self.tall:
            self.most, self.via_y = (448, 352) if late else (384, 288)
        else:
            self.most, self.via_y = (112, 96) if late else (96, 64)


def make_units():
    order = [("a", 0), ("a", 1), ("a", 2), ("b", 0), ("a", 3), ("a", 4), ("a", 5), ("b", 1)]
    for j in range(4):
        order += [("a", 6 + j), ("b", 2 + j)]
    return [Unit(i, kind, index) for i, (kind, index) in enumerate(order)]


def layer_kernel(
    tok, enc, cot, w_in, w_out, w_up, w_down, ids, gain, shift,
    d_ai, u_ai, d_fi, u_fi, d_ao, u_ao, d_fo, u_fo,
    acts, g_tok, g_enc, split_sum, whole_sum,
    ga, gb, rows, grads, memory, normed, q0, k0, v0, mix, q1, k1, v1, lse, hidden, g_now, dd, dkv,
    outbox, inbox, idbuf, rs, rw, ys, yw, ys_own, yw_own, fz, fw, r_in, t_out, r_up, gsplit, gwhole, wz, dsum, t_self, t_query, t_memory, t_mix,
    rwb0, rwb1, rwb2, czs0, czs1, czs2, czw0, czw1, czw2, sb0, sb1, sb2, yb0, yb1, yb2, xb0, xb1, xb2, cb0, cb1, cb2,
    core_s, core_r, up_s, dn_s, z_r, y_s, y_r, x_s, x_r, row_s, row_r, loc, ad_s, ad_r, ex_s, ex_r, b_s, b_r, home_s, home_r,
):
    units = make_units()
    count = len(units)
    frames, groups = 1500 * enc.shape[1] // 1536, 4
    do, dq = dd.at[0], dd.at[1]
    x, y, c, z = (lax.axis_index(a) for a in ("rep", "sh", "core", "tp"))
    al = pl.multiple_of
    sent = {}

    def when(cond, fn):
        fn() if cond is None else pl.when(cond)(fn)

    def remote(src, dst, s, r, dev):
        return pltpu.make_async_remote_copy(
            src_ref=src, dst_ref=dst, send_sem=s, recv_sem=r, device_id=dev, device_id_type=MESH
        )

    def send(key, cond, src, dst, s, r, dev):
        when(cond, lambda: remote(src, dst, s, r, dev).start())
        sent.setdefault(key, []).append((cond, lambda: remote(src, dst, s, r, dev).wait_send()))

    def settle(key):
        for cond, fn in sent.pop(key, []):
            when(cond, fn)

    X, Y, C = {"rep": 1 - x}, {"sh": 1 - y}, {"core": 1 - c}
    YC = {"sh": 1 - y, "core": 1 - c}
    UP, DOWN = {"tp": z + 1}, {"tp": z - 1}
    others = [lax.rem(z + k, 4) for k in (1, 2, 3)]

    def got(dst, r):
        remote(dst, dst, r, r, X).wait_recv()

    bar = pltpu.get_barrier_semaphore()
    for dev in [X, Y, C, YC] + [{"tp": j} for j in others] + [{"tp": j, "core": 1 - c} for j in others]:
        pl.semaphore_signal(bar, inc=1, device_id=dev, device_id_type=MESH)
    pl.semaphore_wait(bar, 10)

    def block(u, yy, zz, first, size):
        if u.tall:
            return ga.at[pl.ds(al(u.index * 1024 + yy * 512 + first, 16), size), pl.ds(al(zz * 128, 128), 128)]
        return gb.at[u.index, zz, pl.ds(al(first, 16), size), pl.ds(al(yy * 512, 512), 512)]

    def across(u, yy, first, size):
        if u.tall:
            return ga.at[pl.ds(al(u.index * 1024 + yy * 512 + first, 16), size)]
        return gb.at[u.index, :, pl.ds(al(first, 16), size), pl.ds(al(yy * 512, 512), 512)]

    def three(u, first, size):
        if u.tall:
            return ga.at[pl.ds(al(u.index * 1024 + y * 512 + first, 16), size), 0:384]
        return gb.at[u.index, 0:3, pl.ds(al(first, 16), size), pl.ds(al(y * 512, 512), 512)]

    def half_src(u, cc):
        m = u.index
        if u.tall:
            if m < 6:
                return w_in.at[m, :, pl.ds(al(cc * 128, 128), 128)]
            return w_up.at[:, pl.ds(al(cc * 512 + (m - 6) * 128, 128), 128)]
        if m < 2:
            return w_out.at[m, pl.ds(al(cc * 128, 128), 128)]
        return w_down.at[pl.ds(al(cc * 512 + (m - 2) * 128, 128), 128)]

    def half_dst(u, cc):
        if u.tall:
            return block(u, y, z, cc * 256, 256)
        return gb.at[u.index, z, :, pl.ds(al(y * 512 + cc * 256, 256), 256)]

    def core_exchange(u):
        i = u.place
        send("core", None, half_src(u, 1 - c), half_dst(u, c), core_s.at[i], core_r.at[i], C)
        pltpu.make_async_copy(half_src(u, c), half_dst(u, c), loc.at[i]).start()

    def to_y(u, j):
        b = block(u, y, j, x * (u.rows - u.via_y), u.via_y)
        remote(b, b, y_s.at[u.place], y_r.at[u.place], Y).start()

    def own(u):
        i = u.place
        got(half_dst(u, 1 - c), core_r.at[i])
        pltpu.make_async_copy(half_src(u, c), half_dst(u, c), loc.at[i]).wait()
        zb = block(u, y, z, x * (u.rows - u.most), u.most)
        send(i, z < 3, zb, zb, up_s.at[i, z], z_r.at[i, z], UP)
        send(i, z > 0, zb, zb, dn_s.at[i, z], z_r.at[i, z], DOWN)
        to_y(u, z)

    def hop(u, k):
        i = u.place
        ways = (
            (z >= k, z - k, (z >= k) & (z < 3), UP, up_s),
            (z + k <= 3, z + k, (z + k <= 3) & (z > 0), DOWN, dn_s),
        )
        for ok, j, more, dev, sems in ways:
            zb = block(u, y, j, x * (u.rows - u.most), u.most)

            def arrive(zb=zb, j=j):
                got(zb, z_r.at[i, j])
                to_y(u, j)
                b = block(u, y, j, x * u.most, u.rows - u.most)
                remote(b, b, x_s.at[i, 0], x_r.at[i, 0], X).start()

            when(ok, arrive)
            send(i, more, zb, zb, sems.at[i, j], z_r.at[i, j], dev)

    def cross(u):
        i = u.place
        got(across(u, 1 - y, x * (u.rows - u.via_y), u.via_y), y_r.at[i])
        b = across(u, 1 - y, x * u.via_y, u.rows - u.via_y)
        send(i, None, b, b, x_s.at[i, 1], x_r.at[i, 1], X)

    def last(u):
        i = u.place
        got(three(u, (1 - x) * u.most, u.rows - u.most), x_r.at[i, 0])
        got(across(u, 1 - y, (1 - x) * u.via_y, u.rows - u.via_y), x_r.at[i, 1])
        b = across(u, y, x * (u.rows - u.via_y), u.via_y)
        remote(b, b, y_s.at[i], y_r.at[i], Y).wait_send()
        b = three(u, x * u.most, u.rows - u.most)
        remote(b, b, x_s.at[i, 0], x_r.at[i, 0], X).wait_send()
        settle(i)

    mine = c == z // 2

    def rows_out(src, dst, slot):
        for i in (0, 1):
            zd = 2 * c + i
            d = dst.at[pl.ds(al(z * 112, 16), 112)]
            send("rows", zd != z, src.at[i], d, row_s.at[slot, i], row_r.at[slot, z], {"tp": zd})
            when(
                zd == z,
                lambda i=i, d=d: pltpu.make_async_copy(src.at[i], d, loc.at[count + slot]).start(),
            )

    def rows_in(dst, slot):
        def wait():
            for j in others:
                got(dst.at[pl.ds(al(j * 112, 16), 112)], row_r.at[slot, j])
            d = dst.at[pl.ds(al(z * 112, 16), 112)]
            pltpu.make_async_copy(d, d, loc.at[count + slot]).wait()

        when(mine, wait)
        send("rows", mine, dst, dst, row_s.at[slot, 2], row_r.at[slot, 4], C)

    def rows_have(dst, slot):
        when(c != z // 2, lambda: got(dst, row_r.at[slot, 4]))

    parts = [slice(t * 96, (t + 1) * 96) for t in range(16)]

    def enc_local(t):
        return pltpu.make_async_copy(
            enc.at[lax.rem(z, 2), parts[t]], memory.at[parts[t]], loc.at[count + 2 + t]
        )

    def enc_send(t):
        send(
            "enc", mine, enc.at[lax.rem(z, 2), parts[t]], memory.at[parts[t]], row_s.at[2, t], row_r.at[2, t], C
        )
        when(mine, lambda: enc_local(t).start())

    def enc_have():
        for t in range(16):
            when(mine, lambda: enc_local(t).wait())
            when(c != z // 2, lambda: got(memory.at[parts[t]], row_r.at[2, t]))

    me = 2 * y + c

    def ids_out():
        for k, dev in enumerate((C, Y, YC)):
            send("ids", None, ids, idbuf.at[me], ad_s.at[k], ad_r.at[k], dev)
        idbuf[pl.ds(me, 1)] = ids[...][None]

    def adapters_pick():
        for k, s in enumerate((2 * y + 1 - c, 2 * (1 - y) + c, 2 * (1 - y) + 1 - c)):
            got(idbuf.at[s], ad_r.at[k])
        held = lax.broadcasted_iota(jnp.int32, (128, 32), 1) + me * 32
        rank = lax.rem(lax.broadcasted_iota(jnp.int32, (128, 32), 0), 16)
        lines = [
            [jnp.broadcast_to(idbuf[2 * s + k // 2, k % 2 : k % 2 + 1, :32], (16, 32)) for k in range(4)]
            for s in range(2)
        ]
        wanted = jnp.concatenate([line for pair in lines for line in pair])
        target = held.astype(f32) - rank.astype(f32)
        picks = jnp.where(wanted * 16.0 == target, 1.0, 0.0).astype(bf16)
        here = []
        for s in range(2):
            line = lines[s][0]
            for k in (1, 2, 3):
                line = jnp.where(z == k, lines[s][k], line)
            here.append(line)
        picks_z = jnp.where(jnp.concatenate(here) * 16.0 == target[:32], 1.0, 0.0).astype(bf16)
        for h in range(2):
            cols = slice(h * 128, h * 128 + 128)
            wide = slice(h * 512, h * 512 + 512)
            given = [u_ai[m][:, cols] for m in range(6)] + [u_fi[:, wide]]
            given += [d_ao[m][:, cols] for m in range(2)] + [d_fo[:, wide]]
            for b in range(4):
                block_of = jnp.concatenate(given, axis=1)[:, b * 512 : b * 512 + 512]
                dkv[h, b * 128 : b * 128 + 128] = nn(picks, block_of).astype(bf16)
            if h == 0:
                given = [d_ai[m] for m in range(5)]
            else:
                given = [d_ai[5], d_fi, u_ao[0], u_ao[1], u_fo]
            for b in range(10):
                block_of = given[b // 2][:, b % 2 * 512 : b % 2 * 512 + 512]
                dd[h, b * 32 : b * 32 + 32] = nn(picks_z, block_of).astype(bf16)
        send("pick", None, dkv.at[1 - c], rs, ad_s.at[3], ad_r.at[3], C)
        send("pick", None, dd.at[1 - c, 0:320], rw, ad_s.at[4], ad_r.at[4], C)

    def adapters_y():
        got(rs, ad_r.at[3])
        got(rw, ad_r.at[4])
        rs[...] += dkv[pl.ds(c, 1)][0]
        rw[...] += dd[pl.ds(c, 1), 0:320][0]
        for b in range(4):
            for k in range(2):
                ys_own[k, :, b * 512 : b * 512 + 512] = rs[b * 128 + k * 64 : b * 128 + k * 64 + 64]
        for b in range(10):
            for k in range(2):
                yw_own[k, :, b * 512 : b * 512 + 512] = rw[b * 32 + k * 16 : b * 32 + k * 16 + 16]
        send("pick", None, ys_own.at[1 - y], ys, ad_s.at[5], ad_r.at[5], Y)
        send("pick", None, yw_own.at[1 - y], yw, ad_s.at[6], ad_r.at[6], Y)

    def adapters_z():
        got(ys, ad_r.at[5])
        got(yw, ad_r.at[6])
        ys[...] += ys_own[pl.ds(y, 1)][0]
        fw[pl.ds(c, 1)] = (yw[...] + yw_own[pl.ds(y, 1)][0])[None]
        for k, j in enumerate(others):
            send("pick", None, ys.at[pl.ds(al(j * 16, 16), 16)], fz.at[z], ad_s.at[7 + k], ad_r.at[7 + z], {"tp": j})
        fz[pl.ds(z, 1)] = ys[pl.ds(al(z * 16, 16), 16)][None]
        send("pick", None, fw.at[c], fw.at[c], ad_s.at[11], ad_r.at[11], C)

    def adapters_have():
        for j in others:
            got(fz.at[j], ad_r.at[7 + j])
        got(fw.at[1 - c], ad_r.at[11])
        settle("pick")
        settle("ids")

    def whole(m):
        return fw[m // 5, :, (m % 5) * 1024 : (m % 5) * 1024 + 1024]

    def split(s):
        return jnp.concatenate([fz[k, :, s * 128 : s * 128 + 128] for k in range(4)], axis=1)

    def merge(u):
        m = u.index
        if u.tall:
            down_t = whole(min(m, 6)).T
            up_rows = split(m)
            for b in range(4):
                place = slice(m * 1024 + b * 256, m * 1024 + b * 256 + 256)
                ga[place] = (ga[place].astype(f32) + nn(down_t[b * 256 : b * 256 + 256], up_rows)).astype(bf16)
        else:
            down_t = split(10 + m).T
            up_rows = whole(7 + m if m < 2 else 9)
            for k in range(4):
                gb[m, k] = (gb[m, k].astype(f32) + nn(down_t[k * 128 : k * 128 + 128], up_rows)).astype(bf16)

    def wa(m):
        return ga[m * 1024 : (m + 1) * 1024]

    def wb(m):
        return gb[m].reshape(512, 1024)

    def part_out(e, slot):
        send(("part", e), None, outbox.at[slot], inbox.at[slot], ex_s.at[e], ex_r.at[e], C)

    def part_sum(e, slot):
        got(inbox.at[slot], ex_r.at[e])
        return outbox[slot] + inbox[slot]

    def part_two(e, slot, fill):
        for h in range(2):
            half = slice(h * 512, h * 512 + 512)
            outbox[slot, :, half] = fill(h)
            here, there = outbox.at[slot, :, half], inbox.at[slot, :, half]
            send(("part", e), None, here, there, ex_s.at[e + 6 * h], ex_r.at[e + 6 * h], C)

    def part_two_sum(e, slot):
        for h in range(2):
            got(inbox.at[slot, :, h * 512 : h * 512 + 512], ex_r.at[e + 6 * h])
        return outbox[slot] + inbox[slot]

    def wa_half(m, h):
        return ga[m * 1024 + h * 512 : m * 1024 + h * 512 + 512]

    def norm_rows(side, source):
        unit, _ = normalize(source)
        normed[side] = (unit * gain[side] + shift[side]).astype(bf16)

    def start_rows():
        rows_have(rows, 0)
        norm_rows(0, rows[...].astype(f32))

    def project(m, source, out, length):
        def run():
            out[:length] = nn(source(), wa(m)).astype(bf16)
        return run

    def attention(side, first, number):
        q, k, v = ((q0, k0, v0), (q1, k1, v1))[side]
        length = (rows.shape[0], frames)[side]
        return lambda: attend_forward(q, k, v, mix.at[side], lse.at[side], length, side == 0, first, number, groups)

    def part0():
        outbox[0] = nn(mix[0], wb(0))
        part_out(0, 0)

    def second_rows():
        hidden[0] = rows[...].astype(f32) + part_sum(0, 0)
        norm_rows(1, hidden[0])

    def part1():
        outbox[1] = nn(mix[1], wb(1))
        part_out(1, 1)

    def third_rows():
        hidden[1] = hidden[0] + part_sum(1, 1)
        norm_rows(2, hidden[1])
        rows_have(grads, 1)

    def feed_first():
        settle(("part", 0))
        settle(("part", 1))
        r_up[0] = rank_t(whole(6), normed[2])
        r_up[1] = rank_t(whole(9), grads[...])

    def chunk(j):
        def run():
            up, down = wa(6 + j), wb(2 + j)
            pre = nn(normed[2], up)
            cdf = 0.5 * (1.0 + lax.erf(pre * (2**-0.5)))
            active = (pre * cdf).astype(bf16)
            slope = cdf + pre * jnp.exp(-0.5 * pre * pre) * 0.3989422804014327
            grad = (nt(grads[...], down) * slope).astype(bf16)
            if j == 0:
                outbox[1] = nn(active, down)
                outbox[0] = nt(grad, up)
                r_in[...] = nt(split(6 + j), grad)
                t_out[...] = nt(split(12 + j), active)
            else:
                outbox[1] += nn(active, down)
                outbox[0] += nt(grad, up)
                r_in[...] += nt(split(6 + j), grad)
                t_out[...] += nt(split(12 + j), active)
            gsplit[j] = nn(r_up[0], grad).astype(bf16)
            gsplit[4 + j] = nn(r_up[1], active).astype(bf16)
        return run

    def ranks_of(out, first, number, source):
        def run():
            stack = jnp.concatenate([whole(first + i) for i in range(number)])
            out[...] = rank_t(stack, source())
        return run

    def mix_rank(side):
        def run():
            t_mix[side] = rank_t(split(10 + side), mix[side])
        return run

    tasks = {}

    def task(tick, fn):
        tasks.setdefault(tick, []).append(fn)

    task(1, adapters_pick)
    task(4, adapters_y)
    task(8, adapters_z)
    task(12, adapters_have)
    task(12, lambda: rows_in(rows, 0))
    first = 13
    task(first, start_rows)
    for u in units:
        task(max(first, 2 * u.place + OFFS[4]), functools.partial(merge, u))
    for tick, fn in (
        (first + 1, project(0, lambda: normed[0], q0, 448)),
        (first + 2, project(1, lambda: normed[0], k0, 448)),
        (first + 2, project(2, lambda: normed[0], v0, 448)),
        (first + 3, attention(0, 0, 2)),
        (first + 4, attention(0, 2, 2)),
        (first + 5, part0),
        (first + 6, ranks_of(t_self, 0, 3, lambda: normed[0])),
        (first + 6, mix_rank(0)),
        (first + 7, second_rows),
        (first + 7, project(3, lambda: normed[1], q1, 448)),
        (first + 8, ranks_of(t_query, 3, 1, lambda: normed[1])),
        (first + 8, enc_have),
        (first + 8, project(4, lambda: memory[...], k1, 1536)),
        (first + 9, ranks_of(t_memory, 4, 2, lambda: memory[...])),
        (first + 10, project(5, lambda: memory[...], v1, 1536)),
        (first + 11, attention(1, 0, 1)),
        (first + 12, attention(1, 1, 1)),
        (first + 13, attention(1, 2, 1)),
        (first + 14, attention(1, 3, 1)),
        (first + 15, part1),
        (first + 16, mix_rank(1)),
        (first + 17, third_rows),
        (first + 17, feed_first),
        (12, lambda: rows_out(cot, grads, 1)),
        (22, lambda: rows_in(grads, 1)),
    ):
        task(tick, fn)
    for j in range(4):
        task(max(first + 18 + j, 2 * (9 + 2 * j) + OFFS[4] + 1), chunk(j))

    ids_out()
    rows_out(tok, rows, 0)
    for u in units:
        core_exchange(u)
    for t in range(max(2 * count + OFFS[4], max(tasks)) + 1):
        def at(offset):
            i, odd = divmod(t - offset, 2)
            return units[i] if not odd and 0 <= i < count else None

        if t == 0:
            own(units[0])
        if at(-2):
            own(at(-2))
        for k in (1, 2, 3):
            if at(OFFS[k - 1]):
                hop(at(OFFS[k - 1]), k)
        if at(OFFS[3]):
            cross(at(OFFS[3]))
        if at(OFFS[4]):
            last(at(OFFS[4]))
        if t < 16:
            enc_send(t)
        for fn in tasks.get(t, []):
            fn()

    boxes = list(
        zip(
            (rwb0, rwb1, rwb2), (czs0, czs1, czs2), (czw0, czw1, czw2), (sb0, sb1, sb2), (yb0, yb1, yb2),
            (xb0, xb1, xb2), (cb0, cb1, cb2), ((0, 8, 0, 1), (8, 4, 2, 2), (12, 4, 6, 2)), strict=True,
        )
    )

    def home_core(b):
        rwb, first, half = boxes[b][0], boxes[b][7][2], boxes[b][7][3]
        send(("home", b), None, gwhole.at[pl.ds(first + (1 - c) * half, half)], rwb, b_s.at[b, 0], b_r.at[b, 0], C)

    def home_z(b):
        rwb, czs, czw = boxes[b][:3]
        s0, ns, first, half = boxes[b][7]
        got(rwb, b_r.at[b, 0])
        rwb[...] += gwhole[pl.ds(first + c * half, half)]

        def cuts(j):
            return gsplit.at[s0 : s0 + ns, :, pl.ds(al(j * 128, 128), 128)], rwb.at[:, :, pl.ds(al(j * 256, 256), 256)]

        for k, j in enumerate(others):
            one, two = cuts(j)
            send(("home", b), None, one, czs.at[z], b_s.at[b, 1 + k], b_r.at[b, 1 + z], {"tp": j})
            send(("home", b), None, two, czw.at[z], b_s.at[b, 5 + k], b_r.at[b, 5 + z], {"tp": j})
        one, two = cuts(z)
        czs[pl.ds(z, 1)] = one[...][None]
        czw[pl.ds(z, 1)] = two[...][None]

    def dense_rows(b, to):
        czs, czw, (_, ns, _, half) = boxes[b][1], boxes[b][2], boxes[b][7]
        stack = jnp.concatenate(
            [jnp.concatenate([czs[k, s] for s in range(ns)] + [czw[k, w] for w in range(half)], axis=1) for k in range(4)]
        )
        row = lax.broadcasted_iota(jnp.int32, (64, 64), 0)
        col = lax.broadcasted_iota(jnp.int32, (64, 64), 1)
        clip = col // 16
        chosen = jnp.zeros((64, 64), f32)
        for k in range(4):
            line = idbuf[pl.ds(2 * y + k // 2, 1), k % 2 : k % 2 + 1, :64][0]
            chosen = jnp.where(clip == k, jnp.broadcast_to(line, (64, 64)), chosen)
        target = (row + 64 * to - lax.rem(col, 16)).astype(f32)
        return nn(jnp.where(chosen * 16.0 == target, 1.0, 0.0).astype(bf16), stack)

    def home_y(b):
        _, czs, czw, sb, yb = boxes[b][:5]
        for j in others:
            got(czs.at[j], b_r.at[b, 1 + j])
            got(czw.at[j], b_r.at[b, 5 + j])
        sb[...] = dense_rows(b, 1 - y).astype(bf16)
        send(("home", b), None, sb, yb, b_s.at[b, 9], b_r.at[b, 9], Y)

    def home_x(b):
        yb, xb = boxes[b][4:6]
        got(yb, b_r.at[b, 9])
        yb[...] = (dense_rows(b, y) + yb[...].astype(f32)).astype(bf16)
        send(("home", b), None, yb, xb, b_s.at[b, 10], b_r.at[b, 10], X)

    def home_rows(b):
        yb, xb, cb = boxes[b][4:7]
        got(xb, b_r.at[b, 10])
        xb[...] += yb[...]
        send(("home", b), None, xb.at[pl.ds(al((1 - c) * 32, 32), 32)], cb, b_s.at[b, 11], b_r.at[b, 11], C)

    def home_last(b):
        xb, cb = boxes[b][5:7]
        s0, ns, first, half = boxes[b][7]
        got(cb, b_r.at[b, 11])
        here, there = xb[pl.ds(al(c * 32, 32), 32)].astype(f32), cb[...].astype(f32)
        low, high = jnp.where(c == 0, here, there), jnp.where(c == 0, there, here)
        for s in range(ns):
            lanes = slice(s * 128, s * 128 + 128)
            split_sum[s0 + s] = jnp.concatenate([low[:, lanes], high[:, lanes]], axis=1)
        for w in range(half):
            lanes = slice(ns * 128 + w * 256, ns * 128 + w * 256 + 256)
            for q in range(4):
                wz[q, first + w] = low[q * 8 : q * 8 + 8, lanes]
                wz[q, first + half + w] = high[q * 8 : q * 8 + 8, lanes]
        slots = pl.ds(first, 2 * half)
        for k, j in enumerate(others):
            send(("home", b), None, wz.at[j, slots], whole_sum.at[z, slots], b_s.at[b, 12 + k], b_r.at[b, 12 + z], {"tp": j})
        pltpu.make_async_copy(wz.at[z, slots], whole_sum.at[z, slots], loc.at[count + 18 + b]).start()

    def home_done(b):
        first, half = boxes[b][7][2:]
        slots = pl.ds(first, 2 * half)
        for j in others:
            got(whole_sum.at[j, slots], b_r.at[b, 12 + j])
        pltpu.make_async_copy(wz.at[z, slots], whole_sum.at[z, slots], loc.at[count + 18 + b]).wait()

    def rows_back(src, dst, slot):
        def go():
            for k, j in enumerate(others):
                part = src.at[pl.ds(al(j * 112, 16), 112)]
                remote(part, dst.at[lax.rem(z, 2)], home_s.at[slot, k], home_r.at[slot, z], {"tp": j}).start()
            own_part(src, dst, slot).start()

        when(mine, go)

    def own_part(src, dst, slot):
        part = src.at[pl.ds(al(z * 112, 16), 112)]
        return pltpu.make_async_copy(part, dst.at[lax.rem(z, 2)], loc.at[count + 21 + slot])

    def rows_back_done(src, dst, slot):
        def go():
            for k, j in enumerate(others):
                part = src.at[pl.ds(al(j * 112, 16), 112)]
                remote(part, part, home_s.at[slot, k], home_r.at[slot, z], {"tp": j}).wait_send()
            own_part(src, dst, slot).wait()

        when(mine, go)
        for i in (0, 1):
            source = 2 * c + i
            when(source != z, lambda: got(dst.at[i], home_r.at[slot, source]))

    def enc_dst(quarter_of):
        return g_enc.at[lax.rem(z, 2), :, :, pl.ds(al(c * 512, 512), 512)]

    def enc_copy(j):
        part = gb.at[2 + j, 0:3, :, 0:512]
        owner = z // 2
        sems = home_s.at[2, j], home_r.at[2 + c, z]
        return part, owner, sems

    def enc_back(j):
        part, owner, (s, r) = enc_copy(j)
        when((j != z) | (c != owner), lambda: remote(part, enc_dst(j), s, r, {"tp": j, "core": owner}).start())
        when((j == z) & (c == owner), lambda: pltpu.make_async_copy(part, enc_dst(j), loc.at[count + 23]).start())

    def enc_back_done():
        for step in range(4):
            j = lax.rem(z + 1 + step, 4)
            part, owner, (s, r) = enc_copy(j)
            when((j != z) | (c != owner), lambda: remote(part, enc_dst(j), s, r, {"tp": j, "core": owner}).wait_send())
            when((j == z) & (c == owner), lambda: pltpu.make_async_copy(part, enc_dst(j), loc.at[count + 23]).wait())
        for i in (0, 1):
            for other in (0, 1):
                source = 2 * c + i
                when(
                    (source != z) | (c != other),
                    lambda: got(g_enc.at[i, :, :, other * 512 : other * 512 + 512], home_r.at[2 + other, source]),
                )

    def rank_in(first, s0, w0, inner, source, given):
        backs = jnp.concatenate([rank_t(split(first + i), g[...]) for i, g in enumerate(given)])
        down = nn(backs, source[...]).astype(bf16)
        for i, g in enumerate(given):
            gwhole[w0 + i] = down[16 * i : 16 * i + 16]
            gsplit[s0 + i] = nn(inner[16 * i : 16 * i + 16], g[...]).astype(bf16)

    def rank_out(side):
        s0, w0 = (12, 6) if side == 0 else (8, 2)
        gsplit[s0 + 3] = nn(rank_t(whole(7 + side), grads[...]), mix[side]).astype(bf16)
        gwhole[w0 + 3] = nn(t_mix[side], grads[...]).astype(bf16)

    def lane_sums(both):
        head = lax.broadcasted_iota(jnp.int32, (8, 128), 1) // HD
        pick_head = jnp.where(head == lax.broadcasted_iota(jnp.int32, (8, 128), 0), 1.0, 0.0).astype(bf16)
        high = both.astype(bf16)
        return nt(pick_head, high) + nt(pick_head, (both - high.astype(f32)).astype(bf16))

    def self_block(start, number):
        edge = 256
        length = rows.shape[0]

        def pair(p, carry):
            lanes = pair_lanes(p)
            qp, dop, kp, vp = q0[:, lanes], do[:, lanes], k0[:, lanes], v0[:, lanes]
            kt = kp.T
            logs = lse[0, p]
            totals = lane_sums(dop.astype(f32) * mix[0, :, lanes].astype(f32))
            first = lax.broadcasted_iota(jnp.int32, qp.shape, 1) < HD
            dqs, dks, dvs = [], [[], []], [[], []]
            for h in (0, 1):
                this = first == (h == 0)
                qm, dom = jnp.where(this, qp * SCALE, 0), jnp.where(this, dop, 0)
                terms = []
                for b, (low, high, start) in enumerate(((0, edge, 0), (edge, length, edge))):
                    sc = nt(kp[low:high], qm[start:])
                    key = low + lax.broadcasted_iota(jnp.int32, sc.shape, 0)
                    query = start + lax.broadcasted_iota(jnp.int32, sc.shape, 1)
                    sc = jnp.where(query >= key, sc, HIDE)
                    probs = jnp.exp(sc - logs[h : h + 1, start:])
                    dvs[b].append(nn(probs.astype(bf16), dop[start:]))
                    dp = nt(vp[low:high], dom[start:])
                    ds = (probs * (dp - totals[h : h + 1, start:])).astype(bf16)
                    dks[b].append(nn(ds, qp[start:]))
                    terms.append(nn(kt[:, low:high], ds))
                joined = jnp.concatenate([terms[0][:, :edge], terms[0][:, edge:] + terms[1]], axis=1)
                dqs.append(joined[h * HD : (h + 1) * HD])
            for b, place in enumerate((slice(0, edge), slice(edge, length))):
                first_k = lax.broadcasted_iota(jnp.int32, dks[b][0].shape, 1) < HD
                dv0[place, lanes] = jnp.where(first_k, dvs[b][0], dvs[b][1]).astype(bf16)
                dk0[place, lanes] = (jnp.where(first_k, dks[b][0], dks[b][1]) * SCALE).astype(bf16)
            dq[:, lanes] = (jnp.concatenate(dqs).T * SCALE).astype(bf16)
            return carry

        lax.fori_loop(start, start + number, pair, 0)

    def memory_half(h, q):
        rows_of = [pl.ds(al(m * 1024 + h * 512, 512), 512) for m in (4, 5)]
        place = pl.ds(al(q * 384, 128), 384)
        return nt(dk1[place], ga[rows_of[0]]) + nt(dv1[place], ga[rows_of[1]])

    def accumulator(p):
        return outbox.at[0, pl.ds(al(p // 2 * 128, 128), 128), pl.ds(al(lax.rem(p, 2) * 512, 512), rows.shape[0])]

    def cross_start():
        def pair(p, carry):
            lanes = pair_lanes(p)
            dsum[p] = lane_sums(do[:, lanes].astype(f32) * mix[1, :, lanes].astype(f32))
            accumulator(p)[...] = jnp.zeros((128, rows.shape[0]), f32)
            return carry

        lax.fori_loop(0, 4, pair, 0)

    def cross_block(q):
        place = pl.ds(al(q * 384, 128), 384)

        def pair(p, carry):
            lanes = pair_lanes(p)
            qp, dop = q1[:, lanes], do[:, lanes]
            kp, vp = k1[place, lanes], v1[place, lanes]
            kt = kp.T
            logs, totals = lse[1, p], dsum[p]
            first = lax.broadcasted_iota(jnp.int32, qp.shape, 1) < HD
            dqs, dks, dvs = [], [], []
            for h in (0, 1):
                this = first == (h == 0)
                sc = scores_t(kp, jnp.where(this, qp, 0), frames // groups, False)
                probs = jnp.exp(sc - logs[h : h + 1])
                dvs.append(nn(probs.astype(bf16), dop))
                dp = nt(vp, jnp.where(this, dop, 0))
                ds = (probs * (dp - totals[h : h + 1])).astype(bf16)
                dks.append(nn(ds, qp))
                dqs.append(nn(kt, ds)[h * HD : (h + 1) * HD])
            first_k = lax.broadcasted_iota(jnp.int32, kp.shape, 1) < HD
            dv1[place, lanes] = jnp.where(first_k, dvs[0], dvs[1]).astype(bf16)
            dk1[place, lanes] = (jnp.where(first_k, dks[0], dks[1]) * SCALE).astype(bf16)
            accumulator(p)[...] += jnp.concatenate(dqs)
            return carry

        lax.fori_loop(0, 4, pair, 0)

    def cross_end():
        def pair(p, carry):
            dq[:, pair_lanes(p)] = (accumulator(p)[...].T * SCALE).astype(bf16)
            return carry

        lax.fori_loop(0, 4, pair, 0)

    def enc_part(step):
        q = lax.rem(z + 1 + step, 4)
        sent_part = gb.at[2 + q, 0:3, :, 512:1024]
        sent_part[...] = memory_half(1 - c, q).astype(bf16).reshape(3, 128, 512)
        send("enc", None, sent_part, gb.at[2 + q, 0:3, :, 0:512], ex_s.at[6 + step], ex_r.at[6 + step], C)

    def enc_whole(step):
        q = lax.rem(z + 1 + step, 4)
        kept = gb.at[2 + q, 0:3, :, 0:512]
        got(kept, ex_r.at[6 + step])
        kept[...] = (memory_half(c, q).reshape(3, 128, 512) + kept[...].astype(f32)).astype(bf16)
        enc_back(q)

    dk1, dv1 = ga.at[pl.ds(6144, 1536)], ga.at[pl.ds(7680, 1536)]
    dk0, dv0 = dkv.at[0, 0:448], dkv.at[1, 0:448]
    part_out(3, 0)
    gwhole[0] = nn(r_in[...].astype(bf16), normed[2]).astype(bf16)
    gwhole[1] = nn(t_out[...].astype(bf16), grads[...]).astype(bf16)
    home_core(0)
    g_now[...] = grads[...].astype(f32) + norm_back(hidden[1], gain[2], part_sum(3, 0))
    part_out(2, 1)
    settle("rows")
    grads[...] = g_now[...].astype(bf16)
    do[...] = nt(grads[...], wb(1)).astype(bf16)
    home_z(0)
    normed[2] = (hidden[1] + part_sum(2, 1)).astype(bf16)
    rows_back(normed.at[2], acts, 0)
    settle(("part", 3))
    cross_start()
    cross_block(lax.rem(z + 1, 4))
    enc_part(0)
    cross_block(lax.rem(z + 2, 4))
    enc_part(1)
    enc_whole(0)
    home_y(0)
    cross_block(lax.rem(z + 3, 4))
    enc_part(2)
    enc_whole(1)
    rank_out(1)
    cross_block(z)
    cross_end()
    part_two(4, 0, lambda h: nt(dq[...], wa_half(3, h)))
    enc_part(3)
    enc_whole(2)
    home_x(0)
    g_now[...] += norm_back(hidden[0], gain[1], part_two_sum(4, 0))
    grads[...] = g_now[...].astype(bf16)
    do[...] = nt(grads[...], wb(0)).astype(bf16)
    enc_whole(3)
    rank_in(3, 8, 2, t_query, normed.at[1], [dq])
    home_rows(0)
    self_block(0, 2)
    home_last(0)
    self_block(2, 2)
    settle(("part", 2))
    part_two(5, 1, lambda h: nt(dq[...], wa_half(0, h)) + nt(dk0[...], wa_half(1, h)) + nt(dv0[...], wa_half(2, h)))
    rank_in(0, 12, 6, t_self, normed.at[0], [dq, dk0, dv0])
    rank_out(0)
    home_core(2)
    normed[0] = (g_now[...] + norm_back(rows[...].astype(f32), gain[0], part_two_sum(5, 1))).astype(bf16)
    home_z(2)
    rows_back(normed.at[0], g_tok, 1)
    rank_in(4, 9, 3, t_memory, memory, [dk1, dv1])
    home_core(1)
    home_y(2)
    home_z(1)
    home_x(2)
    home_y(1)
    home_rows(2)
    home_x(1)
    home_last(2)
    home_rows(1)
    home_last(1)
    for b in range(3):
        home_done(b)
    rows_back_done(normed.at[2], acts, 0)
    rows_back_done(normed.at[0], g_tok, 1)
    enc_back_done()
    for key in list(sent):
        settle(key)


def layer(tok, enc, cot, w_in, w_out, w_up, w_down, ids, gain, shift, *adapters):
    any_ = pl.BlockSpec(memory_space=pl.ANY)
    r, d = 448, tok.shape[2]
    padded = enc.shape[1]
    dma = pltpu.SemaphoreType.DMA

    def vm(*shape, dtype=bf16):
        return pltpu.VMEM(shape, dtype)

    n = 16
    halves = (1, 2, 2)
    splits = (8, 4, 4)
    widths = [s * 128 + w * 256 for s, w in zip(splits, halves, strict=True)]
    return pl.pallas_call(
        layer_kernel,
        out_shape=[
            sds((2, r // 4, d), bf16), sds((2, r // 4, d), bf16), sds((2, 3, padded // 12, d), bf16),
            sds((16, 32, 256), f32), sds((4, 10, 8, 256), f32),
        ],
        in_specs=[any_] * 7 + [VM] * 11,
        out_specs=[any_] * 3 + [VM, any_],
        scratch_shapes=[
            vm(10 * d, 512), vm(6, 4, 128, d), vm(r, d), vm(r, d), vm(padded, d), vm(3, r, d),
            vm(r, 512), vm(r, 512), vm(r, 512), vm(2, r, 512), vm(r, 512), vm(padded, 512), vm(padded, 512),
            vm(2, 4, 2, r, dtype=f32), vm(2, r, d, dtype=f32), vm(r, d, dtype=f32), vm(2, r, 512), vm(2, 512, 512),
            vm(2, r, d, dtype=f32), vm(2, r, d, dtype=f32),
            vm(4, 8, 128, dtype=f32), vm(512, 512), vm(320, 512), vm(64, 2048), vm(16, 5120), vm(2, 64, 2048), vm(2, 16, 5120),
            vm(4, 16, 2048), vm(2, 16, 5120), vm(16, r, dtype=f32), vm(16, r, dtype=f32), vm(2, 16, r),
            vm(16, 16, 512), vm(10, 16, d), vm(4, 10, 8, 256, dtype=f32), vm(4, 8, r, dtype=f32),
            vm(48, r), vm(16, r), vm(32, padded), vm(2, 16, r),
            *[vm(w, 16, d) for w in halves], *[vm(4, s, 16, 128) for s in splits], *[vm(4, w, 16, 256) for w in halves],
            *[vm(64, w) for w in widths], *[vm(64, w) for w in widths], *[vm(64, w) for w in widths], *[vm(32, w) for w in widths],
            dma((n,)), dma((n,)), dma((n, 4)), dma((n, 4)), dma((n, 4)), dma((n,)), dma((n,)), dma((n, 2)), dma((n, 2)),
            dma((3, 16)), dma((3, 16)), dma((n + 24,)), dma((12,)), dma((12,)), dma((12,)), dma((12,)),
            dma((3, 16)), dma((3, 16)), dma((4, 4)), dma((4, 4)),
        ],
        compiler_params=pltpu.CompilerParams(
            collective_id=1, has_side_effects=True, vmem_limit_bytes=int(62.5 * 1024 * 1024)
        ),
        name="layer",
    )(tok, enc, cot, w_in, w_out, w_up, w_down, ids, gain, shift, *adapters)


def swap_core(rows):
    return lax.ppermute(rows, "core", SWAP)


def core_sum(part):
    return part + swap_core(part)


def own_and_other(stacked):
    core = lax.axis_index("core")
    keep = lax.dynamic_index_in_dim(stacked, core, 0, keepdims=False)
    send = lax.dynamic_index_in_dim(stacked, 1 - core, 0, keepdims=False)
    return keep, swap_core(send)


def in_core_order(own, other):
    first = lax.axis_index("core") == 0
    return jnp.stack([jnp.where(first, own, other), jnp.where(first, other, own)])


def scatter_sh(stacked):
    n = lax.axis_size("sh")
    if n == 2:
        me = lax.axis_index("sh")
        keep = lax.dynamic_index_in_dim(stacked, me, 0, keepdims=False)
        send = lax.dynamic_index_in_dim(stacked, 1 - me, 0, keepdims=False)
        return keep + lax.ppermute(send, "sh", SWAP)
    return lax.psum_scatter(stacked, "sh", scatter_dimension=0, tiled=False)


def over_z(stacked):
    return lax.all_to_all(stacked, "tp", 0, 0, tiled=True)


def half_columns(rows):
    width = rows.shape[-1] // 2
    return lax.dynamic_slice_in_dim(rows, lax.axis_index("core") * width, width, rows.ndim - 1)


def rows_home(half):
    tp = lax.axis_size("tp")
    moved = over_z(half.reshape(tp, half.shape[0] // tp, half.shape[1]))
    own, other = own_and_other(moved.reshape(2, tp // 2, *moved.shape[1:]))
    both = in_core_order(own, other)
    return jnp.moveaxis(both, 0, 2).reshape(both.shape[1], both.shape[2], 2 * half.shape[1])


def rows_here(rows):
    tp = lax.axis_size("tp")
    both = in_core_order(rows, swap_core(rows)).reshape(4, *rows.shape[1:])
    moved = over_z(half_columns(both))
    moved = moved.reshape(tp * rows.shape[1], rows.shape[2] // 2)
    pair = in_core_order(moved, swap_core(moved))
    return jnp.concatenate([pair[0], pair[1]], axis=-1)


def gather_weights(w_attn_in, w_attn_out, w_up, w_down):
    def over_shard(block, axis):
        return lax.all_gather(block, ("sh", "core"), axis=axis, tiled=True)

    def over_tp(block, axis):
        return lax.all_gather(block, "tp", axis=axis, tiled=True)

    core = lax.axis_index("core")

    def half(block, axis):
        width = block.shape[axis] // 2
        return lax.dynamic_slice_in_dim(block, core * width, width, axis)

    w_in = over_tp(half(over_shard(w_attn_in.reshape(6, *w_attn_in.shape[3:]), 1), 2), 2)
    w_out = over_tp(half(over_shard(w_attn_out[0], 2), 1), 1)
    w_first = over_tp(half(over_shard(w_up[0], 0), 1), 1)
    w_second = over_tp(half(over_shard(w_down[0], 1), 0), 0)
    return w_in, w_out, w_first, w_second


def wide_parts(args):
    (
        tokens, encoded, cotangent, adapter_of, w_attn_in, w_attn_out, w_up, w_down, norm_gain, norm_shift,
        down_attn_in, up_attn_in, down_feed_in, up_feed_in, down_attn_out, up_attn_out, down_feed_out, up_feed_out,
    ) = args
    n, tp = lax.axis_size("sh"), lax.axis_size("tp")
    sh, core, z = lax.axis_index("sh"), lax.axis_index("core"), lax.axis_index("tp")
    width = w_attn_in.shape[3] * 2 * n
    held_rows = down_feed_in.shape[1]
    quarter = width // tp
    piece = quarter // 2

    ids = lax.all_gather(adapter_of, ("sh", "core"), tiled=True)

    row_ids = (sh * 2 + core) * held_rows + jnp.arange(held_rows)
    wanted = ids.reshape(n, tp)[:, :, None] * RANK + jnp.arange(RANK)
    picks = (wanted[..., None] == row_ids).astype(bf16)
    whole = jnp.concatenate(
        [
            down_attn_in.reshape(6, held_rows, width),
            down_feed_in,
            up_attn_out[0],
            up_feed_out,
        ]
    )
    def in_quarters(rows):
        return jnp.moveaxis(rows.reshape(held_rows, tp, quarter), 1, 0)

    split = jnp.concatenate(
        [
            up_attn_in.reshape(6, held_rows, quarter),
            in_quarters(up_feed_in[0]),
            down_attn_out[0],
            in_quarters(down_feed_out[0]),
        ]
    )
    picks_z = lax.dynamic_index_in_dim(picks, z, 1, keepdims=False)
    chosen_whole = jnp.einsum("srk,mkd->smrd", picks_z, whole, preferred_element_type=f32).astype(bf16)
    chosen_split = jnp.einsum("szrk,mkd->szmrd", picks, split, preferred_element_type=f32).astype(bf16)
    chosen_whole = core_sum(scatter_sh(chosen_whole))
    chosen_split = over_z(core_sum(scatter_sh(chosen_split)))

    def columns(first, count):
        mine = half_columns(chosen_split[:, first : first + count])
        return jnp.moveaxis(mine, 0, 2).reshape(count, RANK, tp * piece)

    def wide_columns(first):
        mine = lax.dynamic_slice_in_dim(chosen_split[:, first : first + tp], core * 2, 2, 1)
        return jnp.moveaxis(mine, 2, 0).reshape(RANK, tp * 2 * quarter)

    a_in, a_up, b_out, b_down = chosen_whole[:6], chosen_whole[6], chosen_whole[7:9], chosen_whole[9]
    b_in, b_up, a_out, a_down = columns(0, 6), wide_columns(6), columns(6 + tp, 2), wide_columns(8 + tp)

    w_in, w_out, w_first, w_second = gather_weights(w_attn_in, w_attn_out, w_up, w_down)
    taken = rows_here(tokens)
    upstream = rows_here(cotangent)
    mine = lax.dynamic_index_in_dim(encoded, z % 2, 0, keepdims=False)
    memory = jnp.where(core == z // 2, mine, swap_core(mine))

    def merge(weight, down_rows, up_rows):
        return (weight.astype(f32) + t_mm(down_rows, up_rows)).astype(bf16)

    w_in = [merge(w_in[i], a_in[i], b_in[i]) for i in range(6)]
    w_out = [merge(w_out[i], a_out[i], b_out[i]) for i in range(2)]
    w_first = merge(w_first, a_up, b_up)
    w_second = merge(w_second, a_down, b_down)

    gain, shift = norm_gain[0][:, None], norm_shift[0][:, None]
    frames = memory.shape[0]
    w_in = jnp.stack(w_in)
    normed0, q0, k0, v0, lse0, mix0, part = self_forward(taken, gain[0], shift[0], w_in[:3], w_out[0])
    k1, v1 = memory_project(memory, w_in[4:])
    hidden1, normed1, q1, lse1, mix1, part1 = cross_forward(
        taken, part, swap_core(part), gain[1], shift[1], w_in[3], k1, v1, w_out[1], frames
    )
    hidden2, part2, back, g_aup, g_bup, g_adown, g_bdown = feed(
        hidden1, part1, swap_core(part1), gain[2], shift[2], w_first, w_second, upstream, a_up, b_up, a_down, b_down
    )
    result = (hidden2 + core_sum(part2)).astype(bf16)
    grad, e1, dq1, dk1, dv1, back1 = cross_backward(
        hidden2, gain[2], upstream, back, swap_core(back), w_out[1], w_in[3], q1, k1, v1, lse1, frames
    )
    part = memory_backward(dk1, dv1, w_in[4:], frames)
    own, other = own_and_other(jnp.moveaxis(part.reshape(part.shape[0], 2, -1), 1, 0))
    memory_rows = (own.astype(f32) + other.astype(f32)).astype(bf16)
    grad, e0, dq0, dk0, dv0, back0 = self_backward(
        hidden1, gain[1], grad, back1, swap_core(back1), w_out[0], w_in[:3], q0, k0, v0, lse0
    )
    grad = final_norm(taken, gain[0], grad, back0, swap_core(back0))
    ranks1 = attention_ranks(normed1, memory, mix1, dq1, dk1, dv1, e1, a_in[3:], b_in[3:], a_out[1], b_out[1])
    ranks0 = attention_ranks(normed0, None, mix0, dq0, dk0, dv0, e0, a_in[:3], b_in[:3], a_out[0], b_out[0])
    feed_up = jnp.moveaxis(g_bup.reshape(RANK, tp, tp, piece), 2, 0).reshape(tp, RANK, tp * piece)
    feed_down = jnp.moveaxis(g_adown.reshape(RANK, tp, tp, piece), 2, 0).reshape(tp, RANK, tp * piece)
    out_split = jnp.stack([ranks0[2], ranks1[2]])
    out_whole = jnp.stack([ranks0[3], ranks1[3]])
    split_grads = jnp.concatenate([ranks0[1], ranks1[1], feed_up.astype(bf16), out_split, feed_down.astype(bf16)])
    whole_grads = jnp.concatenate(
        [ranks0[0], ranks1[0], g_aup.astype(bf16)[None], out_whole, g_bdown.astype(bf16)[None]]
    )
    here = ids.reshape(n, tp)[sh]
    return result, grad, memory_rows, split_grads, whole_grads, here


def narrow_parts(args):
    (
        tokens, encoded, cotangent, adapter_of, w_attn_in, w_attn_out, w_up, w_down, norm_gain, norm_shift,
        down_attn_in, up_attn_in, down_feed_in, up_feed_in, down_attn_out, up_attn_out, down_feed_out, up_feed_out,
    ) = args

    def six(rows):
        return rows.reshape(6, *rows.shape[3:])

    lines = jnp.pad(adapter_of.astype(f32), (0, 6))[:, None] * jnp.ones((1, 128), f32)
    _, frames, d = encoded.shape
    step = frames // 4
    spaced = jnp.pad(encoded.reshape(2, 4, step, d), ((0, 0), (0, 0), (0, 384 - step), (0, 0)))
    spaced = spaced.reshape(2, 1536, d)
    acts, g_tok, g_enc, split_sum, whole_sum = layer(
        tokens, spaced, cotangent, six(w_attn_in), w_attn_out[0], w_up[0], w_down[0], lines,
        norm_gain[0][:, None], norm_shift[0][:, None], six(down_attn_in), six(up_attn_in), down_feed_in[0],
        up_feed_in[0], down_attn_out[0], up_attn_out[0], down_feed_out[0], up_feed_out[0],
    )
    return (acts, *finish(g_tok, g_enc.astype(f32).reshape(2, 384, d)[:, :step], split_sum, whole_sum))


def finish(g_tok, g_enc, split_sum, whole_sum):
    held, d = split_sum.shape[1], g_tok.shape[2]
    part = whole_sum.shape[2]

    def kernel(tok, split_ref, whole_ref, out_tok, down_in, up_in, down_feed, up_feed, down_out, up_out, down_last, up_last):
        out_tok[...] = tok[...].astype(f32)

        def put_whole(out, slot):
            for q in range(4):
                out[:, q * 256 : q * 256 + 256] = whole_ref[q, slot]

        def put_wide(out, first):
            for core in range(2):
                for q in range(4):
                    place = core * 512 + q * 128
                    out[:, place : place + 128] = split_ref[first + q, :, core * 128 : core * 128 + 128]

        for side, (s0, w0) in enumerate(((12, 6), (8, 2))):
            for i in range(3):
                up_in[0, side, i] = split_ref[s0 + i]
                put_whole(down_in.at[0, side, i], w0 + i)
            down_out[0, side] = split_ref[s0 + 3]
            put_whole(up_out.at[0, side], w0 + 3)
        put_whole(down_feed.at[0], 0)
        put_whole(up_last.at[0], 1)
        put_wide(up_feed.at[0], 0)
        put_wide(down_last.at[0], 4)

    outs = pl.pallas_call(
        kernel,
        out_shape=[
            sds(g_tok.shape, f32), sds((1, 2, 3, part, d), f32), sds((1, 2, 3, held, 256), f32), sds((1, part, d), f32),
            sds((1, held, 1024), f32), sds((1, 2, held, 256), f32), sds((1, 2, part, d), f32), sds((1, held, 1024), f32),
            sds((1, part, d), f32),
        ],
        in_specs=[VM] * 3,
        out_specs=[VM] * 9,
        name="finish",
    )(g_tok, split_sum, whole_sum)
    return (outs[0], g_enc, *outs[1:])


def on_device(*args):
    if lax.axis_size("sh") == 2:
        return narrow_parts(args)
    n, tp = lax.axis_size("sh"), lax.axis_size("tp")
    held_rows, quarter = args[12].shape[1], args[11].shape[4]
    width, piece = quarter * tp, quarter // 2
    result, grad, memory_rows, split_grads, whole_grads, here = wide_parts(args)
    activations = rows_home(half_columns(result))
    grad_encoded = rows_home(memory_rows).astype(f32)
    grad_tokens = rows_home(half_columns(grad)).astype(f32)
    compact = jnp.moveaxis(split_grads.reshape(-1, RANK, tp, piece), 2, 0)
    own, other = own_and_other(jnp.moveaxis(whole_grads.reshape(-1, RANK, tp, 2, piece), (3, 2), (0, 1)))
    compact = jnp.concatenate([compact, own + other], axis=1)
    compact = over_z(compact)
    rows = jnp.arange(2 * n * held_rows)
    place = (here[:, None] * RANK + jnp.arange(RANK))[None] == rows[:, None, None]
    dense = jnp.einsum("gkr,kmrp->gmp", place.astype(bf16), compact, preferred_element_type=f32)
    dense = dense.astype(bf16).reshape(n, 2, held_rows, *dense.shape[1:])
    dense = scatter_sh(dense)
    dense = dense + lax.ppermute(dense, "rep", SWAP)
    both = in_core_order(*own_and_other(dense))
    done = jnp.moveaxis(both, 0, 2)
    count = 8 + 2 * tp
    sums = done[:, :count].astype(f32)

    def narrow(first, number):
        block = sums[:, first : first + number].reshape(held_rows, number, quarter)
        return jnp.moveaxis(block, 1, 0)

    def wide_of(first):
        block = jnp.moveaxis(sums[:, first : first + tp], 2, 1)
        return block.reshape(held_rows, 2 * tp * piece)

    grad_up_attn_in = narrow(0, 6).reshape(1, 2, 3, held_rows, quarter)
    grad_up_feed_in = wide_of(6)[None]
    grad_down_attn_out = narrow(6 + tp, 2)[None]
    grad_down_feed_out = wide_of(8 + tp)[None]
    rest = done[:, count:].reshape(tp, held_rows // tp, 10, quarter)
    rest = jnp.moveaxis(over_z(rest), 0, 2)
    rest = jnp.moveaxis(rest.reshape(held_rows // tp, 10, width), 1, 0).astype(f32)
    return (
        activations,
        grad_tokens,
        grad_encoded,
        rest[:6].reshape(1, 2, 3, held_rows // tp, width),
        grad_up_attn_in,
        rest[6:7],
        grad_up_feed_in,
        grad_down_attn_out,
        rest[7:9][None],
        grad_down_feed_out,
        rest[9:10],
    )


def solution(mesh):
    rep, shard, tp = (mesh.shape[name] for name in ("rep", "shard", "tp"))
    fine = Mesh(mesh.devices.reshape(rep, shard // 2, 2, tp), ("rep", "sh", "core", "tp"))
    shard = ("sh", "core")
    clips = ("rep", "sh", "core")
    both = ("sh", "core", "tp")
    placed = (
        P(clips, "tp", None),
        P(clips, None, None),
        P(clips, "tp", None),
        P(clips),
        P(None, None, None, shard, "tp"),
        P(None, None, "tp", shard),
        P(None, shard, "tp"),
        P(None, "tp", shard),
        P(),
        P(),
        P(None, None, None, shard, None),
        P(None, None, None, shard, "tp"),
        P(None, shard, None),
        P(None, shard, "tp"),
        P(None, None, shard, "tp"),
        P(None, None, shard, None),
        P(None, shard, "tp"),
        P(None, shard, None),
    )
    return jax.shard_map(
        on_device,
        mesh=fine,
        in_specs=placed,
        out_specs=(
            P(clips, "tp", None),
            P(clips, "tp", None),
            P(clips, "tp", None),
            P(None, None, None, both, None),
            P(None, None, None, shard, "tp"),
            P(None, both, None),
            P(None, shard, "tp"),
            P(None, None, shard, "tp"),
            P(None, None, both, None),
            P(None, shard, "tp"),
            P(None, both, None),
        ),
        check_vma=False,
    )
```
